256 devices in a mesh: pipe: 4 (over x), sp: 64 (over y, z, core).
Axes of the slice: x: 4, y: 4, z: 8, core: 2. Of those that a mesh axis runs over, the one named last changes fastest.
Arguments:
- latent: bfloat16 [32, 64, 3072], P(None, 'sp'), may hold values from -6 to 6
- modulation: float32 [4, 3, 3072], P('pipe'), may hold values from 0.5 to 3
- w_qkv: bfloat16 [4, 3072, 9216], P('pipe', 'sp'), may hold values from -0.109375 to 0.109375
- w_out: bfloat16 [4, 3072, 3072], P('pipe', None, 'sp'), may hold values from -0.109375 to 0.109375
- stale: bfloat16 [4, 32, 64, 2, 3072], P('pipe', None, 'sp'), may hold values from -4 to 4
Outputs:
- hidden: bfloat16 [4, 32, 64, 3072], P('pipe', None, 'sp')
The draws below stay inside these ranges and needn't reach their ends.
All inputs are finite; a program needn't handle non-finite values.
Results may differ from the reference program's by a relative error of at most 0.022.
Values may be sent and summed in bfloat16 or wider, within the bound.
No kernel may reach another device: no remote copies, remote signals or barrier semaphores. Data moves between devices by JAX's collectives and lax.ppermute only.
A program may use at most 128 MiB of HBM per device.

```python
import math
import jax
import jax.numpy as jnp
from jax import lax

D = 3072
HEADS = 24
HD = 128
PT = 64
PATCHES = 32
SECTIONS = 4
TOKENS = 2048
N_SP = 64


def block_levels(key, shape, pieces, low, top_value):
    factor_of = 1.0
    for axis_at, blocks in pieces:
        heights = jax.random.uniform(jax.random.fold_in(jax.random.fold_in(key, 6), axis_at), (blocks,), jnp.float32, low / len(pieces), top_value / len(pieces))
        factor_of = factor_of * jnp.repeat(jnp.exp(heights), shape[axis_at] // blocks).reshape((-1,) + (1,) * (len(shape) - 1 - axis_at))
    return factor_of


def centred(own_key, extent, scale, most, split=(), kind=jnp.bfloat16):
    loudness = block_levels(own_key, extent, split, -0.22, 0.18) if split else 1.0
    result = jax.random.normal(own_key, extent, jnp.float32) * scale * loudness
    return jnp.minimum(jnp.maximum(result, -most), most).astype(kind)


def setup_inputs(seed: int = 0) -> dict:
    key_list = jax.random.split(jax.random.key(seed), 6)
    latent = centred(key_list[0], (PATCHES, PT, D), 0.5, 6.0, ((1, 64),))
    modulation = jnp.clip(0.5 + 2.5 * jax.random.uniform(key_list[1], (SECTIONS, 3, D), jnp.float32) ** block_levels(key_list[1], (SECTIONS, 3, D), ((0, 4),), -0.2, 0.2), 0.5, 3.0)
    w_qkv = centred(key_list[2], (SECTIONS, D, 3 * D), D ** -0.5, 0.109375, ((0, 4), (1, 64)))
    w_out = centred(key_list[3], (SECTIONS, D, D), D ** -0.5, 0.109375, ((0, 4), (2, 64)))
    stale = centred(key_list[4], (SECTIONS, PATCHES, PT, 2, D), 1.0, 4.0, ((0, 4), (2, 64)))
    return dict(latent=latent, modulation=modulation, w_qkv=w_qkv, w_out=w_out, stale=stale)


def modulate(block_rows, shift_term, scale_term):
    widened = block_rows.astype(jnp.float32)
    average = lax.optimization_barrier(jnp.mean(widened, axis=-1, keepdims=True))
    centered = widened - average
    variance = lax.optimization_barrier(jnp.mean(centered * centered, axis=-1, keepdims=True))
    return (centered * lax.rsqrt(variance + 1e-06) * (1.0 + scale_term) + shift_term).astype(jnp.bfloat16)

def head_norm(head_values):
    return (head_values * lax.rsqrt(lax.optimization_barrier(jnp.mean(head_values * head_values, axis=-1, keepdims=True)) + 1e-06)).astype(jnp.bfloat16)

def reference(latent, modulation, w_qkv, w_out, stale):
    patch_group = min(8, N_SP // 2)
    head_groups = N_SP // patch_group
    heads_each = HEADS // head_groups
    block_width = heads_each * HD
    hidden_state = latent
    outputs = []
    patch_ids = jnp.arange(PATCHES, dtype=jnp.int32)[:, None, None, None]
    for block_index in range(SECTIONS):
        modulators = modulation[block_index]
        normed = modulate(hidden_state, modulators[0], modulators[1])
        projected = jnp.dot(normed.reshape(TOKENS, D), w_qkv[block_index], preferred_element_type=jnp.float32)
        projected = projected.reshape(PATCHES, PT, 3, HEADS, HD)
        queries = head_norm(projected[:, :, 0])
        fresh_keys = head_norm(projected[:, :, 1])
        fresh_values = projected[:, :, 2].astype(jnp.bfloat16)
        stale_keys = stale[block_index][:, :, 0].reshape(PATCHES, PT, HEADS, HD)
        stale_values = stale[block_index][:, :, 1].reshape(PATCHES, PT, HEADS, HD)

        def attend(patch_index):
            chosen = patch_ids == patch_index
            all_keys = jnp.where(chosen, fresh_keys, stale_keys).astype(jnp.float32)
            all_values = jnp.where(chosen, fresh_values, stale_values).astype(jnp.float32)
            query_rows = lax.dynamic_index_in_dim(queries, patch_index, 0, keepdims=False).astype(jnp.float32)
            scores = jnp.einsum('qhd,pshd->hqps', query_rows, all_keys) / math.sqrt(HD)
            numerator = jnp.exp(scores)
            row_total = lax.optimization_barrier(jnp.sum(numerator, axis=(2, 3)))
            weights = lax.optimization_barrier(numerator.astype(jnp.bfloat16)).astype(jnp.float32)
            attended = jnp.einsum('hqps,pshd->qhd', weights, all_values) / row_total.T[:, :, None]
            return attended.astype(jnp.bfloat16)
        attention = lax.map(attend, jnp.arange(PATCHES, dtype=jnp.int32))
        flattened = attention.reshape(TOKENS, D)
        summed = jnp.zeros((TOKENS, D), jnp.float32)
        for group_number in range(head_groups):
            lower = group_number * block_width
            group_part = jnp.dot(flattened[:, lower:lower + block_width], w_out[block_index][lower:lower + block_width], preferred_element_type=jnp.float32).astype(jnp.bfloat16)
            summed = summed + lax.optimization_barrier(group_part).astype(jnp.float32)
        hidden_state = (hidden_state.astype(jnp.float32) + modulators[2] * summed.reshape(PATCHES, PT, D)).astype(jnp.bfloat16)
        outputs.append(hidden_state)
    return jnp.stack(outputs)
```

```python
import math

import jax
import jax.numpy as jnp
from jax import lax
from jax.experimental import pallas as pl
from jax.experimental.pallas import tpu as pltpu
from jax.sharding import Mesh
from jax.sharding import PartitionSpec as P

D = 3072
HEADS = 24
HD = 128
PT = 64
PATCHES = 32
BLOCKS = 4
NX, NY, NZ, NC = 4, 4, 8, 2
SP = ("y", "z", "c")
HEAD_AXES = ("x", "y")
REST_AXES = ("z", "c")
MEMBERS = NX * NY
SOURCES = NY * NZ * NC
ROWS = D // SOURCES
PAIR = 2 * HD
OWN = 8
LOCAL = 2 * PT
AT_V_W, AT_OUT, AT_K, AT_V = 2 * ROWS, 3 * ROWS, 4 * ROWS, 4 * ROWS + PATCHES
PIECE = 4 * ROWS + 2 * PATCHES
VMEM = pl.BlockSpec(memory_space=pltpu.VMEM)
PARAMS = pltpu.CompilerParams(vmem_limit_bytes=48 * 1024 * 1024)


def head_norm(values):
    return (
        values * lax.rsqrt(jnp.mean(values * values, axis=-1, keepdims=True) + 1e-06)
    ).astype(jnp.bfloat16)


def modulate(rows, shift_term, scale_term):
    average = jnp.mean(rows, axis=-1, keepdims=True)
    centered = rows - average
    variance = jnp.mean(centered * centered, axis=-1, keepdims=True)
    return (centered * lax.rsqrt(variance + 1e-06) * (1.0 + scale_term) + shift_term).astype(
        jnp.bfloat16
    )


def pack_kernel(qkv_ref, out_ref, stale_ref, sent_ref):
    for member in range(MEMBERS):
        triple, half = divmod(member, 2)
        for lane, head in ((0, 3 * triple + 2 * half), (HD, 3 * triple + 1)):
            for part in range(3):
                sent_ref[member, part * ROWS : (part + 1) * ROWS, lane : lane + HD] = qkv_ref[
                    :, part * D + head * HD : part * D + (head + 1) * HD
                ]
            columns = slice(head * HD, (head + 1) * HD)
            sent_ref[member, AT_OUT:AT_K, lane : lane + HD] = out_ref[:, columns]
            sent_ref[member, AT_K:AT_V, lane : lane + HD] = stale_ref[0, :, columns]
            sent_ref[member, AT_V:PIECE, lane : lane + HD] = stale_ref[1, :, columns]


def first_kernel(rows_ref, shift_ref, scale_ref, normed_ref):
    normed = modulate(rows_ref[...].astype(jnp.float32), shift_ref[...], scale_ref[...])
    twice = jnp.concatenate([normed, normed], axis=0)
    for at in range(0, LOCAL, 2 * OWN):
        normed_ref[at : at + 2 * OWN, :] = twice


def sum_rows(parts_ref, rows_ref, gate_ref):
    total = jnp.zeros((2 * OWN, D), jnp.float32)
    for at in range(0, LOCAL, 2 * OWN):
        total = total + parts_ref[at : at + 2 * OWN, :].astype(jnp.float32)
    summed = total[:OWN] + total[OWN:]
    return (rows_ref[...].astype(jnp.float32) + gate_ref[...] * summed).astype(jnp.bfloat16)


def middle_kernel(parts_ref, rows_ref, gate_ref, shift_ref, scale_ref, updated_ref, normed_ref):
    updated = sum_rows(parts_ref, rows_ref, gate_ref)
    updated_ref[...] = updated
    normed = modulate(updated.astype(jnp.float32), shift_ref[...], scale_ref[...])
    twice = jnp.concatenate([normed, normed], axis=0)
    for at in range(0, LOCAL, 2 * OWN):
        normed_ref[at : at + 2 * OWN, :] = twice


def last_kernel(parts_ref, rows_ref, gate_ref, updated_ref):
    updated_ref[...] = sum_rows(parts_ref, rows_ref, gate_ref)


def across(left, right):
    return lax.dot_general(
        left, right, (((1,), (1,)), ((), ())), preferred_element_type=jnp.float32
    )


def block_kernel(
    place_ref, rows_ref, pieces_ref, partial_ref, w_q, w_k, w_v, w_o, keys, values, sems
):
    copies = [
        pltpu.make_async_copy(pieces_ref.at[:, low : low + count, :], target, sems.at[number])
        for number, (target, low, count) in enumerate(
            (
                (w_q, 0, ROWS),
                (w_k, ROWS, ROWS),
                (w_v, AT_V_W, ROWS),
                (keys, AT_K, PATCHES),
                (values, AT_V, PATCHES),
                (w_o, AT_OUT, ROWS),
            )
        )
    ]
    for copy in copies:
        copy.start()
    first_patch, half = place_ref[0], place_ref[1]
    rows = rows_ref[...]

    def project(weight):
        return jnp.dot(
            rows, weight[...].reshape(D, PAIR), preferred_element_type=jnp.float32
        )

    copies[0].wait()
    q = project(w_q)
    copies[1].wait()
    k = project(w_k)
    copies[2].wait()
    v = project(w_v).astype(jnp.bfloat16)
    queries = [head_norm(q[:, :HD]), head_norm(q[:, HD:])]
    fresh_keys = [head_norm(k[:, :HD]), head_norm(k[:, HD:])]
    fresh_values = [v[:, :HD], v[:, HD:]]
    for own in (queries, fresh_keys, fresh_values):
        own[1] = jnp.where(half == 0, own[1][:PT], own[1][PT:])
    copies[3].wait()
    copies[4].wait()
    scale = 1.0 / math.sqrt(HD)
    step = 16
    results = []
    for at in range(2):
        asking = queries[at]
        count = asking.shape[0]
        lanes = slice(at * HD, (at + 1) * HD)
        fresh = jnp.exp(across(asking, fresh_keys[at]) * scale)
        row_at = lax.broadcasted_iota(jnp.int32, (count, 1), 0)
        if at == 0:
            row_patch = first_patch + (row_at >= PT).astype(jnp.int32)
            column_at = lax.broadcasted_iota(jnp.int32, (count, count), 1)
            fresh = jnp.where((row_at >= PT) == (column_at >= PT), fresh, 0.0)
        else:
            row_patch = jnp.full((count, 1), first_patch + half, jnp.int32)
        total = jnp.sum(fresh, axis=1, keepdims=True)
        gathered = jnp.dot(
            fresh.astype(jnp.bfloat16), fresh_values[at], preferred_element_type=jnp.float32
        )
        patch_of = lax.broadcasted_iota(jnp.int32, (count, step * PATCHES), 1) % PATCHES
        stale_here = patch_of != row_patch
        for low in range(0, SOURCES, step):
            some_keys = keys[low : low + step, :, lanes].reshape(step * PATCHES, HD)
            some_values = values[low : low + step, :, lanes].reshape(step * PATCHES, HD)
            numerator = jnp.where(stale_here, jnp.exp(across(asking, some_keys) * scale), 0.0)
            total = total + jnp.sum(numerator, axis=1, keepdims=True)
            gathered = gathered + jnp.dot(
                numerator.astype(jnp.bfloat16), some_values, preferred_element_type=jnp.float32
            )
        results.append((gathered / total).astype(jnp.bfloat16))
    shared = results[1]
    nothing = jnp.zeros_like(shared)
    shared = jnp.concatenate(
        [jnp.where(half == 0, shared, nothing), jnp.where(half == 0, nothing, shared)], axis=0
    )
    attention = jnp.concatenate([results[0], shared], axis=1)
    copies[5].wait()
    for low in range(0, SOURCES, 8):
        some = w_o[low : low + 8].reshape(8 * ROWS, PAIR)
        partial_ref[:, low * ROWS : (low + 8) * ROWS] = across(attention, some).astype(
            jnp.bfloat16
        )


def to_own_order(array):
    lead = array.shape[:-1]
    split = array.reshape(lead + (NY, NZ * NC, ROWS))
    return jnp.swapaxes(split, -3, -2).reshape(lead + (D,))


def to_given_order(array):
    lead = array.shape[:-1]
    split = array.reshape(lead + (NZ * NC, NY, ROWS))
    return jnp.swapaxes(split, -3, -2).reshape(lead + (D,))


def exchange(array, axes):
    return lax.all_to_all(array, axes, split_axis=0, concat_axis=0, tiled=True)


def body(latent, modulation, w_qkv, w_out, stale):
    x_at, y_at = lax.axis_index("x"), lax.axis_index("y")
    pair_at = lax.axis_index("z") * NC + lax.axis_index("c")
    place = jnp.stack([2 * pair_at, y_at % 2]).astype(jnp.int32)

    sent = pl.pallas_call(
        pack_kernel,
        out_shape=jax.ShapeDtypeStruct((MEMBERS, PIECE, PAIR), jnp.bfloat16),
        in_specs=[VMEM] * 3,
        out_specs=VMEM,
        compiler_params=PARAMS,
        name="pack",
    )(w_qkv[0], w_out[0].T, jnp.swapaxes(stale[0, :, 0], 0, 1))
    received = exchange(sent, HEAD_AXES).reshape(BLOCKS, NY, PIECE, PAIR)

    def gather(block):
        return lax.all_gather(received[block], REST_AXES, axis=0, tiled=True)

    pieces = [gather(block) for block in range(BLOCKS)]

    terms = to_own_order(lax.all_gather(modulation[0], "x", axis=0, tiled=False))
    mine = exchange(latent[:, 0], REST_AXES).reshape(NZ * NC, 2, D)
    mine = jnp.swapaxes(mine, 0, 1).reshape(NZ * NC * 2, D)
    current = to_own_order(lax.dynamic_slice_in_dim(mine, x_at * OWN, OWN, 0))

    def term(block, which):
        return terms[block, which][None]

    spread = jax.ShapeDtypeStruct((LOCAL, D), jnp.bfloat16)
    owned = jax.ShapeDtypeStruct((OWN, D), jnp.bfloat16)
    normed = pl.pallas_call(
        first_kernel,
        out_shape=spread,
        in_specs=[VMEM] * 3,
        out_specs=VMEM,
        compiler_params=PARAMS,
        name="first",
    )(current, term(0, 0), term(0, 1))
    outputs = []
    for block in range(BLOCKS):
        rows = exchange(normed, HEAD_AXES)
        partial = pl.pallas_call(
            block_kernel,
            out_shape=spread,
            in_specs=[
                pl.BlockSpec(memory_space=pltpu.SMEM),
                VMEM,
                pl.BlockSpec(memory_space=pl.ANY),
            ],
            out_specs=VMEM,
            scratch_shapes=[pltpu.VMEM((SOURCES, ROWS, PAIR), jnp.bfloat16)] * 4
            + [pltpu.VMEM((SOURCES, PATCHES, PAIR), jnp.bfloat16)] * 2
            + [pltpu.SemaphoreType.DMA((6,))],
            compiler_params=PARAMS,
            cost_estimate=pl.CostEstimate(
                flops=2 * LOCAL * D * PAIR * 4 + 4 * 3 * PT * 2048 * HD,
                bytes_accessed=SOURCES * PIECE * PAIR * 2 + 4 * LOCAL * D,
                transcendentals=3 * PT * 2048,
            ),
            name="block",
        )(place, rows, pieces[block])
        parts = exchange(partial, HEAD_AXES)
        if block + 1 < BLOCKS:
            current, normed = pl.pallas_call(
                middle_kernel,
                out_shape=(owned, spread),
                in_specs=[VMEM] * 5,
                out_specs=(VMEM, VMEM),
                compiler_params=PARAMS,
                name="middle",
            )(parts, current, term(block, 2), term(block + 1, 0), term(block + 1, 1))
        else:
            current = pl.pallas_call(
                last_kernel,
                out_shape=owned,
                in_specs=[VMEM] * 3,
                out_specs=VMEM,
                compiler_params=PARAMS,
                name="last",
            )(parts, current, term(block, 2))
        outputs.append(to_given_order(current))
    placed = exchange(jnp.concatenate(outputs, axis=0), "x")
    placed = jnp.swapaxes(placed.reshape(2, NZ * NC, D), 0, 1).reshape(PATCHES, D)
    placed = exchange(placed, REST_AXES)
    return placed[None, :, None]


def solution(mesh):
    own_mesh = Mesh(mesh.devices.reshape(NX, NY, NZ, NC), ("x",) + SP)
    return jax.shard_map(
        body,
        mesh=own_mesh,
        in_specs=(
            P(None, SP, None),
            P("x", None, None),
            P("x", SP, None),
            P("x", None, SP),
            P("x", None, SP, None, None),
        ),
        out_specs=P("x", None, SP, None),
        check_vma=False,
    )
```

```python
import math

import jax
import jax.numpy as jnp
from jax import lax
from jax.experimental import pallas as pl
from jax.experimental.pallas import tpu as pltpu
from jax.sharding import Mesh
from jax.sharding import PartitionSpec as P

D = 3072
HEADS = 24
HD = 128
PT = 64
PATCHES = 32
BLOCKS = 4
NX, NY, NZ, NC = 4, 4, 8, 2
SP = ("y", "z", "c")
HEAD_AXES = ("x", "y")
REST_AXES = ("z", "c")
MEMBERS = NX * NY
SOURCES = NY * NZ * NC
ROWS = D // SOURCES
OWN = 8
LOCAL = 2 * PT
AT_OUT, AT_K, AT_V, AT_HALF = 3 * ROWS, 4 * ROWS, 4 * ROWS + PATCHES, 4 * ROWS + 2 * PATCHES
HALF = 2 * ROWS + PATCHES
PIECE = AT_HALF + HALF
VMEM = pl.BlockSpec(memory_space=pltpu.VMEM)
ANY = pl.BlockSpec(memory_space=pl.ANY)
SMEM = pl.BlockSpec(memory_space=pltpu.SMEM)
PARAMS = pltpu.CompilerParams(vmem_limit_bytes=48 * 1024 * 1024)


def head_norm(values):
    return (
        values * lax.rsqrt(jnp.mean(values * values, axis=-1, keepdims=True) + 1e-06)
    ).astype(jnp.bfloat16)


def modulate(rows, shift_term, scale_term):
    average = jnp.mean(rows, axis=-1, keepdims=True)
    centered = rows - average
    variance = jnp.mean(centered * centered, axis=-1, keepdims=True)
    return (centered * lax.rsqrt(variance + 1e-06) * (1.0 + scale_term) + shift_term).astype(
        jnp.bfloat16
    )


def pack_kernel(qkv_ref, out_ref, stale_ref, sent_ref):
    def columns(head):
        return slice(head * HD, (head + 1) * HD)

    def weight(part, head):
        if part == 3:
            return out_ref[:, columns(head)]
        return qkv_ref[:, columns(part * HEADS + head)]

    for member in range(MEMBERS):
        triple, half = divmod(member, 2)
        own, shared = 3 * triple + 2 * half, 3 * triple + 1
        for part in range(4):
            sent_ref[member, part * ROWS : (part + 1) * ROWS, :] = weight(part, own)
        sent_ref[member, AT_K:AT_V, :] = stale_ref[0, :, columns(own)]
        sent_ref[member, AT_V:AT_HALF, :] = stale_ref[1, :, columns(own)]
        for at in range(2):
            low = AT_HALF + at * ROWS
            sent_ref[member, low : low + ROWS, :] = weight(2 * half + at, shared)
        sent_ref[member, AT_HALF + 2 * ROWS : PIECE, :] = stale_ref[half, :, columns(shared)]


def first_kernel(place_ref, rows_ref, shift_ref, scale_ref, normed_ref, core_ref):
    core_ref[0] = place_ref[2]
    normed = modulate(rows_ref[...].astype(jnp.float32), shift_ref[...], scale_ref[...])
    twice = jnp.concatenate([normed, normed], axis=0)
    for at in range(0, LOCAL, 2 * OWN):
        normed_ref[at : at + 2 * OWN, :] = twice


def sum_rows(parts_ref, rows_ref, gate_ref):
    total = jnp.zeros((2 * OWN, D), jnp.float32)
    for at in range(0, LOCAL, 2 * OWN):
        total = total + parts_ref[at : at + 2 * OWN, :].astype(jnp.float32)
    summed = total[:OWN] + total[OWN:]
    return (rows_ref[...].astype(jnp.float32) + gate_ref[...] * summed).astype(jnp.bfloat16)


def middle_kernel(
    place_ref,
    parts_ref,
    rows_ref,
    gate_ref,
    shift_ref,
    scale_ref,
    updated_ref,
    normed_ref,
    core_ref,
):
    core_ref[0] = place_ref[2]
    updated = sum_rows(parts_ref, rows_ref, gate_ref)
    updated_ref[...] = updated
    normed = modulate(updated.astype(jnp.float32), shift_ref[...], scale_ref[...])
    twice = jnp.concatenate([normed, normed], axis=0)
    for at in range(0, LOCAL, 2 * OWN):
        normed_ref[at : at + 2 * OWN, :] = twice


def after_kernel(array_ref, earlier_ref, same_ref):
    del array_ref, earlier_ref, same_ref


def last_kernel(parts_ref, rows_ref, gate_ref, updated_ref):
    updated_ref[...] = sum_rows(parts_ref, rows_ref, gate_ref)


def across(left, right):
    return lax.dot_general(
        left, right, (((1,), (1,)), ((), ())), preferred_element_type=jnp.float32
    )


def block_kernel(
    place_ref,
    rows_ref,
    pieces_ref,
    near_ref,
    far_ref,
    partial_ref,
    w_q,
    w_k,
    w_v,
    w_o,
    keys,
    values,
    w_qv,
    w_ko,
    shared,
    sems,
):
    first_patch, half, core = place_ref[0], place_ref[1], place_ref[2]
    copies = []

    def fetch(source, target):
        copies.append(pltpu.make_async_copy(source, target, sems.at[len(copies)]))

    def fetch_half(target, low, count):
        fetch(pieces_ref.at[:, :, :, AT_HALF + low : AT_HALF + low + count, :], target.at[half])
        fetch(near_ref.at[:, :, low : low + count, :], target.at[1 - half, :, core])
        fetch(far_ref.at[:, :, low : low + count, :], target.at[1 - half, :, 1 - core])

    for number, target in enumerate((w_q, w_k, w_v)):
        fetch(pieces_ref.at[:, :, :, number * ROWS : (number + 1) * ROWS, :], target)
    fetch_half(w_qv, 0, ROWS)
    fetch_half(w_ko, ROWS, ROWS)
    fetch(pieces_ref.at[:, :, :, AT_K:AT_V, :], keys)
    fetch(pieces_ref.at[:, :, :, AT_V:AT_HALF, :], values)
    fetch_half(shared, 2 * ROWS, PATCHES)
    fetch(pieces_ref.at[:, :, :, AT_OUT:AT_K, :], w_o)
    for copy in copies:
        copy.start()
    rows = rows_ref[...]

    def both(own, other):
        return jnp.concatenate([own.reshape(D, HD), other.reshape(D, HD)], axis=1)

    def project(own, other):
        return jnp.dot(rows, both(own, other), preferred_element_type=jnp.float32)

    for copy in copies[:9]:
        copy.wait()
    q = project(w_q[...], w_qv[0])
    k = project(w_k[...], w_ko[0])
    v = project(w_v[...], w_qv[1]).astype(jnp.bfloat16)
    queries = [head_norm(q[:, :HD]), head_norm(q[:, HD:])]
    fresh_keys = [head_norm(k[:, :HD]), head_norm(k[:, HD:])]
    fresh_values = [v[:, :HD], v[:, HD:]]
    for own in (queries, fresh_keys, fresh_values):
        own[1] = jnp.where(half == 0, own[1][:PT], own[1][PT:])
    for copy in copies[9:14]:
        copy.wait()
    scale = 1.0 / math.sqrt(HD)
    step = 2
    some = step * NC * NY * PATCHES
    results = []
    for at in range(2):
        asking = queries[at]
        count = asking.shape[0]
        fresh = jnp.exp(across(asking, fresh_keys[at]) * scale)
        row_at = lax.broadcasted_iota(jnp.int32, (count, 1), 0)
        if at == 0:
            row_patch = first_patch + (row_at >= PT).astype(jnp.int32)
            column_at = lax.broadcasted_iota(jnp.int32, (count, count), 1)
            fresh = jnp.where((row_at >= PT) == (column_at >= PT), fresh, 0.0)
        else:
            row_patch = jnp.full((count, 1), first_patch + half, jnp.int32)
        total = jnp.sum(fresh, axis=1, keepdims=True)
        gathered = jnp.dot(
            fresh.astype(jnp.bfloat16), fresh_values[at], preferred_element_type=jnp.float32
        )
        patch_of = lax.broadcasted_iota(jnp.int32, (count, some), 1) % PATCHES
        stale_here = patch_of != row_patch
        for low in range(0, NZ, step):
            if at == 0:
                some_keys, some_values = keys[low : low + step], values[low : low + step]
            else:
                some_keys, some_values = shared[0, low : low + step], shared[1, low : low + step]
            some_keys, some_values = some_keys.reshape(some, HD), some_values.reshape(some, HD)
            numerator = jnp.where(stale_here, jnp.exp(across(asking, some_keys) * scale), 0.0)
            total = total + jnp.sum(numerator, axis=1, keepdims=True)
            gathered = gathered + jnp.dot(
                numerator.astype(jnp.bfloat16), some_values, preferred_element_type=jnp.float32
            )
        results.append((gathered / total).astype(jnp.bfloat16))
    answer = results[1]
    nothing = jnp.zeros_like(answer)
    answer = jnp.concatenate(
        [jnp.where(half == 0, answer, nothing), jnp.where(half == 0, nothing, answer)], axis=0
    )
    attention = jnp.concatenate([results[0], answer], axis=1)
    copies[14].wait()
    width = NC * NY * ROWS
    for low in range(NZ):
        weight = jnp.concatenate(
            [w_o[low].reshape(width, HD), w_ko[1, low].reshape(width, HD)], axis=1
        )
        partial_ref[:, low * width : (low + 1) * width] = across(attention, weight).astype(
            jnp.bfloat16
        )


def to_own_order(array):
    lead = array.shape[:-1]
    split = array.reshape(lead + (NY, NZ * NC, ROWS))
    return jnp.swapaxes(split, -3, -2).reshape(lead + (D,))


def to_given_order(array):
    lead = array.shape[:-1]
    split = array.reshape(lead + (NZ * NC, NY, ROWS))
    return jnp.swapaxes(split, -3, -2).reshape(lead + (D,))


def exchange(array, axes):
    return lax.all_to_all(array, axes, split_axis=0, concat_axis=0, tiled=True)


def body(latent, modulation, w_qkv, w_out, stale):
    x_at, y_at = lax.axis_index("x"), lax.axis_index("y")
    pair_at = lax.axis_index("z") * NC + lax.axis_index("c")
    core_at = lax.axis_index("c")
    place = jnp.stack([2 * pair_at, y_at % 2, core_at]).astype(jnp.int32)

    sent = pl.pallas_call(
        pack_kernel,
        out_shape=jax.ShapeDtypeStruct((MEMBERS, PIECE, HD), jnp.bfloat16),
        in_specs=[VMEM] * 3,
        out_specs=VMEM,
        compiler_params=PARAMS,
        name="pack",
    )(w_qkv[0], w_out[0].T, jnp.swapaxes(stale[0, :, 0], 0, 1))
    received = exchange(sent, HEAD_AXES).reshape(BLOCKS, NY, PIECE, HD)

    def gather(block):
        gathered = lax.all_gather(received[block], REST_AXES, axis=0, tiled=True)
        return gathered.reshape(NZ, NC, NY, PIECE, HD)

    def after(array, earlier):
        return pl.pallas_call(
            after_kernel,
            out_shape=jax.ShapeDtypeStruct(array.shape, array.dtype),
            in_specs=[ANY, ANY],
            out_specs=ANY,
            input_output_aliases={0: 0},
            name="after",
        )(array, earlier)

    pieces = [gather(block) for block in range(BLOCKS)]

    terms = to_own_order(lax.all_gather(modulation[0], "x", axis=0, tiled=False))
    mine = exchange(latent[:, 0], REST_AXES).reshape(NZ * NC, 2, D)
    mine = jnp.swapaxes(mine, 0, 1).reshape(NZ * NC * 2, D)
    current = to_own_order(lax.dynamic_slice_in_dim(mine, x_at * OWN, OWN, 0))

    def term(block, which):
        return terms[block, which][None]

    spread = jax.ShapeDtypeStruct((LOCAL, D), jnp.bfloat16)
    owned = jax.ShapeDtypeStruct((OWN, D), jnp.bfloat16)
    index = jax.ShapeDtypeStruct((1,), jnp.int32)
    normed, core = pl.pallas_call(
        first_kernel,
        out_shape=(spread, index),
        in_specs=[SMEM] + [VMEM] * 3,
        out_specs=(VMEM, SMEM),
        compiler_params=PARAMS,
        name="first",
    )(place, current, term(0, 0), term(0, 1))
    outputs = []
    for block in range(BLOCKS):
        half = lax.dynamic_slice(
            pieces[block], (0, core[0], 0, AT_HALF, 0), (NZ, 1, NY, HALF, HD)
        ).reshape(NZ, NY, HALF, HD)
        near = lax.ppermute(half, "y", [(at, at ^ 1) for at in range(NY)])
        rows = exchange(normed, HEAD_AXES)
        near = after(near, rows)
        far = lax.ppermute(near, "c", [(0, 1), (1, 0)])
        partial = pl.pallas_call(
            block_kernel,
            out_shape=spread,
            in_specs=[
                SMEM,
                VMEM,
                ANY,
                ANY,
                ANY,
            ],
            out_specs=VMEM,
            scratch_shapes=[pltpu.VMEM((NZ, NC, NY, ROWS, HD), jnp.bfloat16)] * 4
            + [pltpu.VMEM((NZ, NC, NY, PATCHES, HD), jnp.bfloat16)] * 2
            + [pltpu.VMEM((2, NZ, NC, NY, ROWS, HD), jnp.bfloat16)] * 2
            + [pltpu.VMEM((2, NZ, NC, NY, PATCHES, HD), jnp.bfloat16)]
            + [pltpu.SemaphoreType.DMA((15,))],
            compiler_params=PARAMS,
            cost_estimate=pl.CostEstimate(
                flops=2 * LOCAL * D * 2 * HD * 4 + 4 * 3 * PT * 2048 * HD,
                bytes_accessed=SOURCES * PIECE * HD * 2 + 4 * LOCAL * D,
                transcendentals=3 * PT * 2048,
            ),
            name="block",
        )(place, rows, pieces[block], near, far)
        parts = exchange(partial, HEAD_AXES)
        if block + 1 < BLOCKS:
            current, normed, core = pl.pallas_call(
                middle_kernel,
                out_shape=(owned, spread, index),
                in_specs=[SMEM] + [VMEM] * 5,
                out_specs=(VMEM, VMEM, SMEM),
                compiler_params=PARAMS,
                name="middle",
            )(place, parts, current, term(block, 2), term(block + 1, 0), term(block + 1, 1))
        else:
            current = pl.pallas_call(
                last_kernel,
                out_shape=owned,
                in_specs=[VMEM] * 3,
                out_specs=VMEM,
                compiler_params=PARAMS,
                name="last",
            )(parts, current, term(block, 2))
        outputs.append(to_given_order(current))
    placed = exchange(jnp.concatenate(outputs, axis=0), "x")
    placed = jnp.swapaxes(placed.reshape(2, NZ * NC, D), 0, 1).reshape(PATCHES, D)
    placed = exchange(placed, REST_AXES)
    return placed[None, :, None]


def solution(mesh):
    own_mesh = Mesh(mesh.devices.reshape(NX, NY, NZ, NC), ("x",) + SP)
    return jax.shard_map(
        body,
        mesh=own_mesh,
        in_specs=(
            P(None, SP, None),
            P("x", None, None),
            P("x", SP, None),
            P("x", None, SP),
            P("x", None, SP, None, None),
        ),
        out_specs=P("x", None, SP, None),
        check_vma=False,
    )
```

```python
import math

import jax
import jax.numpy as jnp
from jax import lax
from jax.experimental import pallas as pl
from jax.experimental.pallas import tpu as pltpu
from jax.sharding import Mesh
from jax.sharding import PartitionSpec as P

D = 3072
HEADS = 24
HD = 128
PT = 64
PATCHES = 32
BLOCKS = 4
NX, NY, NZ, NC = 4, 4, 8, 2
SP = ("y", "z", "c")
HEAD_AXES = ("x", "y")
REST_AXES = ("z", "c")
MEMBERS = NX * NY
SOURCES = NY * NZ * NC
ROWS = D // SOURCES
OWN = 8
LOCAL = 2 * PT
AT_OUT, AT_K, AT_V, AT_SHARED = 3 * ROWS, 4 * ROWS, 4 * ROWS + PATCHES, 4 * ROWS + 2 * PATCHES
AT_SHARED_OUT = AT_SHARED + 2 * ROWS
AT_SHARED_K = AT_SHARED + 3 * ROWS
AT_SHARED_V = AT_SHARED_K + PATCHES
PIECE = AT_SHARED_V + PATCHES
AT_KEPT = 3 * LOCAL
LEFT = AT_KEPT + 2 * PT
ANY = pl.BlockSpec(memory_space=pl.ANY)
SMEM = pl.BlockSpec(memory_space=pltpu.SMEM)
VMEM = pl.BlockSpec(memory_space=pltpu.VMEM)
PARAMS = pltpu.CompilerParams(vmem_limit_bytes=48 * 1024 * 1024)


def head_norm(values):
    return (
        values * lax.rsqrt(jnp.mean(values * values, axis=-1, keepdims=True) + 1e-06)
    ).astype(jnp.bfloat16)


def modulate(rows, shift_term, scale_term):
    average = jnp.mean(rows, axis=-1, keepdims=True)
    centered = rows - average
    variance = jnp.mean(centered * centered, axis=-1, keepdims=True)
    return (centered * lax.rsqrt(variance + 1e-06) * (1.0 + scale_term) + shift_term).astype(
        jnp.bfloat16
    )


def pack_kernel(qkv_from, out_from, stale_ref, sent_ref, qkv_ref, out_ref, sems):
    copies = [
        pltpu.make_async_copy(qkv_from, qkv_ref, sems.at[0]),
        pltpu.make_async_copy(out_from, out_ref, sems.at[1]),
    ]
    for copy in copies:
        copy.start()

    def columns(head):
        return slice(head * HD, (head + 1) * HD)

    def put(member, low, rows):
        sent_ref[member, low : low + rows.shape[0], :] = rows

    def each():
        for member in range(MEMBERS):
            triple, half = divmod(member, 2)
            yield member, half, 3 * triple + 2 * half, 3 * triple + 1

    for member, half, own, shared in each():
        put(member, AT_K, stale_ref[0, :, columns(own)])
        put(member, AT_V, stale_ref[1, :, columns(own)])
        put(member, AT_SHARED_K, stale_ref[0, :, columns(shared)])
        put(member, AT_SHARED_V, stale_ref[1, :, columns(shared)])
    copies[1].wait()
    for member, half, own, shared in each():
        put(member, AT_OUT, out_ref[:, columns(own)])
        put(member, AT_SHARED_OUT, out_ref[:, columns(shared)])
    copies[0].wait()
    for member, half, own, shared in each():
        for part in range(3):
            put(member, part * ROWS, qkv_ref[:, columns(part * HEADS + own)])
        put(member, AT_SHARED, qkv_ref[:, columns(half * HEADS + shared)])
        put(member, AT_SHARED + ROWS, qkv_ref[:, columns(2 * HEADS + shared)])


def first_kernel(rows_ref, shift_ref, scale_ref, normed_ref):
    normed = modulate(rows_ref[...].astype(jnp.float32), shift_ref[...], scale_ref[...])
    twice = jnp.concatenate([normed, normed], axis=0)
    for at in range(0, LOCAL, 2 * OWN):
        normed_ref[at : at + 2 * OWN, :] = twice


def sum_rows(parts_ref, rows_ref, gate_ref):
    total = jnp.zeros((2 * OWN, D), jnp.float32)
    for at in range(0, LOCAL, 2 * OWN):
        total = total + parts_ref[at : at + 2 * OWN, :].astype(jnp.float32)
    summed = total[:OWN] + total[OWN:]
    return (rows_ref[...].astype(jnp.float32) + gate_ref[...] * summed).astype(jnp.bfloat16)


def middle_kernel(parts_ref, rows_ref, gate_ref, shift_ref, scale_ref, updated_ref, normed_ref):
    updated = sum_rows(parts_ref, rows_ref, gate_ref)
    updated_ref[...] = updated
    normed = modulate(updated.astype(jnp.float32), shift_ref[...], scale_ref[...])
    twice = jnp.concatenate([normed, normed], axis=0)
    for at in range(0, LOCAL, 2 * OWN):
        normed_ref[at : at + 2 * OWN, :] = twice


def last_kernel(parts_ref, rows_ref, gate_ref, updated_ref):
    updated_ref[...] = sum_rows(parts_ref, rows_ref, gate_ref)


def across(left, right):
    return lax.dot_general(
        left, right, (((1,), (1,)), ((), ())), preferred_element_type=jnp.float32
    )


def fetch(pieces_ref, sems, wanted):
    copies = [
        pltpu.make_async_copy(
            pieces_ref.at[:, low : low + target.shape[1], :], target, sems.at[number]
        )
        for number, (target, low) in enumerate(wanted)
    ]
    for copy in copies:
        copy.start()
    return copies


def project_kernel(
    place_ref, rows_ref, pieces_ref, left_ref, given_ref, w_q, w_k, w_v, w_qk, w_sv, sems
):
    weights = (w_q, w_k, w_v, w_qk, w_sv)
    lows = (0, ROWS, 2 * ROWS, AT_SHARED, AT_SHARED + ROWS)
    copies = fetch(pieces_ref, sems, list(zip(weights, lows)))
    half = place_ref[1]
    rows = rows_ref[...]

    def project(*parts):
        weight = jnp.concatenate([part[...].reshape(D, HD) for part in parts], axis=1)
        return jnp.dot(rows, weight, preferred_element_type=jnp.float32)

    def mine(both):
        return jnp.where(half == 0, both[:PT], both[PT:])

    copies[0].wait()
    copies[1].wait()
    first = project(w_q, w_k)
    left_ref[:LOCAL] = head_norm(first[:, :HD])
    left_ref[LOCAL : 2 * LOCAL] = head_norm(first[:, HD:])
    copies[3].wait()
    copies[4].wait()
    second = project(w_qk, w_sv)
    shared = head_norm(second[:, :HD])
    left_ref[AT_KEPT : AT_KEPT + PT] = mine(shared)
    given_ref[...] = jnp.where(half == 0, shared[PT:], shared[:PT])
    left_ref[AT_KEPT + PT :] = mine(second[:, HD:].astype(jnp.bfloat16))
    copies[2].wait()
    left_ref[2 * LOCAL : 3 * LOCAL] = project(w_v).astype(jnp.bfloat16)


def attend(queries, fresh_keys, fresh_values, keys, values, row_patch):
    count = queries.shape[0]
    scale = 1.0 / math.sqrt(HD)
    fresh = jnp.exp(across(queries, fresh_keys) * scale)
    if count > PT:
        row_at = lax.broadcasted_iota(jnp.int32, (count, 1), 0)
        column_at = lax.broadcasted_iota(jnp.int32, (count, count), 1)
        fresh = jnp.where((row_at >= PT) == (column_at >= PT), fresh, 0.0)
    total = jnp.sum(fresh, axis=1, keepdims=True)
    gathered = jnp.dot(
        fresh.astype(jnp.bfloat16), fresh_values, preferred_element_type=jnp.float32
    )
    step = 16
    patch_of = lax.broadcasted_iota(jnp.int32, (count, step * PATCHES), 1) % PATCHES
    stale_here = patch_of != row_patch
    for low in range(0, SOURCES, step):
        some_keys = keys[low : low + step].reshape(step * PATCHES, HD)
        some_values = values[low : low + step].reshape(step * PATCHES, HD)
        numerator = jnp.where(stale_here, jnp.exp(across(queries, some_keys) * scale), 0.0)
        total = total + jnp.sum(numerator, axis=1, keepdims=True)
        gathered = gathered + jnp.dot(
            numerator.astype(jnp.bfloat16), some_values, preferred_element_type=jnp.float32
        )
    return (gathered / total).astype(jnp.bfloat16)


def own_kernel(place_ref, left_ref, pieces_ref, attended_ref, keys, values, sems):
    copies = fetch(pieces_ref, sems, [(keys, AT_K), (values, AT_V)])
    second = lax.broadcasted_iota(jnp.int32, (LOCAL, 1), 0) >= PT
    row_patch = place_ref[0] + second.astype(jnp.int32)
    for copy in copies:
        copy.wait()
    attended_ref[...] = attend(
        left_ref[:LOCAL],
        left_ref[LOCAL : 2 * LOCAL],
        left_ref[2 * LOCAL : 3 * LOCAL],
        keys,
        values,
        row_patch,
    )


def finish_kernel(
    place_ref,
    left_ref,
    attended_ref,
    got_ref,
    pieces_ref,
    partial_ref,
    keys,
    values,
    w_own,
    w_shared,
    sems,
):
    copies = fetch(
        pieces_ref,
        sems,
        [(keys, AT_SHARED_K), (values, AT_SHARED_V), (w_own, AT_OUT), (w_shared, AT_SHARED_OUT)],
    )
    half = place_ref[1]
    kept, got = left_ref[AT_KEPT : AT_KEPT + PT], got_ref[...]
    queries = jnp.where(half == 0, kept, got)
    fresh_keys = jnp.where(half == 0, got, kept)
    copies[0].wait()
    copies[1].wait()
    shared = attend(
        queries,
        fresh_keys,
        left_ref[AT_KEPT + PT :],
        keys,
        values,
        jnp.full((PT, 1), place_ref[0] + half, jnp.int32),
    )
    nothing = jnp.zeros_like(shared)
    shared = jnp.concatenate(
        [jnp.where(half == 0, shared, nothing), jnp.where(half == 0, nothing, shared)], axis=0
    )
    attention = jnp.concatenate([attended_ref[...], shared], axis=1)
    copies[2].wait()
    copies[3].wait()
    step = 8
    width = step * ROWS
    for low in range(0, SOURCES, step):
        weight = jnp.concatenate(
            [
                w_own[low : low + step].reshape(width, HD),
                w_shared[low : low + step].reshape(width, HD),
            ],
            axis=1,
        )
        partial_ref[:, low * ROWS : low * ROWS + width] = across(attention, weight).astype(
            jnp.bfloat16
        )


def to_own_order(array):
    lead = array.shape[:-1]
    split = array.reshape(lead + (NY, NZ * NC, ROWS))
    return jnp.swapaxes(split, -3, -2).reshape(lead + (D,))


def to_given_order(array):
    lead = array.shape[:-1]
    split = array.reshape(lead + (NZ * NC, NY, ROWS))
    return jnp.swapaxes(split, -3, -2).reshape(lead + (D,))


def exchange(array, axes):
    return lax.all_to_all(array, axes, split_axis=0, concat_axis=0, tiled=True)


def body(latent, modulation, w_qkv, w_out, stale):
    x_at, y_at = lax.axis_index("x"), lax.axis_index("y")
    pair_at = lax.axis_index("z") * NC + lax.axis_index("c")
    place = jnp.stack([2 * pair_at, y_at % 2]).astype(jnp.int32)

    sent = pl.pallas_call(
        pack_kernel,
        out_shape=jax.ShapeDtypeStruct((MEMBERS, PIECE, HD), jnp.bfloat16),
        in_specs=[ANY, ANY, VMEM],
        out_specs=VMEM,
        scratch_shapes=[
            pltpu.VMEM((ROWS, 3 * D), jnp.bfloat16),
            pltpu.VMEM((ROWS, D), jnp.bfloat16),
            pltpu.SemaphoreType.DMA((2,)),
        ],
        compiler_params=PARAMS,
        name="pack",
    )(w_qkv[0], w_out[0].T, jnp.swapaxes(stale[0, :, 0], 0, 1))
    received = exchange(sent, HEAD_AXES).reshape(BLOCKS, NY, PIECE, HD)

    def gather(block):
        return lax.all_gather(received[block], REST_AXES, axis=0, tiled=True)

    pieces = [gather(block) for block in range(BLOCKS)]

    terms = to_own_order(lax.all_gather(modulation[0], "x", axis=0, tiled=False))
    mine = exchange(latent[:, 0], REST_AXES).reshape(NZ * NC, 2, D)
    mine = jnp.swapaxes(mine, 0, 1).reshape(NZ * NC * 2, D)
    current = to_own_order(lax.dynamic_slice_in_dim(mine, x_at * OWN, OWN, 0))

    def term(block, which):
        return terms[block, which][None]

    spread = jax.ShapeDtypeStruct((LOCAL, D), jnp.bfloat16)
    weight = pltpu.VMEM((SOURCES, ROWS, HD), jnp.bfloat16)
    cache = pltpu.VMEM((SOURCES, PATCHES, HD), jnp.bfloat16)
    owned = jax.ShapeDtypeStruct((OWN, D), jnp.bfloat16)
    normed = pl.pallas_call(
        first_kernel,
        out_shape=spread,
        in_specs=[VMEM] * 3,
        out_specs=VMEM,
        compiler_params=PARAMS,
        name="first",
    )(current, term(0, 0), term(0, 1))
    outputs = []
    for block in range(BLOCKS):
        rows = exchange(normed, HEAD_AXES)
        left, given = pl.pallas_call(
            project_kernel,
            out_shape=(
                jax.ShapeDtypeStruct((LEFT, HD), jnp.bfloat16),
                jax.ShapeDtypeStruct((PT, HD), jnp.bfloat16),
            ),
            in_specs=[SMEM, VMEM, ANY],
            out_specs=(VMEM, VMEM),
            scratch_shapes=[weight] * 5 + [pltpu.SemaphoreType.DMA((5,))],
            compiler_params=PARAMS,
            cost_estimate=pl.CostEstimate(
                flops=2 * LOCAL * D * 5 * HD,
                bytes_accessed=2 * 5 * D * HD + 2 * LOCAL * D,
                transcendentals=0,
            ),
            name="project",
        )(place, rows, pieces[block])
        got = lax.ppermute(given, "y", [(at, at ^ 1) for at in range(NY)])
        attended = pl.pallas_call(
            own_kernel,
            out_shape=jax.ShapeDtypeStruct((LOCAL, HD), jnp.bfloat16),
            in_specs=[SMEM, VMEM, ANY],
            out_specs=VMEM,
            scratch_shapes=[cache] * 2 + [pltpu.SemaphoreType.DMA((2,))],
            compiler_params=PARAMS,
            cost_estimate=pl.CostEstimate(
                flops=4 * LOCAL * PATCHES * PT * HD,
                bytes_accessed=4 * PATCHES * PT * HD,
                transcendentals=LOCAL * PATCHES * PT,
            ),
            name="own",
        )(place, left, pieces[block])
        partial = pl.pallas_call(
            finish_kernel,
            out_shape=spread,
            in_specs=[SMEM, VMEM, VMEM, VMEM, ANY],
            out_specs=VMEM,
            scratch_shapes=[cache] * 2 + [weight] * 2 + [pltpu.SemaphoreType.DMA((4,))],
            compiler_params=PARAMS,
            cost_estimate=pl.CostEstimate(
                flops=4 * PT * PATCHES * PT * HD + 4 * LOCAL * D * HD,
                bytes_accessed=4 * PATCHES * PT * HD + 4 * D * HD + 2 * LOCAL * D,
                transcendentals=PT * PATCHES * PT,
            ),
            name="finish",
        )(place, left, attended, got, pieces[block])
        parts = exchange(partial, HEAD_AXES)
        if block + 1 < BLOCKS:
            current, normed = pl.pallas_call(
                middle_kernel,
                out_shape=(owned, spread),
                in_specs=[VMEM] * 5,
                out_specs=(VMEM, VMEM),
                compiler_params=PARAMS,
                name="middle",
            )(parts, current, term(block, 2), term(block + 1, 0), term(block + 1, 1))
        else:
            current = pl.pallas_call(
                last_kernel,
                out_shape=owned,
                in_specs=[VMEM] * 3,
                out_specs=VMEM,
                compiler_params=PARAMS,
                name="last",
            )(parts, current, term(block, 2))
        outputs.append(to_given_order(current))
    placed = exchange(jnp.concatenate(outputs, axis=0), "x")
    placed = jnp.swapaxes(placed.reshape(2, NZ * NC, D), 0, 1).reshape(PATCHES, D)
    placed = exchange(placed, REST_AXES)
    return placed[None, :, None]


def solution(mesh):
    own_mesh = Mesh(mesh.devices.reshape(NX, NY, NZ, NC), ("x",) + SP)
    return jax.shard_map(
        body,
        mesh=own_mesh,
        in_specs=(
            P(None, SP, None),
            P("x", None, None),
            P("x", SP, None),
            P("x", None, SP),
            P("x", None, SP, None, None),
        ),
        out_specs=P("x", None, SP, None),
        check_vma=False,
    )
```

```python
import math

import jax
import jax.numpy as jnp
from jax import lax
from jax.experimental import pallas as pl
from jax.experimental.pallas import tpu as pltpu
from jax.sharding import Mesh
from jax.sharding import PartitionSpec as P

D = 3072
HEADS = 24
HD = 128
PT = 64
PATCHES = 32
BLOCKS = 4
NX, NY, NZ, NC = 4, 4, 8, 2
SP = ("y", "z", "c")
HEAD_AXES = ("x", "y")
REST_AXES = ("z", "c")
MEMBERS = NX * NY
SOURCES = NY * NZ * NC
ROWS = D // SOURCES
OWN = 8
LOCAL = 2 * PT
AT_OUT, AT_K, AT_V, AT_SHARED = 3 * ROWS, 4 * ROWS, 4 * ROWS + PATCHES, 4 * ROWS + 2 * PATCHES
AT_SHARED_VO = AT_SHARED + ROWS
AT_SHARED_K = AT_SHARED + 2 * ROWS
AT_SHARED_V = AT_SHARED_K + PATCHES // 2
PIECE = AT_SHARED_V + PATCHES // 2
HALF = HD // 2
ANY = pl.BlockSpec(memory_space=pl.ANY)
SMEM = pl.BlockSpec(memory_space=pltpu.SMEM)
VMEM = pl.BlockSpec(memory_space=pltpu.VMEM)
PARAMS = pltpu.CompilerParams(vmem_limit_bytes=48 * 1024 * 1024)


def head_norm(values):
    return (
        values * lax.rsqrt(jnp.mean(values * values, axis=-1, keepdims=True) + 1e-06)
    ).astype(jnp.bfloat16)


def modulate(rows, shift_term, scale_term):
    average = jnp.mean(rows, axis=-1, keepdims=True)
    centered = rows - average
    variance = jnp.mean(centered * centered, axis=-1, keepdims=True)
    return (centered * lax.rsqrt(variance + 1e-06) * (1.0 + scale_term) + shift_term).astype(
        jnp.bfloat16
    )


def pack_kernel(qkv_from, out_from, stale_ref, sent_ref, qkv_ref, out_ref, sems):
    copies = [
        pltpu.make_async_copy(qkv_from, qkv_ref, sems.at[0]),
        pltpu.make_async_copy(out_from, out_ref, sems.at[1]),
    ]
    for copy in copies:
        copy.start()

    def columns(head):
        return slice(head * HD, (head + 1) * HD)

    def put(member, low, rows):
        sent_ref[member, low : low + rows.shape[0], :] = rows

    def each():
        for member in range(MEMBERS):
            triple, half = divmod(member, 2)
            yield member, half, 3 * triple + 2 * half, 3 * triple + 1

    for member, half, own, shared in each():
        put(member, AT_K, stale_ref[0, :, columns(own)])
        put(member, AT_V, stale_ref[1, :, columns(own)])
        some = slice(half * PATCHES // 2, (half + 1) * PATCHES // 2)
        put(member, AT_SHARED_K, stale_ref[0, some, columns(shared)])
        put(member, AT_SHARED_V, stale_ref[1, some, columns(shared)])
    copies[1].wait()
    for member, half, own, shared in each():
        put(member, AT_OUT, out_ref[:, columns(own)])
    copies[0].wait()
    for member, half, own, shared in each():
        for part in range(3):
            put(member, part * ROWS, qkv_ref[:, columns(part * HEADS + own)])
        put(member, AT_SHARED, qkv_ref[:, columns(half * HEADS + shared)])
        w_v = qkv_ref[:, columns(2 * HEADS + shared)]
        w_o = out_ref[:, columns(shared)]
        lanes = slice(half * HALF, (half + 1) * HALF)
        put(member, AT_SHARED_VO, jnp.concatenate([w_v[:, lanes], w_o[:, lanes]], axis=1))


def first_kernel(rows_ref, shift_ref, scale_ref, normed_ref):
    normed = modulate(rows_ref[...].astype(jnp.float32), shift_ref[...], scale_ref[...])
    twice = jnp.concatenate([normed, normed], axis=0)
    for at in range(0, LOCAL, 2 * OWN):
        normed_ref[at : at + 2 * OWN, :] = twice


def sum_rows(parts_ref, rows_ref, gate_ref):
    total = jnp.zeros((2 * OWN, D), jnp.float32)
    for at in range(0, LOCAL, 2 * OWN):
        total = total + parts_ref[at : at + 2 * OWN, :].astype(jnp.float32)
    summed = total[:OWN] + total[OWN:]
    return (rows_ref[...].astype(jnp.float32) + gate_ref[...] * summed).astype(jnp.bfloat16)


def middle_kernel(parts_ref, rows_ref, gate_ref, shift_ref, scale_ref, updated_ref, normed_ref):
    updated = sum_rows(parts_ref, rows_ref, gate_ref)
    updated_ref[...] = updated
    normed = modulate(updated.astype(jnp.float32), shift_ref[...], scale_ref[...])
    twice = jnp.concatenate([normed, normed], axis=0)
    for at in range(0, LOCAL, 2 * OWN):
        normed_ref[at : at + 2 * OWN, :] = twice


def last_kernel(parts_ref, rows_ref, gate_ref, updated_ref):
    updated_ref[...] = sum_rows(parts_ref, rows_ref, gate_ref)


def across(left, right):
    return lax.dot_general(
        left, right, (((1,), (1,)), ((), ())), preferred_element_type=jnp.float32
    )


def fetch(pieces_ref, sems, wanted):
    copies = [
        pltpu.make_async_copy(
            pieces_ref.at[:, low : low + target.shape[1], :], target, sems.at[number]
        )
        for number, (target, low) in enumerate(wanted)
    ]
    for copy in copies:
        copy.start()
    return copies


def project(rows, *parts):
    weight = jnp.concatenate([part[...].reshape(D, HD) for part in parts], axis=1)
    return jnp.dot(rows, weight, preferred_element_type=jnp.float32)


def low_lanes(rows):
    return lax.broadcasted_iota(jnp.int32, (rows, HD), 1) < HALF


def pick(half, both):
    return jnp.where(half == 0, both[:PT], both[PT:])


def shared_project_kernel(place_ref, rows_ref, pieces_ref, kept_ref, given_ref, w_qk, w_vo, sems):
    copies = fetch(pieces_ref, sems, [(w_qk, AT_SHARED), (w_vo, AT_SHARED_VO)])
    half = place_ref[1]
    rows = rows_ref[...]
    for copy in copies:
        copy.wait()
    both = project(rows, w_qk, w_vo)
    normed = head_norm(both[:, :HD])
    values = jnp.where(low_lanes(LOCAL), both[:, HD:], 0.0).astype(jnp.bfloat16)
    kept_ref[:LOCAL] = normed
    kept_ref[LOCAL:] = pick(half, values)
    given_ref[:LOCAL] = normed
    given_ref[LOCAL:] = pick(1 - half, values)


def own_project_kernel(rows_ref, pieces_ref, own_ref, w_q, w_k, w_v, sems):
    copies = fetch(pieces_ref, sems, [(w_q, 0), (w_k, ROWS), (w_v, 2 * ROWS)])
    rows = rows_ref[...]
    copies[0].wait()
    copies[1].wait()
    both = project(rows, w_q, w_k)
    own_ref[:LOCAL] = head_norm(both[:, :HD])
    own_ref[LOCAL : 2 * LOCAL] = head_norm(both[:, HD:])
    copies[2].wait()
    own_ref[2 * LOCAL :] = project(rows, w_v).astype(jnp.bfloat16)


def weigh(queries, keys):
    return jnp.exp(across(queries, keys) * (1.0 / math.sqrt(HD)))


def gather_values(numerator, values):
    return jnp.dot(numerator.astype(jnp.bfloat16), values, preferred_element_type=jnp.float32)


def attend_stale(queries, keys, values, first_column, row_patch, total, gathered):
    patches = keys.shape[1]
    step = 512 // patches
    shape = (queries.shape[0], step * patches)
    column_patch = first_column + lax.broadcasted_iota(jnp.int32, shape, 1) % patches
    stale_here = column_patch != row_patch
    for low in range(0, SOURCES, step):
        some_keys = keys[low : low + step].reshape(step * patches, HD)
        some_values = values[low : low + step].reshape(step * patches, HD)
        numerator = jnp.where(stale_here, weigh(queries, some_keys), 0.0)
        total = total + jnp.sum(numerator, axis=1, keepdims=True)
        gathered = gathered + gather_values(numerator, some_values)
    return total, gathered


def patch_of_rows(place_ref):
    second = lax.broadcasted_iota(jnp.int32, (LOCAL, 1), 0) >= PT
    return place_ref[0] + second.astype(jnp.int32)


def shared_attend_kernel(
    place_ref, kept_ref, got_ref, earlier_ref, pieces_ref, sums_ref, given_ref, keys, values, sems
):
    del earlier_ref
    copies = fetch(pieces_ref, sems, [(keys, AT_SHARED_K), (values, AT_SHARED_V)])
    half = place_ref[1]
    kept, got = kept_ref[:LOCAL], got_ref[:LOCAL]
    queries = jnp.where(half == 0, kept, got)
    fresh_keys = jnp.where(half == 0, got[:PT], kept[PT:])
    mine, other = kept_ref[LOCAL:].astype(jnp.float32), got_ref[LOCAL:].astype(jnp.float32)
    low = jnp.where(half == 0, mine, other)
    high = jnp.where(half == 0, other, mine)
    fresh_values = jnp.where(low_lanes(PT), low, pltpu.roll(high, HALF, 1)).astype(jnp.bfloat16)
    fresh = weigh(pick(half, queries), fresh_keys)

    def placed(rows):
        nothing = jnp.zeros_like(rows)
        return jnp.concatenate(
            [jnp.where(half == 0, rows, nothing), jnp.where(half == 0, nothing, rows)], axis=0
        )

    total = placed(jnp.sum(fresh, axis=1, keepdims=True))
    gathered = placed(gather_values(fresh, fresh_values))
    for copy in copies:
        copy.wait()
    total, gathered = attend_stale(
        queries,
        keys,
        values,
        half * (PATCHES // 2),
        patch_of_rows(place_ref),
        total,
        gathered,
    )
    swapped = pltpu.roll(gathered, HALF, 1)
    first = low_lanes(LOCAL)
    sums_ref[...] = jnp.where(first, total, jnp.where(half == 0, swapped, gathered))
    given_ref[...] = jnp.where(first, total, jnp.where(half == 0, gathered, swapped))


def own_attend_kernel(place_ref, own_ref, earlier_ref, pieces_ref, attended_ref, keys, values, sems):
    del earlier_ref
    copies = fetch(pieces_ref, sems, [(keys, AT_K), (values, AT_V)])
    queries = own_ref[:LOCAL]
    fresh = weigh(queries, own_ref[LOCAL : 2 * LOCAL])
    row_at = lax.broadcasted_iota(jnp.int32, (LOCAL, 1), 0)
    column_at = lax.broadcasted_iota(jnp.int32, (LOCAL, LOCAL), 1)
    fresh = jnp.where((row_at >= PT) == (column_at >= PT), fresh, 0.0)
    total = jnp.sum(fresh, axis=1, keepdims=True)
    gathered = gather_values(fresh, own_ref[2 * LOCAL :])
    for copy in copies:
        copy.wait()
    total, gathered = attend_stale(
        queries, keys, values, 0, patch_of_rows(place_ref), total, gathered
    )
    attended_ref[...] = (gathered / total).astype(jnp.bfloat16)


def finish_kernel(attended_ref, sums_ref, got_ref, pieces_ref, partial_ref, w_own, w_vo, sems):
    copies = fetch(pieces_ref, sems, [(w_own, AT_OUT), (w_vo, AT_SHARED_VO)])
    sums = sums_ref[...] + got_ref[...]
    shared = jnp.where(low_lanes(LOCAL), 0.0, sums / sums[:, :1]).astype(jnp.bfloat16)
    attention = jnp.concatenate([attended_ref[...], shared], axis=1)
    for copy in copies:
        copy.wait()
    step = 8
    width = step * ROWS
    for low in range(0, SOURCES, step):
        weight = jnp.concatenate(
            [
                w_own[low : low + step].reshape(width, HD),
                w_vo[low : low + step].reshape(width, HD),
            ],
            axis=1,
        )
        partial_ref[:, low * ROWS : low * ROWS + width] = across(attention, weight).astype(
            jnp.bfloat16
        )


def to_own_order(array):
    lead = array.shape[:-1]
    split = array.reshape(lead + (NY, NZ * NC, ROWS))
    return jnp.swapaxes(split, -3, -2).reshape(lead + (D,))


def to_given_order(array):
    lead = array.shape[:-1]
    split = array.reshape(lead + (NZ * NC, NY, ROWS))
    return jnp.swapaxes(split, -3, -2).reshape(lead + (D,))


def exchange(array, axes):
    return lax.all_to_all(array, axes, split_axis=0, concat_axis=0, tiled=True)


def body(latent, modulation, w_qkv, w_out, stale):
    x_at, y_at = lax.axis_index("x"), lax.axis_index("y")
    pair_at = lax.axis_index("z") * NC + lax.axis_index("c")
    place = jnp.stack([2 * pair_at, y_at % 2]).astype(jnp.int32)

    sent = pl.pallas_call(
        pack_kernel,
        out_shape=jax.ShapeDtypeStruct((MEMBERS, PIECE, HD), jnp.bfloat16),
        in_specs=[ANY, ANY, VMEM],
        out_specs=VMEM,
        scratch_shapes=[
            pltpu.VMEM((ROWS, 3 * D), jnp.bfloat16),
            pltpu.VMEM((ROWS, D), jnp.bfloat16),
            pltpu.SemaphoreType.DMA((2,)),
        ],
        compiler_params=PARAMS,
        name="pack",
    )(w_qkv[0], w_out[0].T, jnp.swapaxes(stale[0, :, 0], 0, 1))
    received = exchange(sent, HEAD_AXES).reshape(BLOCKS, NY, PIECE, HD)

    def gather(block):
        return lax.all_gather(received[block], REST_AXES, axis=0, tiled=True)

    pieces = [gather(block) for block in range(BLOCKS)]

    terms = to_own_order(lax.all_gather(modulation[0], "x", axis=0, tiled=False))
    mine = exchange(latent[:, 0], REST_AXES).reshape(NZ * NC, 2, D)
    mine = jnp.swapaxes(mine, 0, 1).reshape(NZ * NC * 2, D)
    current = to_own_order(lax.dynamic_slice_in_dim(mine, x_at * OWN, OWN, 0))

    def term(block, which):
        return terms[block, which][None]

    spread = jax.ShapeDtypeStruct((LOCAL, D), jnp.bfloat16)
    weight = pltpu.VMEM((SOURCES, ROWS, HD), jnp.bfloat16)
    cache = pltpu.VMEM((SOURCES, PATCHES, HD), jnp.bfloat16)
    owned = jax.ShapeDtypeStruct((OWN, D), jnp.bfloat16)
    normed = pl.pallas_call(
        first_kernel,
        out_shape=spread,
        in_specs=[VMEM] * 3,
        out_specs=VMEM,
        compiler_params=PARAMS,
        name="first",
    )(current, term(0, 0), term(0, 1))
    half_cache = pltpu.VMEM((SOURCES, PATCHES // 2, HD), jnp.bfloat16)
    sums_of = jax.ShapeDtypeStruct((LOCAL, HD), jnp.float32)

    def rows_of(count):
        return jax.ShapeDtypeStruct((count, HD), jnp.bfloat16)

    def local(kernel, in_specs, out_specs, out_shape, scratch, elements):
        return pl.pallas_call(
            kernel,
            out_shape=out_shape,
            in_specs=in_specs,
            out_specs=out_specs,
            scratch_shapes=scratch + [pltpu.SemaphoreType.DMA((len(scratch),))],
            compiler_params=PARAMS,
            cost_estimate=pl.CostEstimate(
                flops=2 * LOCAL * elements, bytes_accessed=2 * elements, transcendentals=0
            ),
            name=kernel.__name__,
        )

    def swap(array):
        return lax.ppermute(array, "y", [(at, at ^ 1) for at in range(NY)])

    outputs = []
    for block in range(BLOCKS):
        rows = exchange(normed, HEAD_AXES)
        source = pieces[block]
        kept, given = local(
            shared_project_kernel, (SMEM, VMEM, ANY), (VMEM, VMEM),
            (rows_of(LOCAL + PT), rows_of(LOCAL + PT)), [weight] * 2, 2 * D * HD,
        )(place, rows, source)
        got = swap(given)
        own = local(
            own_project_kernel, (VMEM, ANY), VMEM, rows_of(3 * LOCAL), [weight] * 3, 3 * D * HD,
        )(rows, source)
        sums, given = local(
            shared_attend_kernel, (SMEM, VMEM, VMEM, VMEM, ANY), (VMEM, VMEM),
            (sums_of, sums_of), [half_cache] * 2, PATCHES * PT * HD,
        )(place, kept, got, own, source)
        got = swap(given)
        attended = local(
            own_attend_kernel, (SMEM, VMEM, VMEM, ANY), VMEM,
            rows_of(LOCAL), [cache] * 2, 2 * PATCHES * PT * HD,
        )(place, own, sums, source)
        partial = local(
            finish_kernel, (VMEM, VMEM, VMEM, ANY), VMEM, spread, [weight] * 2, 2 * D * HD,
        )(attended, sums, got, source)
        parts = exchange(partial, HEAD_AXES)
        if block + 1 < BLOCKS:
            current, normed = pl.pallas_call(
                middle_kernel,
                out_shape=(owned, spread),
                in_specs=[VMEM] * 5,
                out_specs=(VMEM, VMEM),
                compiler_params=PARAMS,
                name="middle",
            )(parts, current, term(block, 2), term(block + 1, 0), term(block + 1, 1))
        else:
            current = pl.pallas_call(
                last_kernel,
                out_shape=owned,
                in_specs=[VMEM] * 3,
                out_specs=VMEM,
                compiler_params=PARAMS,
                name="last",
            )(parts, current, term(block, 2))
        outputs.append(to_given_order(current))
    placed = exchange(jnp.concatenate(outputs, axis=0), "x")
    placed = jnp.swapaxes(placed.reshape(2, NZ * NC, D), 0, 1).reshape(PATCHES, D)
    placed = exchange(placed, REST_AXES)
    return placed[None, :, None]


def solution(mesh):
    own_mesh = Mesh(mesh.devices.reshape(NX, NY, NZ, NC), ("x",) + SP)
    return jax.shard_map(
        body,
        mesh=own_mesh,
        in_specs=(
            P(None, SP, None),
            P("x", None, None),
            P("x", SP, None),
            P("x", None, SP),
            P("x", None, SP, None, None),
        ),
        out_specs=P("x", None, SP, None),
        check_vma=False,
    )
```

```python
import math

import jax
import jax.numpy as jnp
from jax import lax
from jax.experimental import pallas as pl
from jax.experimental.pallas import tpu as pltpu
from jax.sharding import Mesh
from jax.sharding import PartitionSpec as P

D = 3072
HEADS = 24
HD = 128
PT = 64
PATCHES = 32
BLOCKS = 4
NX, NY, NZ, NC = 4, 4, 8, 2
SP = ("y", "z", "c")
HEAD_AXES = ("x", "y")
REST_AXES = ("z", "c")
MEMBERS = NX * NY
SOURCES = NY * NZ * NC
ROWS = D // SOURCES
OWN = 8
LOCAL = 2 * PT
AT_OUT, AT_K, AT_V, AT_SHARED = 3 * ROWS, 4 * ROWS, 4 * ROWS + PATCHES, 4 * ROWS + 2 * PATCHES
AT_SHARED_VO = AT_SHARED + ROWS
AT_SHARED_K = AT_SHARED + 2 * ROWS
AT_SHARED_V = AT_SHARED_K + PATCHES // 2
PIECE = AT_SHARED_V + PATCHES // 2
HALF = HD // 2
ANY = pl.BlockSpec(memory_space=pl.ANY)
SMEM = pl.BlockSpec(memory_space=pltpu.SMEM)
VMEM = pl.BlockSpec(memory_space=pltpu.VMEM)
SMALL = pltpu.CompilerParams(vmem_limit_bytes=24 * 1024 * 1024)
PARAMS = pltpu.CompilerParams(vmem_limit_bytes=48 * 1024 * 1024)


def head_norm(values):
    return (
        values * lax.rsqrt(jnp.mean(values * values, axis=-1, keepdims=True) + 1e-06)
    ).astype(jnp.bfloat16)


def modulate(rows, shift_term, scale_term):
    average = jnp.mean(rows, axis=-1, keepdims=True)
    centered = rows - average
    variance = jnp.mean(centered * centered, axis=-1, keepdims=True)
    return (centered * lax.rsqrt(variance + 1e-06) * (1.0 + scale_term) + shift_term).astype(
        jnp.bfloat16
    )


def pack_kernel(qkv_from, out_from, stale_ref, sent_ref, qkv_ref, out_ref, sems):
    copies = [
        pltpu.make_async_copy(qkv_from, qkv_ref, sems.at[0]),
        pltpu.make_async_copy(out_from, out_ref, sems.at[1]),
    ]
    for copy in copies:
        copy.start()

    def columns(head):
        return slice(head * HD, (head + 1) * HD)

    def put(member, low, rows):
        sent_ref[member, low : low + rows.shape[0], :] = rows

    def each():
        for member in range(MEMBERS):
            triple, half = divmod(member, 2)
            yield member, half, 3 * triple + 2 * half, 3 * triple + 1

    for member, half, own, shared in each():
        put(member, AT_K, stale_ref[0, :, columns(own)])
        put(member, AT_V, stale_ref[1, :, columns(own)])
        some = slice(half * PATCHES // 2, (half + 1) * PATCHES // 2)
        put(member, AT_SHARED_K, stale_ref[0, some, columns(shared)])
        put(member, AT_SHARED_V, stale_ref[1, some, columns(shared)])
    copies[1].wait()
    for member, half, own, shared in each():
        put(member, AT_OUT, out_ref[:, columns(own)])
    copies[0].wait()
    for member, half, own, shared in each():
        for part in range(3):
            put(member, part * ROWS, qkv_ref[:, columns(part * HEADS + own)])
        put(member, AT_SHARED, qkv_ref[:, columns(half * HEADS + shared)])
        w_v = qkv_ref[:, columns(2 * HEADS + shared)]
        w_o = out_ref[:, columns(shared)]
        lanes = slice(half * HALF, (half + 1) * HALF)
        put(member, AT_SHARED_VO, jnp.concatenate([w_v[:, lanes], w_o[:, lanes]], axis=1))


def first_kernel(place_ref, rows_ref, shift_ref, scale_ref, normed_ref, blocks_ref):
    for block in range(BLOCKS):
        blocks_ref[block] = place_ref[2] + block
    normed = modulate(rows_ref[...].astype(jnp.float32), shift_ref[...], scale_ref[...])
    twice = jnp.concatenate([normed, normed], axis=0)
    for at in range(0, LOCAL, 2 * OWN):
        normed_ref[at : at + 2 * OWN, :] = twice


def sum_rows(parts_ref, rows_ref, gate_ref):
    total = jnp.zeros((2 * OWN, D), jnp.float32)
    for at in range(0, LOCAL, 2 * OWN):
        total = total + parts_ref[at : at + 2 * OWN, :].astype(jnp.float32)
    summed = total[:OWN] + total[OWN:]
    return (rows_ref[...].astype(jnp.float32) + gate_ref[...] * summed).astype(jnp.bfloat16)


def middle_kernel(parts_ref, rows_ref, gate_ref, shift_ref, scale_ref, updated_ref, normed_ref):
    updated = sum_rows(parts_ref, rows_ref, gate_ref)
    updated_ref[...] = updated
    normed = modulate(updated.astype(jnp.float32), shift_ref[...], scale_ref[...])
    twice = jnp.concatenate([normed, normed], axis=0)
    for at in range(0, LOCAL, 2 * OWN):
        normed_ref[at : at + 2 * OWN, :] = twice


def last_kernel(parts_ref, rows_ref, gate_ref, updated_ref):
    updated_ref[...] = sum_rows(parts_ref, rows_ref, gate_ref)


def across(left, right):
    return lax.dot_general(
        left, right, (((1,), (1,)), ((), ())), preferred_element_type=jnp.float32
    )


def fetch(pieces_ref, sems, wanted):
    copies = [
        pltpu.make_async_copy(
            pieces_ref.at[:, low : low + target.shape[1], :], target, sems.at[number]
        )
        for number, (target, low) in enumerate(wanted)
    ]
    for copy in copies:
        copy.start()
    return copies


def project(rows, *parts):
    weight = jnp.concatenate([part[...].reshape(D, HD) for part in parts], axis=1)
    return jnp.dot(rows, weight, preferred_element_type=jnp.float32)


def low_lanes(rows):
    return lax.broadcasted_iota(jnp.int32, (rows, HD), 1) < HALF


def pick(half, both):
    return jnp.where(half == 0, both[:PT], both[PT:])


def shared_project_kernel(place_ref, rows_ref, pieces_ref, kept_ref, given_ref, w_qk, w_vo, sems):
    copies = fetch(pieces_ref, sems, [(w_qk, AT_SHARED), (w_vo, AT_SHARED_VO)])
    half = place_ref[1]
    rows = rows_ref[...]
    for copy in copies:
        copy.wait()
    both = project(rows, w_qk, w_vo)
    normed = head_norm(both[:, :HD])
    values = jnp.where(low_lanes(LOCAL), both[:, HD:], 0.0).astype(jnp.bfloat16)
    kept_ref[:LOCAL] = normed
    kept_ref[LOCAL:] = pick(half, values)
    given_ref[:LOCAL] = normed
    given_ref[LOCAL:] = pick(1 - half, values)


def own_project_kernel(rows_ref, pieces_ref, own_ref, keys, values, w_q, w_k, w_v, sems):
    copies = fetch(
        pieces_ref,
        sems,
        [
            (w_q, 0),
            (w_k, ROWS),
            (w_v, 2 * ROWS),
            (keys, AT_SHARED_K),
            (values, AT_SHARED_V),
        ],
    )
    rows = rows_ref[...]
    copies[0].wait()
    copies[1].wait()
    both = project(rows, w_q, w_k)
    own_ref[:LOCAL] = head_norm(both[:, :HD])
    own_ref[LOCAL : 2 * LOCAL] = head_norm(both[:, HD:])
    copies[2].wait()
    own_ref[2 * LOCAL :] = project(rows, w_v).astype(jnp.bfloat16)
    copies[3].wait()
    copies[4].wait()


def weigh(queries, keys):
    return jnp.exp(across(queries, keys) * (1.0 / math.sqrt(HD)))


def gather_values(numerator, values):
    return jnp.dot(numerator.astype(jnp.bfloat16), values, preferred_element_type=jnp.float32)


def attend_stale(queries, keys, values, first_column, row_patch, total, gathered):
    patches = keys.shape[1]
    step = 512 // patches
    shape = (queries.shape[0], step * patches)
    column_patch = first_column + lax.broadcasted_iota(jnp.int32, shape, 1) % patches
    stale_here = column_patch != row_patch
    for low in range(0, SOURCES, step):
        some_keys = keys[low : low + step].reshape(step * patches, HD)
        some_values = values[low : low + step].reshape(step * patches, HD)
        numerator = jnp.where(stale_here, weigh(queries, some_keys), 0.0)
        total = total + jnp.sum(numerator, axis=1, keepdims=True)
        gathered = gathered + gather_values(numerator, some_values)
    return total, gathered


def patch_of_rows(place_ref):
    second = lax.broadcasted_iota(jnp.int32, (LOCAL, 1), 0) >= PT
    return place_ref[0] + second.astype(jnp.int32)


def shared_attend_kernel(
    place_ref, kept_ref, got_ref, keys, values, sums_ref, given_ref
):
    half = place_ref[1]
    kept, got = kept_ref[:LOCAL], got_ref[:LOCAL]
    queries = jnp.where(half == 0, kept, got)
    fresh_keys = jnp.where(half == 0, got[:PT], kept[PT:])
    mine, other = kept_ref[LOCAL:].astype(jnp.float32), got_ref[LOCAL:].astype(jnp.float32)
    low = jnp.where(half == 0, mine, other)
    high = jnp.where(half == 0, other, mine)
    fresh_values = jnp.where(low_lanes(PT), low, pltpu.roll(high, HALF, 1)).astype(jnp.bfloat16)
    fresh = weigh(pick(half, queries), fresh_keys)

    def placed(rows):
        nothing = jnp.zeros_like(rows)
        return jnp.concatenate(
            [jnp.where(half == 0, rows, nothing), jnp.where(half == 0, nothing, rows)], axis=0
        )

    total = placed(jnp.sum(fresh, axis=1, keepdims=True))
    gathered = placed(gather_values(fresh, fresh_values))
    total, gathered = attend_stale(
        queries,
        keys,
        values,
        half * (PATCHES // 2),
        patch_of_rows(place_ref),
        total,
        gathered,
    )
    swapped = pltpu.roll(gathered, HALF, 1)
    first = low_lanes(LOCAL)
    sums_ref[...] = jnp.where(first, total, jnp.where(half == 0, swapped, gathered))
    given_ref[...] = jnp.where(first, total, jnp.where(half == 0, gathered, swapped))


def own_attend_kernel(
    place_ref, own_ref, earlier_ref, pieces_ref, attended_ref, w_own, w_vo, keys, values, sems
):
    del earlier_ref
    copies = fetch(
        pieces_ref,
        sems,
        [(keys, AT_K), (values, AT_V), (w_own, AT_OUT), (w_vo, AT_SHARED_VO)],
    )
    queries = own_ref[:LOCAL]
    fresh = weigh(queries, own_ref[LOCAL : 2 * LOCAL])
    row_at = lax.broadcasted_iota(jnp.int32, (LOCAL, 1), 0)
    column_at = lax.broadcasted_iota(jnp.int32, (LOCAL, LOCAL), 1)
    fresh = jnp.where((row_at >= PT) == (column_at >= PT), fresh, 0.0)
    total = jnp.sum(fresh, axis=1, keepdims=True)
    gathered = gather_values(fresh, own_ref[2 * LOCAL :])
    copies[0].wait()
    copies[1].wait()
    total, gathered = attend_stale(
        queries, keys, values, 0, patch_of_rows(place_ref), total, gathered
    )
    attended_ref[...] = (gathered / total).astype(jnp.bfloat16)
    copies[2].wait()
    copies[3].wait()


def finish_kernel(attended_ref, sums_ref, got_ref, w_own, w_vo, partial_ref):
    sums = sums_ref[...] + got_ref[...]
    shared = jnp.where(low_lanes(LOCAL), 0.0, sums / sums[:, :1]).astype(jnp.bfloat16)
    attention = jnp.concatenate([attended_ref[...], shared], axis=1)
    step = 8
    width = step * ROWS
    for low in range(0, SOURCES, step):
        weight = jnp.concatenate(
            [
                w_own[low : low + step].reshape(width, HD),
                w_vo[low : low + step].reshape(width, HD),
            ],
            axis=1,
        )
        partial_ref[:, low * ROWS : low * ROWS + width] = across(attention, weight).astype(
            jnp.bfloat16
        )


def to_own_order(array):
    lead = array.shape[:-1]
    split = array.reshape(lead + (NY, NZ * NC, ROWS))
    return jnp.swapaxes(split, -3, -2).reshape(lead + (D,))


def to_given_order(array):
    lead = array.shape[:-1]
    split = array.reshape(lead + (NZ * NC, NY, ROWS))
    return jnp.swapaxes(split, -3, -2).reshape(lead + (D,))


def exchange(array, axes):
    return lax.all_to_all(array, axes, split_axis=0, concat_axis=0, tiled=True)


def body(latent, modulation, w_qkv, w_out, stale):
    x_at, y_at = lax.axis_index("x"), lax.axis_index("y")
    pair_at = lax.axis_index("z") * NC + lax.axis_index("c")
    place = jnp.stack([2 * pair_at, y_at % 2, 0 * y_at]).astype(jnp.int32)

    sent = pl.pallas_call(
        pack_kernel,
        out_shape=jax.ShapeDtypeStruct((MEMBERS, PIECE, HD), jnp.bfloat16),
        in_specs=[ANY, ANY, VMEM],
        out_specs=VMEM,
        scratch_shapes=[
            pltpu.VMEM((ROWS, 3 * D), jnp.bfloat16),
            pltpu.VMEM((ROWS, D), jnp.bfloat16),
            pltpu.SemaphoreType.DMA((2,)),
        ],
        compiler_params=PARAMS,
        name="pack",
    )(w_qkv[0], w_out[0].T, jnp.swapaxes(stale[0, :, 0], 0, 1))
    received = exchange(sent, HEAD_AXES).reshape(BLOCKS, NY, PIECE, HD)

    def gather(block):
        own_piece = lax.dynamic_index_in_dim(received, block, 0, keepdims=False)
        return lax.all_gather(own_piece, REST_AXES, axis=0, tiled=True)

    pieces = [gather(0)]

    terms = to_own_order(lax.all_gather(modulation[0], "x", axis=0, tiled=False))
    wanted = latent.reshape(NZ * NC, 2, D)
    wanted = lax.dynamic_index_in_dim(wanted, x_at // 2, 1, keepdims=False)
    mine = exchange(wanted, REST_AXES)
    current = to_own_order(lax.dynamic_slice_in_dim(mine, (x_at % 2) * OWN, OWN, 0))

    def term(block, which):
        return terms[block, which][None]

    spread = jax.ShapeDtypeStruct((LOCAL, D), jnp.bfloat16)
    weight = pltpu.VMEM((SOURCES, ROWS, HD), jnp.bfloat16)
    cache = pltpu.VMEM((SOURCES, PATCHES, HD), jnp.bfloat16)
    owned = jax.ShapeDtypeStruct((OWN, D), jnp.bfloat16)
    normed, blocks = pl.pallas_call(
        first_kernel,
        out_shape=(spread, jax.ShapeDtypeStruct((BLOCKS,), jnp.int32)),
        in_specs=[SMEM] + [VMEM] * 3,
        out_specs=(VMEM, SMEM),
        compiler_params=PARAMS,
        name="first",
    )(place, current, term(0, 0), term(0, 1))
    pieces += [gather(blocks[block]) for block in range(1, BLOCKS)]
    half_cache = jax.ShapeDtypeStruct((SOURCES, PATCHES // 2, HD), jnp.bfloat16)
    kept_weight = jax.ShapeDtypeStruct((SOURCES, ROWS, HD), jnp.bfloat16)
    sums_of = jax.ShapeDtypeStruct((LOCAL, HD), jnp.float32)

    def rows_of(count):
        return jax.ShapeDtypeStruct((count, HD), jnp.bfloat16)

    def local(kernel, in_specs, out_specs, out_shape, scratch, copies, elements):
        return pl.pallas_call(
            kernel,
            out_shape=out_shape,
            in_specs=in_specs,
            out_specs=out_specs,
            scratch_shapes=scratch + [pltpu.SemaphoreType.DMA((copies,))] * (copies > 0),
            compiler_params=PARAMS if copies else SMALL,
            cost_estimate=pl.CostEstimate(
                flops=2 * LOCAL * elements, bytes_accessed=2 * elements, transcendentals=0
            ),
            name=kernel.__name__,
        )

    def swap(array):
        return lax.ppermute(array, "y", [(at, at ^ 1) for at in range(NY)])

    outputs = []
    for block in range(BLOCKS):
        rows = exchange(normed, HEAD_AXES)
        source = pieces[block]
        kept, given = local(
            shared_project_kernel, (SMEM, VMEM, ANY), (VMEM, VMEM),
            (rows_of(LOCAL + PT), rows_of(LOCAL + PT)), [weight] * 2, 2, 2 * D * HD,
        )(place, rows, source)
        got = swap(given)
        own, keys, values = local(
            own_project_kernel, (VMEM, ANY), (VMEM, VMEM, VMEM),
            (rows_of(3 * LOCAL), half_cache, half_cache), [weight] * 3, 5, 3 * D * HD,
        )(rows, source)
        sums, given = local(
            shared_attend_kernel, (SMEM,) + (VMEM,) * 4, (VMEM, VMEM),
            (sums_of, sums_of), [], 0, PATCHES * PT * HD,
        )(place, kept, got, keys, values)
        got = swap(given)
        attended, w_own, w_vo = local(
            own_attend_kernel, (SMEM, VMEM, VMEM, ANY), (VMEM, VMEM, VMEM),
            (rows_of(LOCAL), kept_weight, kept_weight), [cache] * 2, 4, 2 * PATCHES * PT * HD,
        )(place, own, sums, source)
        partial = local(
            finish_kernel, (VMEM,) * 5, VMEM, spread, [], 0, 2 * D * HD,
        )(attended, sums, got, w_own, w_vo)
        parts = exchange(partial, HEAD_AXES)
        if block + 1 < BLOCKS:
            current, normed = pl.pallas_call(
                middle_kernel,
                out_shape=(owned, spread),
                in_specs=[VMEM] * 5,
                out_specs=(VMEM, VMEM),
                compiler_params=PARAMS,
                name="middle",
            )(parts, current, term(block, 2), term(block + 1, 0), term(block + 1, 1))
        else:
            current = pl.pallas_call(
                last_kernel,
                out_shape=owned,
                in_specs=[VMEM] * 3,
                out_specs=VMEM,
                compiler_params=PARAMS,
                name="last",
            )(parts, current, term(block, 2))
        outputs.append(to_given_order(current))
    placed = exchange(jnp.concatenate(outputs, axis=0), "x")
    placed = jnp.swapaxes(placed.reshape(2, NZ * NC, D), 0, 1).reshape(PATCHES, D)
    placed = exchange(placed, REST_AXES)
    return placed[None, :, None]


def solution(mesh):
    own_mesh = Mesh(mesh.devices.reshape(NX, NY, NZ, NC), ("x",) + SP)
    return jax.shard_map(
        body,
        mesh=own_mesh,
        in_specs=(
            P(None, SP, None),
            P("x", None, None),
            P("x", SP, None),
            P("x", None, SP),
            P("x", None, SP, None, None),
        ),
        out_specs=P("x", None, SP, None),
        check_vma=False,
    )
```

```python
import math

import jax
import jax.numpy as jnp
from jax import lax
from jax.experimental import pallas as pl
from jax.experimental.pallas import tpu as pltpu
from jax.sharding import Mesh
from jax.sharding import PartitionSpec as P

D = 3072
HEADS = 24
HD = 128
PT = 64
PATCHES = 32
BLOCKS = 4
NX, NY, NZ, NC = 4, 4, 8, 2
SP = ("y", "z", "c")
HEAD_AXES = ("x", "y")
REST_AXES = ("z", "c")
MEMBERS = NX * NY
SOURCES = NY * NZ * NC
ROWS = D // SOURCES
OWN = 8
LOCAL = 2 * PT
AT_OUT, AT_K, AT_V, AT_SHARED = 3 * ROWS, 4 * ROWS, 4 * ROWS + PATCHES, 4 * ROWS + 2 * PATCHES
AT_SHARED_VO = AT_SHARED + ROWS
AT_SHARED_K = AT_SHARED + 2 * ROWS
AT_SHARED_V = AT_SHARED_K + PATCHES // 2
PIECE = AT_SHARED_V + PATCHES // 2
HALF = HD // 2
ANY = pl.BlockSpec(memory_space=pl.ANY)
HBM = pl.BlockSpec(memory_space=pltpu.HBM)
SMEM = pl.BlockSpec(memory_space=pltpu.SMEM)
VMEM = pl.BlockSpec(memory_space=pltpu.VMEM)
SMALL = pltpu.CompilerParams(vmem_limit_bytes=24 * 1024 * 1024)
PARAMS = pltpu.CompilerParams(vmem_limit_bytes=48 * 1024 * 1024)


def head_norm(values):
    return (
        values * lax.rsqrt(jnp.mean(values * values, axis=-1, keepdims=True) + 1e-06)
    ).astype(jnp.bfloat16)


def modulate(rows, shift_term, scale_term):
    average = jnp.mean(rows, axis=-1, keepdims=True)
    centered = rows - average
    variance = jnp.mean(centered * centered, axis=-1, keepdims=True)
    return (centered * lax.rsqrt(variance + 1e-06) * (1.0 + scale_term) + shift_term).astype(
        jnp.bfloat16
    )


def pack_kernel(qkv_from, out_from, stale_ref, sent_ref, qkv_ref, out_ref, sems):
    copies = [
        pltpu.make_async_copy(qkv_from, qkv_ref, sems.at[0]),
        pltpu.make_async_copy(out_from, out_ref, sems.at[1]),
    ]
    for copy in copies:
        copy.start()

    def columns(head):
        return slice(head * HD, (head + 1) * HD)

    def put(member, low, rows):
        sent_ref[member, low : low + rows.shape[0], :] = rows

    def each():
        for member in range(MEMBERS):
            triple, half = divmod(member, 2)
            yield member, half, 3 * triple + 2 * half, 3 * triple + 1

    for member, half, own, shared in each():
        put(member, AT_K, stale_ref[0, :, columns(own)])
        put(member, AT_V, stale_ref[1, :, columns(own)])
        some = slice(half * PATCHES // 2, (half + 1) * PATCHES // 2)
        put(member, AT_SHARED_K, stale_ref[0, some, columns(shared)])
        put(member, AT_SHARED_V, stale_ref[1, some, columns(shared)])
    copies[1].wait()
    for member, half, own, shared in each():
        put(member, AT_OUT, out_ref[:, columns(own)])
    copies[0].wait()
    for member, half, own, shared in each():
        for part in range(3):
            put(member, part * ROWS, qkv_ref[:, columns(part * HEADS + own)])
        put(member, AT_SHARED, qkv_ref[:, columns(half * HEADS + shared)])
        w_v = qkv_ref[:, columns(2 * HEADS + shared)]
        w_o = out_ref[:, columns(shared)]
        lanes = slice(half * HALF, (half + 1) * HALF)
        put(member, AT_SHARED_VO, jnp.concatenate([w_v[:, lanes], w_o[:, lanes]], axis=1))


def cut_kernel(received_ref, earlier_ref, *rest):
    del earlier_ref
    targets, sems = rest[:-1], rest[-1]
    copies = [
        pltpu.make_async_copy(received_ref.at[block + 1], target, sems.at[block])
        for block, target in enumerate(targets)
    ]
    for copy in copies:
        copy.start()
    for copy in copies:
        copy.wait()


def first_kernel(rows_ref, shift_ref, scale_ref, normed_ref):
    normed = modulate(rows_ref[...].astype(jnp.float32), shift_ref[...], scale_ref[...])
    twice = jnp.concatenate([normed, normed], axis=0)
    for at in range(0, LOCAL, 2 * OWN):
        normed_ref[at : at + 2 * OWN, :] = twice


def sum_rows(parts_ref, rows_ref, gate_ref):
    total = jnp.zeros((2 * OWN, D), jnp.float32)
    for at in range(0, LOCAL, 2 * OWN):
        total = total + parts_ref[at : at + 2 * OWN, :].astype(jnp.float32)
    summed = total[:OWN] + total[OWN:]
    return (rows_ref[...].astype(jnp.float32) + gate_ref[...] * summed).astype(jnp.bfloat16)


def middle_kernel(parts_ref, rows_ref, gate_ref, shift_ref, scale_ref, updated_ref, normed_ref):
    updated = sum_rows(parts_ref, rows_ref, gate_ref)
    updated_ref[...] = updated
    normed = modulate(updated.astype(jnp.float32), shift_ref[...], scale_ref[...])
    twice = jnp.concatenate([normed, normed], axis=0)
    for at in range(0, LOCAL, 2 * OWN):
        normed_ref[at : at + 2 * OWN, :] = twice


def last_kernel(parts_ref, rows_ref, gate_ref, updated_ref):
    updated_ref[...] = sum_rows(parts_ref, rows_ref, gate_ref)


def across(left, right):
    return lax.dot_general(
        left, right, (((1,), (1,)), ((), ())), preferred_element_type=jnp.float32
    )


def fetch(pieces_ref, sems, wanted):
    copies = [
        pltpu.make_async_copy(
            pieces_ref.at[:, low : low + target.shape[1], :], target, sems.at[number]
        )
        for number, (target, low) in enumerate(wanted)
    ]
    for copy in copies:
        copy.start()
    return copies


def project(rows, *parts):
    weight = jnp.concatenate([part[...].reshape(D, HD) for part in parts], axis=1)
    return jnp.dot(rows, weight, preferred_element_type=jnp.float32)


def low_lanes(rows):
    return lax.broadcasted_iota(jnp.int32, (rows, HD), 1) < HALF


def pick(half, both):
    return jnp.where(half == 0, both[:PT], both[PT:])


def shared_project_kernel(place_ref, rows_ref, pieces_ref, kept_ref, given_ref, w_qk, w_vo, sems):
    copies = fetch(pieces_ref, sems, [(w_qk, AT_SHARED), (w_vo, AT_SHARED_VO)])
    half = place_ref[1]
    rows = rows_ref[...]
    for copy in copies:
        copy.wait()
    both = project(rows, w_qk, w_vo)
    normed = head_norm(both[:, :HD])
    values = jnp.where(low_lanes(LOCAL), both[:, HD:], 0.0).astype(jnp.bfloat16)
    kept_ref[:LOCAL] = normed
    kept_ref[LOCAL:] = pick(half, values)
    given_ref[:LOCAL] = normed
    given_ref[LOCAL:] = pick(1 - half, values)


def own_project_kernel(rows_ref, pieces_ref, own_ref, keys, values, w_q, w_k, w_v, sems):
    copies = fetch(
        pieces_ref,
        sems,
        [
            (w_q, 0),
            (w_k, ROWS),
            (w_v, 2 * ROWS),
            (keys, AT_SHARED_K),
            (values, AT_SHARED_V),
        ],
    )
    rows = rows_ref[...]
    copies[0].wait()
    copies[1].wait()
    both = project(rows, w_q, w_k)
    own_ref[:LOCAL] = head_norm(both[:, :HD])
    own_ref[LOCAL : 2 * LOCAL] = head_norm(both[:, HD:])
    copies[2].wait()
    own_ref[2 * LOCAL :] = project(rows, w_v).astype(jnp.bfloat16)
    copies[3].wait()
    copies[4].wait()


def weigh(queries, keys):
    return jnp.exp(across(queries, keys) * (1.0 / math.sqrt(HD)))


def gather_values(numerator, values):
    return jnp.dot(numerator.astype(jnp.bfloat16), values, preferred_element_type=jnp.float32)


def attend_stale(queries, keys, values, first_column, row_patch, total, gathered):
    patches = keys.shape[1]
    step = 512 // patches
    shape = (queries.shape[0], step * patches)
    column_patch = first_column + lax.broadcasted_iota(jnp.int32, shape, 1) % patches
    stale_here = column_patch != row_patch
    for low in range(0, SOURCES, step):
        some_keys = keys[low : low + step].reshape(step * patches, HD)
        some_values = values[low : low + step].reshape(step * patches, HD)
        numerator = jnp.where(stale_here, weigh(queries, some_keys), 0.0)
        total = total + jnp.sum(numerator, axis=1, keepdims=True)
        gathered = gathered + gather_values(numerator, some_values)
    return total, gathered


def patch_of_rows(place_ref):
    second = lax.broadcasted_iota(jnp.int32, (LOCAL, 1), 0) >= PT
    return place_ref[0] + second.astype(jnp.int32)


def shared_attend_kernel(
    place_ref, kept_ref, got_ref, keys, values, sums_ref, given_ref
):
    half = place_ref[1]
    kept, got = kept_ref[:LOCAL], got_ref[:LOCAL]
    queries = jnp.where(half == 0, kept, got)
    fresh_keys = jnp.where(half == 0, got[:PT], kept[PT:])
    mine, other = kept_ref[LOCAL:].astype(jnp.float32), got_ref[LOCAL:].astype(jnp.float32)
    low = jnp.where(half == 0, mine, other)
    high = jnp.where(half == 0, other, mine)
    fresh_values = jnp.where(low_lanes(PT), low, pltpu.roll(high, HALF, 1)).astype(jnp.bfloat16)
    fresh = weigh(pick(half, queries), fresh_keys)

    def placed(rows):
        nothing = jnp.zeros_like(rows)
        return jnp.concatenate(
            [jnp.where(half == 0, rows, nothing), jnp.where(half == 0, nothing, rows)], axis=0
        )

    total = placed(jnp.sum(fresh, axis=1, keepdims=True))
    gathered = placed(gather_values(fresh, fresh_values))
    total, gathered = attend_stale(
        queries,
        keys,
        values,
        half * (PATCHES // 2),
        patch_of_rows(place_ref),
        total,
        gathered,
    )
    swapped = pltpu.roll(gathered, HALF, 1)
    first = low_lanes(LOCAL)
    sums_ref[...] = jnp.where(first, total, jnp.where(half == 0, swapped, gathered))
    given_ref[...] = jnp.where(first, total, jnp.where(half == 0, gathered, swapped))


def own_attend_kernel(
    place_ref, own_ref, earlier_ref, pieces_ref, attended_ref, w_own, w_vo, keys, values, sems
):
    del earlier_ref
    copies = fetch(
        pieces_ref,
        sems,
        [(keys, AT_K), (values, AT_V), (w_own, AT_OUT), (w_vo, AT_SHARED_VO)],
    )
    queries = own_ref[:LOCAL]
    fresh = weigh(queries, own_ref[LOCAL : 2 * LOCAL])
    row_at = lax.broadcasted_iota(jnp.int32, (LOCAL, 1), 0)
    column_at = lax.broadcasted_iota(jnp.int32, (LOCAL, LOCAL), 1)
    fresh = jnp.where((row_at >= PT) == (column_at >= PT), fresh, 0.0)
    total = jnp.sum(fresh, axis=1, keepdims=True)
    gathered = gather_values(fresh, own_ref[2 * LOCAL :])
    copies[0].wait()
    copies[1].wait()
    total, gathered = attend_stale(
        queries, keys, values, 0, patch_of_rows(place_ref), total, gathered
    )
    attended_ref[...] = (gathered / total).astype(jnp.bfloat16)
    copies[2].wait()
    copies[3].wait()


def finish_kernel(attended_ref, sums_ref, got_ref, w_own, w_vo, partial_ref):
    sums = sums_ref[...] + got_ref[...]
    shared = jnp.where(low_lanes(LOCAL), 0.0, sums / sums[:, :1]).astype(jnp.bfloat16)
    attention = jnp.concatenate([attended_ref[...], shared], axis=1)
    step = 8
    width = step * ROWS
    for low in range(0, SOURCES, step):
        weight = jnp.concatenate(
            [
                w_own[low : low + step].reshape(width, HD),
                w_vo[low : low + step].reshape(width, HD),
            ],
            axis=1,
        )
        partial_ref[:, low * ROWS : low * ROWS + width] = across(attention, weight).astype(
            jnp.bfloat16
        )


def to_own_order(array):
    lead = array.shape[:-1]
    split = array.reshape(lead + (NY, NZ * NC, ROWS))
    return jnp.swapaxes(split, -3, -2).reshape(lead + (D,))


def to_given_order(array):
    lead = array.shape[:-1]
    split = array.reshape(lead + (NZ * NC, NY, ROWS))
    return jnp.swapaxes(split, -3, -2).reshape(lead + (D,))


def exchange(array, axes):
    return lax.all_to_all(array, axes, split_axis=0, concat_axis=0, tiled=True)


def body(latent, modulation, w_qkv, w_out, stale):
    x_at, y_at = lax.axis_index("x"), lax.axis_index("y")
    pair_at = lax.axis_index("z") * NC + lax.axis_index("c")
    place = jnp.stack([2 * pair_at, y_at % 2]).astype(jnp.int32)

    sent = pl.pallas_call(
        pack_kernel,
        out_shape=jax.ShapeDtypeStruct((MEMBERS, PIECE, HD), jnp.bfloat16),
        in_specs=[HBM, HBM, VMEM],
        out_specs=VMEM,
        scratch_shapes=[
            pltpu.VMEM((ROWS, 3 * D), jnp.bfloat16),
            pltpu.VMEM((ROWS, D), jnp.bfloat16),
            pltpu.SemaphoreType.DMA((2,)),
        ],
        compiler_params=PARAMS,
        name="pack",
    )(w_qkv[0], w_out[0].T, jnp.swapaxes(stale[0, :, 0], 0, 1))
    received = exchange(sent, HEAD_AXES).reshape(BLOCKS, NY, PIECE, HD)

    def gather(own_piece):
        return lax.all_gather(own_piece, REST_AXES, axis=0, tiled=True)

    pieces = [gather(received[0])]

    terms = to_own_order(lax.all_gather(modulation[0], "x", axis=0, tiled=False))
    wanted = latent.reshape(NZ * NC, 2, D)
    wanted = lax.dynamic_index_in_dim(wanted, x_at // 2, 1, keepdims=False)
    mine = exchange(wanted, REST_AXES)
    current = to_own_order(lax.dynamic_slice_in_dim(mine, (x_at % 2) * OWN, OWN, 0))

    def term(block, which):
        return terms[block, which][None]

    spread = jax.ShapeDtypeStruct((LOCAL, D), jnp.bfloat16)
    normed = pl.pallas_call(
        first_kernel,
        out_shape=spread,
        in_specs=[VMEM] * 3,
        out_specs=VMEM,
        compiler_params=PARAMS,
        name="first",
    )(current, term(0, 0), term(0, 1))
    later = pl.pallas_call(
        cut_kernel,
        out_shape=[jax.ShapeDtypeStruct((NY, PIECE, HD), jnp.bfloat16)] * (BLOCKS - 1),
        in_specs=[ANY, VMEM],
        out_specs=[HBM] * (BLOCKS - 1),
        scratch_shapes=[pltpu.SemaphoreType.DMA((BLOCKS - 1,))],
        name="cut",
    )(received, normed)
    pieces += [gather(own_piece) for own_piece in later]
    weight = pltpu.VMEM((SOURCES, ROWS, HD), jnp.bfloat16)
    cache = pltpu.VMEM((SOURCES, PATCHES, HD), jnp.bfloat16)
    owned = jax.ShapeDtypeStruct((OWN, D), jnp.bfloat16)
    half_cache = jax.ShapeDtypeStruct((SOURCES, PATCHES // 2, HD), jnp.bfloat16)
    kept_weight = jax.ShapeDtypeStruct((SOURCES, ROWS, HD), jnp.bfloat16)
    sums_of = jax.ShapeDtypeStruct((LOCAL, HD), jnp.float32)

    def rows_of(count):
        return jax.ShapeDtypeStruct((count, HD), jnp.bfloat16)

    def local(kernel, in_specs, out_specs, out_shape, scratch, copies, elements):
        return pl.pallas_call(
            kernel,
            out_shape=out_shape,
            in_specs=in_specs,
            out_specs=out_specs,
            scratch_shapes=scratch + [pltpu.SemaphoreType.DMA((copies,))] * (copies > 0),
            compiler_params=PARAMS if copies else SMALL,
            cost_estimate=pl.CostEstimate(
                flops=2 * LOCAL * elements, bytes_accessed=2 * elements, transcendentals=0
            ),
            name=kernel.__name__,
        )

    def swap(array):
        return lax.ppermute(array, "y", [(at, at ^ 1) for at in range(NY)])

    outputs = []
    for block in range(BLOCKS):
        rows = exchange(normed, HEAD_AXES)
        source = pieces[block]
        kept, given = local(
            shared_project_kernel, (SMEM, VMEM, HBM), (VMEM, VMEM),
            (rows_of(LOCAL + PT), rows_of(LOCAL + PT)), [weight] * 2, 2, 2 * D * HD,
        )(place, rows, source)
        got = swap(given)
        own, keys, values = local(
            own_project_kernel, (VMEM, HBM), (VMEM, VMEM, VMEM),
            (rows_of(3 * LOCAL), half_cache, half_cache), [weight] * 3, 5, 3 * D * HD,
        )(rows, source)
        sums, given = local(
            shared_attend_kernel, (SMEM,) + (VMEM,) * 4, (VMEM, VMEM),
            (sums_of, sums_of), [], 0, PATCHES * PT * HD,
        )(place, kept, got, keys, values)
        got = swap(given)
        attended, w_own, w_vo = local(
            own_attend_kernel, (SMEM, VMEM, VMEM, HBM), (VMEM, VMEM, VMEM),
            (rows_of(LOCAL), kept_weight, kept_weight), [cache] * 2, 4, 2 * PATCHES * PT * HD,
        )(place, own, sums, source)
        partial = local(
            finish_kernel, (VMEM,) * 5, VMEM, spread, [], 0, 2 * D * HD,
        )(attended, sums, got, w_own, w_vo)
        parts = exchange(partial, HEAD_AXES)
        if block + 1 < BLOCKS:
            current, normed = pl.pallas_call(
                middle_kernel,
                out_shape=(owned, spread),
                in_specs=[VMEM] * 5,
                out_specs=(VMEM, VMEM),
                compiler_params=PARAMS,
                name="middle",
            )(parts, current, term(block, 2), term(block + 1, 0), term(block + 1, 1))
        else:
            current = pl.pallas_call(
                last_kernel,
                out_shape=owned,
                in_specs=[VMEM] * 3,
                out_specs=VMEM,
                compiler_params=PARAMS,
                name="last",
            )(parts, current, term(block, 2))
        outputs.append(to_given_order(current))
    outputs = jnp.stack(outputs)
    moved = [lax.dynamic_index_in_dim(outputs, x_at, 0, keepdims=False)]
    for step in range(1, NX):
        leaving = lax.dynamic_index_in_dim(outputs, (x_at + step) % NX, 0, keepdims=False)
        moved.append(lax.ppermute(leaving, "x", [(at, (at + step) % NX) for at in range(NX)]))
    moved = jnp.stack(moved)
    placed = jnp.stack(
        [
            lax.dynamic_index_in_dim(moved, (x_at - origin) % NX, 0, keepdims=False)
            for origin in range(NX)
        ]
    )
    placed = jnp.swapaxes(placed.reshape(2, NZ * NC, D), 0, 1).reshape(PATCHES, D)
    placed = exchange(placed, REST_AXES)
    return placed[None, :, None]


def solution(mesh):
    own_mesh = Mesh(mesh.devices.reshape(NX, NY, NZ, NC), ("x",) + SP)
    return jax.shard_map(
        body,
        mesh=own_mesh,
        in_specs=(
            P(None, SP, None),
            P("x", None, None),
            P("x", SP, None),
            P("x", None, SP),
            P("x", None, SP, None, None),
        ),
        out_specs=P("x", None, SP, None),
        check_vma=False,
    )
```

```python
import math

import jax
import jax.numpy as jnp
from jax import lax
from jax.experimental import pallas as pl
from jax.experimental.pallas import tpu as pltpu
from jax.sharding import Mesh
from jax.sharding import PartitionSpec as P

D = 3072
HEADS = 24
HD = 128
PT = 64
PATCHES = 32
BLOCKS = 4
NX, NY, NZ, NC = 4, 4, 8, 2
SP = ("y", "z", "c")
HEAD_AXES = ("x", "y")
REST_AXES = ("z", "c")
MEMBERS = NX * NY
SOURCES = NY * NZ * NC
ROWS = D // SOURCES
OWN = 8
LOCAL = 2 * PT
AT_OUT, AT_K, AT_V, AT_SHARED = 3 * ROWS, 4 * ROWS, 4 * ROWS + PATCHES, 4 * ROWS + 2 * PATCHES
AT_SHARED_VO = AT_SHARED + ROWS
AT_SHARED_K = AT_SHARED + 2 * ROWS
AT_SHARED_V = AT_SHARED_K + PATCHES // 2
PIECE = AT_SHARED_V + PATCHES // 2
HALF = HD // 2
ANY = pl.BlockSpec(memory_space=pl.ANY)
SMEM = pl.BlockSpec(memory_space=pltpu.SMEM)
VMEM = pl.BlockSpec(memory_space=pltpu.VMEM)
SMALL = pltpu.CompilerParams(vmem_limit_bytes=24 * 1024 * 1024)
PARAMS = pltpu.CompilerParams(vmem_limit_bytes=48 * 1024 * 1024)


def head_norm(values):
    return (
        values * lax.rsqrt(jnp.mean(values * values, axis=-1, keepdims=True) + 1e-06)
    ).astype(jnp.bfloat16)


def modulate(rows, shift_term, scale_term):
    average = jnp.mean(rows, axis=-1, keepdims=True)
    centered = rows - average
    variance = jnp.mean(centered * centered, axis=-1, keepdims=True)
    return (centered * lax.rsqrt(variance + 1e-06) * (1.0 + scale_term) + shift_term).astype(
        jnp.bfloat16
    )


def pack_kernel(qkv_from, out_from, stale_ref, sent_ref, qkv_ref, out_ref, sems):
    copies = [
        pltpu.make_async_copy(qkv_from, qkv_ref, sems.at[0]),
        pltpu.make_async_copy(out_from, out_ref, sems.at[1]),
    ]
    for copy in copies:
        copy.start()

    def columns(head):
        return slice(head * HD, (head + 1) * HD)

    def put(member, low, rows):
        sent_ref[member, low : low + rows.shape[0], :] = rows

    def each():
        for member in range(MEMBERS):
            triple, half = divmod(member, 2)
            yield member, half, 3 * triple + 2 * half, 3 * triple + 1

    for member, half, own, shared in each():
        put(member, AT_K, stale_ref[0, :, columns(own)])
        put(member, AT_V, stale_ref[1, :, columns(own)])
        some = slice(half * PATCHES // 2, (half + 1) * PATCHES // 2)
        put(member, AT_SHARED_K, stale_ref[0, some, columns(shared)])
        put(member, AT_SHARED_V, stale_ref[1, some, columns(shared)])
    copies[1].wait()
    for member, half, own, shared in each():
        put(member, AT_OUT, out_ref[:, columns(own)])
    copies[0].wait()
    for member, half, own, shared in each():
        for part in range(3):
            put(member, part * ROWS, qkv_ref[:, columns(part * HEADS + own)])
        put(member, AT_SHARED, qkv_ref[:, columns(half * HEADS + shared)])
        w_v = qkv_ref[:, columns(2 * HEADS + shared)]
        w_o = out_ref[:, columns(shared)]
        lanes = slice(half * HALF, (half + 1) * HALF)
        put(member, AT_SHARED_VO, jnp.concatenate([w_v[:, lanes], w_o[:, lanes]], axis=1))


def first_kernel(rows_ref, shift_ref, scale_ref, normed_ref):
    normed = modulate(rows_ref[...].astype(jnp.float32), shift_ref[...], scale_ref[...])
    twice = jnp.concatenate([normed, normed], axis=0)
    for at in range(0, LOCAL, 2 * OWN):
        normed_ref[at : at + 2 * OWN, :] = twice


def sum_rows(parts_ref, rows_ref, gate_ref):
    total = jnp.zeros((2 * OWN, D), jnp.float32)
    for at in range(0, LOCAL, 2 * OWN):
        total = total + parts_ref[at : at + 2 * OWN, :].astype(jnp.float32)
    summed = total[:OWN] + total[OWN:]
    return (rows_ref[...].astype(jnp.float32) + gate_ref[...] * summed).astype(jnp.bfloat16)


def middle_kernel(parts_ref, rows_ref, gate_ref, shift_ref, scale_ref, updated_ref, normed_ref):
    updated = sum_rows(parts_ref, rows_ref, gate_ref)
    updated_ref[...] = updated
    normed = modulate(updated.astype(jnp.float32), shift_ref[...], scale_ref[...])
    twice = jnp.concatenate([normed, normed], axis=0)
    for at in range(0, LOCAL, 2 * OWN):
        normed_ref[at : at + 2 * OWN, :] = twice


def last_kernel(parts_ref, rows_ref, gate_ref, updated_ref):
    updated_ref[...] = sum_rows(parts_ref, rows_ref, gate_ref)


def across(left, right):
    return lax.dot_general(
        left, right, (((1,), (1,)), ((), ())), preferred_element_type=jnp.float32
    )


def fetch(pieces_ref, sems, wanted):
    copies = [
        pltpu.make_async_copy(
            pieces_ref.at[:, low : low + target.shape[1], :], target, sems.at[number]
        )
        for number, (target, low) in enumerate(wanted)
    ]
    for copy in copies:
        copy.start()
    return copies


def project(rows, *parts):
    weight = jnp.concatenate([part[...].reshape(D, HD) for part in parts], axis=1)
    return jnp.dot(rows, weight, preferred_element_type=jnp.float32)


def low_lanes(rows):
    return lax.broadcasted_iota(jnp.int32, (rows, HD), 1) < HALF


def pick(half, both):
    return jnp.where(half == 0, both[:PT], both[PT:])


def shared_project_kernel(place_ref, rows_ref, pieces_ref, kept_ref, given_ref, w_qk, w_vo, sems):
    copies = fetch(pieces_ref, sems, [(w_qk, AT_SHARED), (w_vo, AT_SHARED_VO)])
    half = place_ref[1]
    rows = rows_ref[...]
    for copy in copies:
        copy.wait()
    both = project(rows, w_qk, w_vo)
    normed = head_norm(both[:, :HD])
    values = jnp.where(low_lanes(LOCAL), both[:, HD:], 0.0).astype(jnp.bfloat16)
    kept_ref[:LOCAL] = normed
    kept_ref[LOCAL:] = pick(half, values)
    given_ref[:LOCAL] = normed
    given_ref[LOCAL:] = pick(1 - half, values)


def own_project_kernel(rows_ref, pieces_ref, own_ref, keys, values, w_q, w_k, w_v, sems):
    copies = fetch(
        pieces_ref,
        sems,
        [
            (w_q, 0),
            (w_k, ROWS),
            (w_v, 2 * ROWS),
            (keys, AT_SHARED_K),
            (values, AT_SHARED_V),
        ],
    )
    rows = rows_ref[...]
    copies[0].wait()
    copies[1].wait()
    both = project(rows, w_q, w_k)
    own_ref[:LOCAL] = head_norm(both[:, :HD])
    own_ref[LOCAL : 2 * LOCAL] = head_norm(both[:, HD:])
    copies[2].wait()
    own_ref[2 * LOCAL :] = project(rows, w_v).astype(jnp.bfloat16)
    copies[3].wait()
    copies[4].wait()


def weigh(queries, keys):
    return jnp.exp(across(queries, keys) * (1.0 / math.sqrt(HD)))


def gather_values(numerator, values):
    return jnp.dot(numerator.astype(jnp.bfloat16), values, preferred_element_type=jnp.float32)


def attend_stale(queries, keys, values, first_column, row_patch, total, gathered):
    patches = keys.shape[1]
    step = 512 // patches
    shape = (queries.shape[0], step * patches)
    column_patch = first_column + lax.broadcasted_iota(jnp.int32, shape, 1) % patches
    stale_here = column_patch != row_patch
    for low in range(0, SOURCES, step):
        some_keys = keys[low : low + step].reshape(step * patches, HD)
        some_values = values[low : low + step].reshape(step * patches, HD)
        numerator = jnp.where(stale_here, weigh(queries, some_keys), 0.0)
        total = total + jnp.sum(numerator, axis=1, keepdims=True)
        gathered = gathered + gather_values(numerator, some_values)
    return total, gathered


def patch_of_rows(place_ref):
    second = lax.broadcasted_iota(jnp.int32, (LOCAL, 1), 0) >= PT
    return place_ref[0] + second.astype(jnp.int32)


def shared_attend_kernel(
    place_ref, kept_ref, got_ref, keys, values, sums_ref, given_ref
):
    half = place_ref[1]
    kept, got = kept_ref[:LOCAL], got_ref[:LOCAL]
    queries = jnp.where(half == 0, kept, got)
    fresh_keys = jnp.where(half == 0, got[:PT], kept[PT:])
    mine, other = kept_ref[LOCAL:].astype(jnp.float32), got_ref[LOCAL:].astype(jnp.float32)
    low = jnp.where(half == 0, mine, other)
    high = jnp.where(half == 0, other, mine)
    fresh_values = jnp.where(low_lanes(PT), low, pltpu.roll(high, HALF, 1)).astype(jnp.bfloat16)
    fresh = weigh(pick(half, queries), fresh_keys)

    def placed(rows):
        nothing = jnp.zeros_like(rows)
        return jnp.concatenate(
            [jnp.where(half == 0, rows, nothing), jnp.where(half == 0, nothing, rows)], axis=0
        )

    total = placed(jnp.sum(fresh, axis=1, keepdims=True))
    gathered = placed(gather_values(fresh, fresh_values))
    total, gathered = attend_stale(
        queries,
        keys,
        values,
        half * (PATCHES // 2),
        patch_of_rows(place_ref),
        total,
        gathered,
    )
    swapped = pltpu.roll(gathered, HALF, 1)
    first = low_lanes(LOCAL)
    sums_ref[...] = jnp.where(first, total, jnp.where(half == 0, swapped, gathered))
    given_ref[...] = jnp.where(first, total, jnp.where(half == 0, gathered, swapped))


def own_attend_kernel(
    place_ref, own_ref, earlier_ref, pieces_ref, attended_ref, w_own, w_vo, keys, values, sems
):
    del earlier_ref
    copies = fetch(
        pieces_ref,
        sems,
        [(keys, AT_K), (values, AT_V), (w_own, AT_OUT), (w_vo, AT_SHARED_VO)],
    )
    queries = own_ref[:LOCAL]
    fresh = weigh(queries, own_ref[LOCAL : 2 * LOCAL])
    row_at = lax.broadcasted_iota(jnp.int32, (LOCAL, 1), 0)
    column_at = lax.broadcasted_iota(jnp.int32, (LOCAL, LOCAL), 1)
    fresh = jnp.where((row_at >= PT) == (column_at >= PT), fresh, 0.0)
    total = jnp.sum(fresh, axis=1, keepdims=True)
    gathered = gather_values(fresh, own_ref[2 * LOCAL :])
    copies[0].wait()
    copies[1].wait()
    total, gathered = attend_stale(
        queries, keys, values, 0, patch_of_rows(place_ref), total, gathered
    )
    attended_ref[...] = (gathered / total).astype(jnp.bfloat16)
    copies[2].wait()
    copies[3].wait()


def finish_kernel(attended_ref, sums_ref, got_ref, w_own, w_vo, partial_ref):
    sums = sums_ref[...] + got_ref[...]
    shared = jnp.where(low_lanes(LOCAL), 0.0, sums / sums[:, :1]).astype(jnp.bfloat16)
    attention = jnp.concatenate([attended_ref[...], shared], axis=1)
    step = 8
    width = step * ROWS
    for low in range(0, SOURCES, step):
        weight = jnp.concatenate(
            [
                w_own[low : low + step].reshape(width, HD),
                w_vo[low : low + step].reshape(width, HD),
            ],
            axis=1,
        )
        partial_ref[:, low * ROWS : low * ROWS + width] = across(attention, weight).astype(
            jnp.bfloat16
        )


def to_own_order(array):
    lead = array.shape[:-1]
    split = array.reshape(lead + (NY, NZ * NC, ROWS))
    return jnp.swapaxes(split, -3, -2).reshape(lead + (D,))


def to_given_order(array):
    lead = array.shape[:-1]
    split = array.reshape(lead + (NZ * NC, NY, ROWS))
    return jnp.swapaxes(split, -3, -2).reshape(lead + (D,))


def exchange(array, axes):
    return lax.all_to_all(array, axes, split_axis=0, concat_axis=0, tiled=True)


def body(latent, modulation, w_qkv, w_out, stale):
    x_at, y_at = lax.axis_index("x"), lax.axis_index("y")
    pair_at = lax.axis_index("z") * NC + lax.axis_index("c")
    place = jnp.stack([2 * pair_at, y_at % 2]).astype(jnp.int32)

    sent = pl.pallas_call(
        pack_kernel,
        out_shape=jax.ShapeDtypeStruct((MEMBERS, PIECE, HD), jnp.bfloat16),
        in_specs=[ANY, ANY, VMEM],
        out_specs=VMEM,
        scratch_shapes=[
            pltpu.VMEM((ROWS, 3 * D), jnp.bfloat16),
            pltpu.VMEM((ROWS, D), jnp.bfloat16),
            pltpu.SemaphoreType.DMA((2,)),
        ],
        compiler_params=PARAMS,
        name="pack",
    )(w_qkv[0], w_out[0].T, jnp.swapaxes(stale[0, :, 0], 0, 1))
    received = exchange(sent, HEAD_AXES).reshape(BLOCKS, NY, PIECE, HD)

    pieces = [
        lax.all_gather(received[block], REST_AXES, axis=0, tiled=True) for block in range(BLOCKS)
    ]

    terms = to_own_order(lax.all_gather(modulation[0], "x", axis=0, tiled=False))
    wanted = latent.reshape(NZ * NC, 2, D)
    wanted = lax.dynamic_index_in_dim(wanted, x_at // 2, 1, keepdims=False)
    mine = exchange(wanted, REST_AXES)
    current = to_own_order(lax.dynamic_slice_in_dim(mine, (x_at % 2) * OWN, OWN, 0))

    def term(block, which):
        return terms[block, which][None]

    spread = jax.ShapeDtypeStruct((LOCAL, D), jnp.bfloat16)
    owned = jax.ShapeDtypeStruct((OWN, D), jnp.bfloat16)
    normed = pl.pallas_call(
        first_kernel,
        out_shape=spread,
        in_specs=[VMEM] * 3,
        out_specs=VMEM,
        compiler_params=PARAMS,
        name="first",
    )(current, term(0, 0), term(0, 1))
    weight = pltpu.VMEM((SOURCES, ROWS, HD), jnp.bfloat16)
    cache = pltpu.VMEM((SOURCES, PATCHES, HD), jnp.bfloat16)
    half_cache = jax.ShapeDtypeStruct((SOURCES, PATCHES // 2, HD), jnp.bfloat16)
    kept_weight = jax.ShapeDtypeStruct((SOURCES, ROWS, HD), jnp.bfloat16)
    sums_of = jax.ShapeDtypeStruct((LOCAL, HD), jnp.float32)

    def rows_of(count):
        return jax.ShapeDtypeStruct((count, HD), jnp.bfloat16)

    def local(kernel, in_specs, out_specs, out_shape, scratch, copies, elements):
        return pl.pallas_call(
            kernel,
            out_shape=out_shape,
            in_specs=in_specs,
            out_specs=out_specs,
            scratch_shapes=scratch + [pltpu.SemaphoreType.DMA((copies,))] * (copies > 0),
            compiler_params=PARAMS if copies else SMALL,
            cost_estimate=pl.CostEstimate(
                flops=2 * LOCAL * elements, bytes_accessed=2 * elements, transcendentals=0
            ),
            name=kernel.__name__,
        )

    def swap(array):
        return lax.ppermute(array, "y", [(at, at ^ 1) for at in range(NY)])

    outputs = []
    for block in range(BLOCKS):
        rows = exchange(normed, HEAD_AXES)
        source = pieces[block]
        kept, given = local(
            shared_project_kernel, (SMEM, VMEM, ANY), (VMEM, VMEM),
            (rows_of(LOCAL + PT), rows_of(LOCAL + PT)), [weight] * 2, 2, 2 * D * HD,
        )(place, rows, source)
        got = swap(given)
        own, keys, values = local(
            own_project_kernel, (VMEM, ANY), (VMEM, VMEM, VMEM),
            (rows_of(3 * LOCAL), half_cache, half_cache), [weight] * 3, 5, 3 * D * HD,
        )(rows, source)
        sums, given = local(
            shared_attend_kernel, (SMEM,) + (VMEM,) * 4, (VMEM, VMEM),
            (sums_of, sums_of), [], 0, PATCHES * PT * HD,
        )(place, kept, got, keys, values)
        got = swap(given)
        attended, w_own, w_vo = local(
            own_attend_kernel, (SMEM, VMEM, VMEM, ANY), (VMEM, VMEM, VMEM),
            (rows_of(LOCAL), kept_weight, kept_weight), [cache] * 2, 4, 2 * PATCHES * PT * HD,
        )(place, own, sums, source)
        partial = local(
            finish_kernel, (VMEM,) * 5, VMEM, spread, [], 0, 2 * D * HD,
        )(attended, sums, got, w_own, w_vo)
        parts = exchange(partial, HEAD_AXES)
        if block + 1 < BLOCKS:
            current, normed = pl.pallas_call(
                middle_kernel,
                out_shape=(owned, spread),
                in_specs=[VMEM] * 5,
                out_specs=(VMEM, VMEM),
                compiler_params=PARAMS,
                name="middle",
            )(parts, current, term(block, 2), term(block + 1, 0), term(block + 1, 1))
        else:
            current = pl.pallas_call(
                last_kernel,
                out_shape=owned,
                in_specs=[VMEM] * 3,
                out_specs=VMEM,
                compiler_params=PARAMS,
                name="last",
            )(parts, current, term(block, 2))
        outputs.append(to_given_order(current))
    outputs = jnp.stack(outputs)
    moved = [lax.dynamic_index_in_dim(outputs, x_at, 0, keepdims=False)]
    for step in range(1, NX):
        leaving = lax.dynamic_index_in_dim(outputs, (x_at + step) % NX, 0, keepdims=False)
        moved.append(lax.ppermute(leaving, "x", [(at, (at + step) % NX) for at in range(NX)]))
    moved = jnp.stack(moved)
    placed = jnp.stack(
        [
            lax.dynamic_index_in_dim(moved, (x_at - origin) % NX, 0, keepdims=False)
            for origin in range(NX)
        ]
    )
    placed = jnp.swapaxes(placed.reshape(2, NZ * NC, D), 0, 1).reshape(PATCHES, D)
    placed = exchange(placed, REST_AXES)
    return placed[None, :, None]


def solution(mesh):
    own_mesh = Mesh(mesh.devices.reshape(NX, NY, NZ, NC), ("x",) + SP)
    return jax.shard_map(
        body,
        mesh=own_mesh,
        in_specs=(
            P(None, SP, None),
            P("x", None, None),
            P("x", SP, None),
            P("x", None, SP),
            P("x", None, SP, None, None),
        ),
        out_specs=P("x", None, SP, None),
        check_vma=False,
    )
```

```python
import math

import jax
import jax.numpy as jnp
from jax import lax
from jax.experimental import pallas as pl
from jax.experimental.pallas import tpu as pltpu
from jax.sharding import Mesh
from jax.sharding import PartitionSpec as P

D = 3072
HEADS = 24
HD = 128
PT = 64
PATCHES = 32
BLOCKS = 4
NX, NY, NZ, NC = 4, 4, 8, 2
SP = ("y", "z", "c")
HEAD_AXES = ("x", "y")
REST_AXES = ("z", "c")
MEMBERS = NX * NY
SOURCES = NY * NZ * NC
ROWS = D // SOURCES
OWN = 8
LOCAL = 2 * PT
AT_OUT, AT_K, AT_V, AT_SHARED = 3 * ROWS, 4 * ROWS, 4 * ROWS + PATCHES, 4 * ROWS + 2 * PATCHES
AT_SHARED_VO = AT_SHARED + ROWS
AT_SHARED_K = AT_SHARED + 2 * ROWS
AT_SHARED_V = AT_SHARED_K + PATCHES // 2
PIECE = AT_SHARED_V + PATCHES // 2
HALF = HD // 2
ANY = pl.BlockSpec(memory_space=pl.ANY)
SMEM = pl.BlockSpec(memory_space=pltpu.SMEM)
VMEM = pl.BlockSpec(memory_space=pltpu.VMEM)
SMALL = pltpu.CompilerParams(vmem_limit_bytes=24 * 1024 * 1024)
PARAMS = pltpu.CompilerParams(vmem_limit_bytes=48 * 1024 * 1024)


def head_norm(values):
    return (
        values * lax.rsqrt(jnp.mean(values * values, axis=-1, keepdims=True) + 1e-06)
    ).astype(jnp.bfloat16)


def modulate(rows, shift_term, scale_term):
    average = jnp.mean(rows, axis=-1, keepdims=True)
    centered = rows - average
    variance = jnp.mean(centered * centered, axis=-1, keepdims=True)
    return (centered * lax.rsqrt(variance + 1e-06) * (1.0 + scale_term) + shift_term).astype(
        jnp.bfloat16
    )


def pack_kernel(qkv_from, out_from, stale_ref, sent_ref, qkv_ref, out_ref, sems):
    copies = [
        pltpu.make_async_copy(qkv_from, qkv_ref, sems.at[0]),
        pltpu.make_async_copy(out_from, out_ref, sems.at[1]),
    ]
    for copy in copies:
        copy.start()

    def columns(head):
        return slice(head * HD, (head + 1) * HD)

    def put(member, low, rows):
        sent_ref[member, low : low + rows.shape[0], :] = rows

    def each():
        for member in range(MEMBERS):
            triple, half = divmod(member, 2)
            yield member, half, 3 * triple + 2 * half, 3 * triple + 1

    for member, half, own, shared in each():
        put(member, AT_K, stale_ref[0, :, columns(own)])
        put(member, AT_V, stale_ref[1, :, columns(own)])
        some = slice(half * PATCHES // 2, (half + 1) * PATCHES // 2)
        put(member, AT_SHARED_K, stale_ref[0, some, columns(shared)])
        put(member, AT_SHARED_V, stale_ref[1, some, columns(shared)])
    copies[1].wait()
    for member, half, own, shared in each():
        put(member, AT_OUT, out_ref[:, columns(own)])
    copies[0].wait()
    for member, half, own, shared in each():
        for part in range(3):
            put(member, part * ROWS, qkv_ref[:, columns(part * HEADS + own)])
        put(member, AT_SHARED, qkv_ref[:, columns(half * HEADS + shared)])
        w_v = qkv_ref[:, columns(2 * HEADS + shared)]
        w_o = out_ref[:, columns(shared)]
        lanes = slice(half * HALF, (half + 1) * HALF)
        put(member, AT_SHARED_VO, jnp.concatenate([w_v[:, lanes], w_o[:, lanes]], axis=1))


def first_kernel(rows_ref, shift_ref, scale_ref, normed_ref):
    normed = modulate(rows_ref[...].astype(jnp.float32), shift_ref[...], scale_ref[...])
    twice = jnp.concatenate([normed, normed], axis=0)
    for at in range(0, LOCAL, 2 * OWN):
        normed_ref[at : at + 2 * OWN, :] = twice


def sum_rows(parts_ref, rows_ref, gate_ref):
    total = jnp.zeros((2 * OWN, D), jnp.float32)
    for at in range(0, LOCAL, 2 * OWN):
        total = total + parts_ref[at : at + 2 * OWN, :].astype(jnp.float32)
    summed = total[:OWN] + total[OWN:]
    return (rows_ref[...].astype(jnp.float32) + gate_ref[...] * summed).astype(jnp.bfloat16)


def middle_kernel(parts_ref, rows_ref, gate_ref, shift_ref, scale_ref, updated_ref, normed_ref):
    updated = sum_rows(parts_ref, rows_ref, gate_ref)
    updated_ref[...] = updated
    normed = modulate(updated.astype(jnp.float32), shift_ref[...], scale_ref[...])
    twice = jnp.concatenate([normed, normed], axis=0)
    for at in range(0, LOCAL, 2 * OWN):
        normed_ref[at : at + 2 * OWN, :] = twice


def last_kernel(parts_ref, rows_ref, gate_ref, updated_ref):
    updated_ref[...] = sum_rows(parts_ref, rows_ref, gate_ref)


def across(left, right):
    return lax.dot_general(
        left, right, (((1,), (1,)), ((), ())), preferred_element_type=jnp.float32
    )


def fetch(pieces_ref, sems, wanted):
    copies = [
        pltpu.make_async_copy(
            pieces_ref.at[:, low : low + target.shape[1], :], target, sems.at[number]
        )
        for number, (target, low) in enumerate(wanted)
    ]
    for copy in copies:
        copy.start()
    return copies


def project(rows, *parts):
    weight = jnp.concatenate([part[...].reshape(D, HD) for part in parts], axis=1)
    return jnp.dot(rows, weight, preferred_element_type=jnp.float32)


def low_lanes(rows):
    return lax.broadcasted_iota(jnp.int32, (rows, HD), 1) < HALF


def pick(half, both):
    return jnp.where(half == 0, both[:PT], both[PT:])


def shared_project_kernel(place_ref, rows_ref, pieces_ref, kept_ref, given_ref, w_qk, w_vo, sems):
    parts = 2
    count = SOURCES // parts
    copies = []
    for low in range(0, SOURCES, count):
        for target, at in ((w_qk, AT_SHARED), (w_vo, AT_SHARED_VO)):
            copies.append(
                pltpu.make_async_copy(
                    pieces_ref.at[low : low + count, at : at + ROWS, :],
                    target.at[low : low + count],
                    sems.at[len(copies)],
                )
            )
    for copy in copies:
        copy.start()
    half = place_ref[1]
    both = jnp.zeros((LOCAL, 2 * HD), jnp.float32)
    for part in range(parts):
        copies[2 * part].wait()
        copies[2 * part + 1].wait()
        low, width = part * count, count * ROWS
        some = [w[low : low + count].reshape(width, HD) for w in (w_qk, w_vo)]
        both = both + jnp.dot(
            rows_ref[:, part * width : (part + 1) * width],
            jnp.concatenate(some, axis=1),
            preferred_element_type=jnp.float32,
        )
    normed = head_norm(both[:, :HD])
    values = jnp.where(low_lanes(LOCAL), both[:, HD:], 0.0).astype(jnp.bfloat16)
    kept_ref[:LOCAL] = normed
    kept_ref[LOCAL:] = pick(half, values)
    given_ref[:LOCAL] = normed
    given_ref[LOCAL:] = pick(1 - half, values)


def own_project_kernel(rows_ref, pieces_ref, own_ref, keys, values, w_q, w_k, w_v, sems):
    copies = fetch(
        pieces_ref,
        sems,
        [
            (w_q, 0),
            (w_k, ROWS),
            (w_v, 2 * ROWS),
            (keys, AT_SHARED_K),
            (values, AT_SHARED_V),
        ],
    )
    rows = rows_ref[...]
    copies[0].wait()
    copies[1].wait()
    both = project(rows, w_q, w_k)
    own_ref[:LOCAL] = head_norm(both[:, :HD])
    own_ref[LOCAL : 2 * LOCAL] = head_norm(both[:, HD:])
    copies[2].wait()
    own_ref[2 * LOCAL :] = project(rows, w_v).astype(jnp.bfloat16)
    copies[3].wait()
    copies[4].wait()


def weigh(queries, keys):
    return jnp.exp(across(queries, keys) * (1.0 / math.sqrt(HD)))


def gather_values(numerator, values):
    return jnp.dot(numerator.astype(jnp.bfloat16), values, preferred_element_type=jnp.float32)


def attend_stale(queries, keys, values, first_column, row_patch, total, gathered):
    patches = keys.shape[1]
    step = 512 // patches
    shape = (queries.shape[0], step * patches)
    column_patch = first_column + lax.broadcasted_iota(jnp.int32, shape, 1) % patches
    stale_here = column_patch != row_patch
    for low in range(0, SOURCES, step):
        some_keys = keys[low : low + step].reshape(step * patches, HD)
        some_values = values[low : low + step].reshape(step * patches, HD)
        numerator = jnp.where(stale_here, weigh(queries, some_keys), 0.0)
        total = total + jnp.sum(numerator, axis=1, keepdims=True)
        gathered = gathered + gather_values(numerator, some_values)
    return total, gathered


def patch_of_rows(place_ref):
    second = lax.broadcasted_iota(jnp.int32, (LOCAL, 1), 0) >= PT
    return place_ref[0] + second.astype(jnp.int32)


def shared_attend_kernel(
    place_ref, kept_ref, got_ref, keys, values, sums_ref, given_ref
):
    half = place_ref[1]
    kept, got = kept_ref[:LOCAL], got_ref[:LOCAL]
    queries = jnp.where(half == 0, kept, got)
    fresh_keys = jnp.where(half == 0, got[:PT], kept[PT:])
    mine, other = kept_ref[LOCAL:].astype(jnp.float32), got_ref[LOCAL:].astype(jnp.float32)
    low = jnp.where(half == 0, mine, other)
    high = jnp.where(half == 0, other, mine)
    fresh_values = jnp.where(low_lanes(PT), low, pltpu.roll(high, HALF, 1)).astype(jnp.bfloat16)
    fresh = weigh(pick(half, queries), fresh_keys)

    def placed(rows):
        nothing = jnp.zeros_like(rows)
        return jnp.concatenate(
            [jnp.where(half == 0, rows, nothing), jnp.where(half == 0, nothing, rows)], axis=0
        )

    total = placed(jnp.sum(fresh, axis=1, keepdims=True))
    gathered = placed(gather_values(fresh, fresh_values))
    total, gathered = attend_stale(
        queries,
        keys,
        values,
        half * (PATCHES // 2),
        patch_of_rows(place_ref),
        total,
        gathered,
    )
    swapped = pltpu.roll(gathered, HALF, 1)
    first = low_lanes(LOCAL)
    sums_ref[...] = jnp.where(first, total, jnp.where(half == 0, swapped, gathered))
    leading = total.astype(jnp.bfloat16).astype(jnp.float32)
    lane = lax.broadcasted_iota(jnp.int32, (LOCAL, HD), 1)
    sent = jnp.where(half == 0, gathered, swapped)
    sent = jnp.where(first, jnp.where(lane == 0, leading, total - leading), sent)
    given_ref[...] = sent.astype(jnp.bfloat16)


def own_attend_kernel(
    place_ref, own_ref, earlier_ref, pieces_ref, attended_ref, w_own, w_vo, keys, values, sems
):
    del earlier_ref
    copies = fetch(
        pieces_ref,
        sems,
        [(keys, AT_K), (values, AT_V), (w_own, AT_OUT), (w_vo, AT_SHARED_VO)],
    )
    queries = own_ref[:LOCAL]
    fresh = weigh(queries, own_ref[LOCAL : 2 * LOCAL])
    row_at = lax.broadcasted_iota(jnp.int32, (LOCAL, 1), 0)
    column_at = lax.broadcasted_iota(jnp.int32, (LOCAL, LOCAL), 1)
    fresh = jnp.where((row_at >= PT) == (column_at >= PT), fresh, 0.0)
    total = jnp.sum(fresh, axis=1, keepdims=True)
    gathered = gather_values(fresh, own_ref[2 * LOCAL :])
    copies[0].wait()
    copies[1].wait()
    total, gathered = attend_stale(
        queries, keys, values, 0, patch_of_rows(place_ref), total, gathered
    )
    attended_ref[...] = (gathered / total).astype(jnp.bfloat16)
    copies[2].wait()
    copies[3].wait()


def finish_kernel(attended_ref, sums_ref, got_ref, w_own, w_vo, partial_ref):
    sums, got = sums_ref[...], got_ref[...].astype(jnp.float32)
    total = sums[:, :1] + got[:, :1] + got[:, 1:2]
    shared = jnp.where(low_lanes(LOCAL), 0.0, (sums + got) / total).astype(jnp.bfloat16)
    attention = jnp.concatenate([attended_ref[...], shared], axis=1)
    step = 8
    width = step * ROWS
    for low in range(0, SOURCES, step):
        weight = jnp.concatenate(
            [
                w_own[low : low + step].reshape(width, HD),
                w_vo[low : low + step].reshape(width, HD),
            ],
            axis=1,
        )
        partial_ref[:, low * ROWS : low * ROWS + width] = across(attention, weight).astype(
            jnp.bfloat16
        )


def to_own_order(array):
    lead = array.shape[:-1]
    split = array.reshape(lead + (NY, NZ * NC, ROWS))
    return jnp.swapaxes(split, -3, -2).reshape(lead + (D,))


def to_given_order(array):
    lead = array.shape[:-1]
    split = array.reshape(lead + (NZ * NC, NY, ROWS))
    return jnp.swapaxes(split, -3, -2).reshape(lead + (D,))


def exchange(array, axes):
    return lax.all_to_all(array, axes, split_axis=0, concat_axis=0, tiled=True)


def body(latent, modulation, w_qkv, w_out, stale):
    x_at, y_at = lax.axis_index("x"), lax.axis_index("y")
    pair_at = lax.axis_index("z") * NC + lax.axis_index("c")
    place = jnp.stack([2 * pair_at, y_at % 2]).astype(jnp.int32)

    sent = pl.pallas_call(
        pack_kernel,
        out_shape=jax.ShapeDtypeStruct((MEMBERS, PIECE, HD), jnp.bfloat16),
        in_specs=[ANY, ANY, VMEM],
        out_specs=VMEM,
        scratch_shapes=[
            pltpu.VMEM((ROWS, 3 * D), jnp.bfloat16),
            pltpu.VMEM((ROWS, D), jnp.bfloat16),
            pltpu.SemaphoreType.DMA((2,)),
        ],
        compiler_params=PARAMS,
        name="pack",
    )(w_qkv[0], w_out[0].T, jnp.swapaxes(stale[0, :, 0], 0, 1))
    received = exchange(sent, HEAD_AXES).reshape(BLOCKS, NY, PIECE, HD)

    pieces = [
        lax.all_gather(received[block], REST_AXES, axis=0, tiled=True) for block in range(BLOCKS)
    ]

    terms = to_own_order(lax.all_gather(modulation[0], "x", axis=0, tiled=False))
    wanted = latent.reshape(NZ * NC, 2, D)
    wanted = lax.dynamic_index_in_dim(wanted, x_at // 2, 1, keepdims=False)
    mine = exchange(wanted, REST_AXES)
    current = to_own_order(lax.dynamic_slice_in_dim(mine, (x_at % 2) * OWN, OWN, 0))

    def term(block, which):
        return terms[block, which][None]

    spread = jax.ShapeDtypeStruct((LOCAL, D), jnp.bfloat16)
    owned = jax.ShapeDtypeStruct((OWN, D), jnp.bfloat16)
    normed = pl.pallas_call(
        first_kernel,
        out_shape=spread,
        in_specs=[VMEM] * 3,
        out_specs=VMEM,
        compiler_params=PARAMS,
        name="first",
    )(current, term(0, 0), term(0, 1))
    weight = pltpu.VMEM((SOURCES, ROWS, HD), jnp.bfloat16)
    cache = pltpu.VMEM((SOURCES, PATCHES, HD), jnp.bfloat16)
    half_cache = jax.ShapeDtypeStruct((SOURCES, PATCHES // 2, HD), jnp.bfloat16)
    kept_weight = jax.ShapeDtypeStruct((SOURCES, ROWS, HD), jnp.bfloat16)
    sums_of = jax.ShapeDtypeStruct((LOCAL, HD), jnp.float32)

    def rows_of(count):
        return jax.ShapeDtypeStruct((count, HD), jnp.bfloat16)

    def local(kernel, in_specs, out_specs, out_shape, scratch, copies, elements):
        return pl.pallas_call(
            kernel,
            out_shape=out_shape,
            in_specs=in_specs,
            out_specs=out_specs,
            scratch_shapes=scratch + [pltpu.SemaphoreType.DMA((copies,))] * (copies > 0),
            compiler_params=PARAMS if copies else SMALL,
            cost_estimate=pl.CostEstimate(
                flops=2 * LOCAL * elements, bytes_accessed=2 * elements, transcendentals=0
            ),
            name=kernel.__name__,
        )

    def swap(array):
        return lax.ppermute(array, "y", [(at, at ^ 1) for at in range(NY)])

    outputs = []
    for block in range(BLOCKS):
        rows = exchange(normed, HEAD_AXES)
        source = pieces[block]
        kept, given = local(
            shared_project_kernel, (SMEM, VMEM, ANY), (VMEM, VMEM),
            (rows_of(LOCAL + PT), rows_of(LOCAL + PT)), [weight] * 2, 4, 2 * D * HD,
        )(place, rows, source)
        got = swap(given)
        own, keys, values = local(
            own_project_kernel, (VMEM, ANY), (VMEM, VMEM, VMEM),
            (rows_of(3 * LOCAL), half_cache, half_cache), [weight] * 3, 5, 3 * D * HD,
        )(rows, source)
        sums, given = local(
            shared_attend_kernel, (SMEM,) + (VMEM,) * 4, (VMEM, VMEM),
            (sums_of, rows_of(LOCAL)), [], 0, PATCHES * PT * HD,
        )(place, kept, got, keys, values)
        got = swap(given)
        attended, w_own, w_vo = local(
            own_attend_kernel, (SMEM, VMEM, VMEM, ANY), (VMEM, VMEM, VMEM),
            (rows_of(LOCAL), kept_weight, kept_weight), [cache] * 2, 4, 2 * PATCHES * PT * HD,
        )(place, own, sums, source)
        partial = local(
            finish_kernel, (VMEM,) * 5, VMEM, spread, [], 0, 2 * D * HD,
        )(attended, sums, got, w_own, w_vo)
        parts = exchange(partial, HEAD_AXES)
        if block + 1 < BLOCKS:
            current, normed = pl.pallas_call(
                middle_kernel,
                out_shape=(owned, spread),
                in_specs=[VMEM] * 5,
                out_specs=(VMEM, VMEM),
                compiler_params=PARAMS,
                name="middle",
            )(parts, current, term(block, 2), term(block + 1, 0), term(block + 1, 1))
        else:
            current = pl.pallas_call(
                last_kernel,
                out_shape=owned,
                in_specs=[VMEM] * 3,
                out_specs=VMEM,
                compiler_params=PARAMS,
                name="last",
            )(parts, current, term(block, 2))
        outputs.append(to_given_order(current))
    outputs = jnp.stack(outputs)
    moved = [lax.dynamic_index_in_dim(outputs, x_at, 0, keepdims=False)]
    for step in range(1, NX):
        leaving = lax.dynamic_index_in_dim(outputs, (x_at + step) % NX, 0, keepdims=False)
        moved.append(lax.ppermute(leaving, "x", [(at, (at + step) % NX) for at in range(NX)]))
    moved = jnp.stack(moved)
    placed = jnp.stack(
        [
            lax.dynamic_index_in_dim(moved, (x_at - origin) % NX, 0, keepdims=False)
            for origin in range(NX)
        ]
    )
    placed = jnp.swapaxes(placed.reshape(2, NZ * NC, D), 0, 1).reshape(PATCHES, D)
    placed = exchange(placed, REST_AXES)
    return placed[None, :, None]


def solution(mesh):
    own_mesh = Mesh(mesh.devices.reshape(NX, NY, NZ, NC), ("x",) + SP)
    return jax.shard_map(
        body,
        mesh=own_mesh,
        in_specs=(
            P(None, SP, None),
            P("x", None, None),
            P("x", SP, None),
            P("x", None, SP),
            P("x", None, SP, None, None),
        ),
        out_specs=P("x", None, SP, None),
        check_vma=False,
    )
```

```python
import math

import jax
import jax.numpy as jnp
from jax import lax
from jax.experimental import pallas as pl
from jax.experimental.pallas import tpu as pltpu
from jax.sharding import Mesh
from jax.sharding import PartitionSpec as P

D = 3072
HEADS = 24
HD = 128
PT = 64
PATCHES = 32
BLOCKS = 4
NX, NY, NZ, NC = 4, 4, 8, 2
SP = ("y", "z", "c")
HEAD_AXES = ("x", "y")
REST_AXES = ("z", "c")
MEMBERS = NX * NY
SOURCES = NY * NZ * NC
ROWS = D // SOURCES
OWN = 8
LOCAL = 2 * PT
AT_OUT, AT_K, AT_V, AT_SHARED = 3 * ROWS, 4 * ROWS, 4 * ROWS + PATCHES, 4 * ROWS + 2 * PATCHES
AT_SHARED_VO = AT_SHARED + ROWS
AT_SHARED_K = AT_SHARED + 2 * ROWS
AT_SHARED_V = AT_SHARED_K + PATCHES // 2
PIECE = AT_SHARED_V + PATCHES // 2
HALF = HD // 2
ANY = pl.BlockSpec(memory_space=pl.ANY)
SMEM = pl.BlockSpec(memory_space=pltpu.SMEM)
VMEM = pl.BlockSpec(memory_space=pltpu.VMEM)
SMALL = pltpu.CompilerParams(vmem_limit_bytes=24 * 1024 * 1024)
PARAMS = pltpu.CompilerParams(vmem_limit_bytes=48 * 1024 * 1024)


def head_norm(values):
    return (
        values * lax.rsqrt(jnp.mean(values * values, axis=-1, keepdims=True) + 1e-06)
    ).astype(jnp.bfloat16)


def modulate(rows, shift_term, scale_term):
    average = jnp.mean(rows, axis=-1, keepdims=True)
    centered = rows - average
    variance = jnp.mean(centered * centered, axis=-1, keepdims=True)
    return (centered * lax.rsqrt(variance + 1e-06) * (1.0 + scale_term) + shift_term).astype(
        jnp.bfloat16
    )


def pack_kernel(qkv_from, out_from, stale_ref, sent_ref, qkv_ref, out_ref, sems):
    copies = [
        pltpu.make_async_copy(qkv_from, qkv_ref, sems.at[0]),
        pltpu.make_async_copy(out_from, out_ref, sems.at[1]),
    ]
    for copy in copies:
        copy.start()

    def columns(head):
        return slice(head * HD, (head + 1) * HD)

    def put(member, low, rows):
        sent_ref[member, low : low + rows.shape[0], :] = rows

    def each():
        for member in range(MEMBERS):
            triple, half = divmod(member, 2)
            yield member, half, 3 * triple + 2 * half, 3 * triple + 1

    for member, half, own, shared in each():
        put(member, AT_K, stale_ref[0, :, columns(own)])
        put(member, AT_V, stale_ref[1, :, columns(own)])
        some = slice(half * PATCHES // 2, (half + 1) * PATCHES // 2)
        put(member, AT_SHARED_K, stale_ref[0, some, columns(shared)])
        put(member, AT_SHARED_V, stale_ref[1, some, columns(shared)])
    copies[1].wait()
    for member, half, own, shared in each():
        put(member, AT_OUT, out_ref[:, columns(own)])
    copies[0].wait()
    for member, half, own, shared in each():
        for part in range(3):
            put(member, part * ROWS, qkv_ref[:, columns(part * HEADS + own)])
        put(member, AT_SHARED, qkv_ref[:, columns(half * HEADS + shared)])
        w_v = qkv_ref[:, columns(2 * HEADS + shared)]
        w_o = out_ref[:, columns(shared)]
        lanes = slice(half * HALF, (half + 1) * HALF)
        put(member, AT_SHARED_VO, jnp.concatenate([w_v[:, lanes], w_o[:, lanes]], axis=1))


def first_kernel(rows_ref, shift_ref, scale_ref, normed_ref):
    normed = modulate(rows_ref[...].astype(jnp.float32), shift_ref[...], scale_ref[...])
    twice = jnp.concatenate([normed, normed], axis=0)
    for at in range(0, LOCAL, 2 * OWN):
        normed_ref[at : at + 2 * OWN, :] = twice


def sum_rows(parts_ref, rows_ref, gate_ref):
    total = jnp.zeros((2 * OWN, D), jnp.float32)
    for at in range(0, LOCAL, 2 * OWN):
        total = total + parts_ref[at : at + 2 * OWN, :].astype(jnp.float32)
    summed = total[:OWN] + total[OWN:]
    return (rows_ref[...].astype(jnp.float32) + gate_ref[...] * summed).astype(jnp.bfloat16)


def middle_kernel(parts_ref, rows_ref, gate_ref, shift_ref, scale_ref, updated_ref, normed_ref):
    updated = sum_rows(parts_ref, rows_ref, gate_ref)
    updated_ref[...] = updated
    normed = modulate(updated.astype(jnp.float32), shift_ref[...], scale_ref[...])
    twice = jnp.concatenate([normed, normed], axis=0)
    for at in range(0, LOCAL, 2 * OWN):
        normed_ref[at : at + 2 * OWN, :] = twice


def last_kernel(parts_ref, rows_ref, gate_ref, updated_ref):
    updated_ref[...] = sum_rows(parts_ref, rows_ref, gate_ref)


def across(left, right):
    return lax.dot_general(
        left, right, (((1,), (1,)), ((), ())), preferred_element_type=jnp.float32
    )


def fetch(pieces_ref, sems, wanted):
    copies = [
        pltpu.make_async_copy(
            pieces_ref.at[:, low : low + target.shape[1], :], target, sems.at[number]
        )
        for number, (target, low) in enumerate(wanted)
    ]
    for copy in copies:
        copy.start()
    return copies


def project(rows, *parts):
    weight = jnp.concatenate([part[...].reshape(D, HD) for part in parts], axis=1)
    return jnp.dot(rows, weight, preferred_element_type=jnp.float32)


def low_lanes(rows):
    return lax.broadcasted_iota(jnp.int32, (rows, HD), 1) < HALF


def pick(half, both):
    return jnp.where(half == 0, both[:PT], both[PT:])


def shared_project_kernel(place_ref, rows_ref, pieces_ref, kept_ref, given_ref, w_qk, w_vo, sems):
    copies = fetch(pieces_ref, sems, [(w_qk, AT_SHARED), (w_vo, AT_SHARED_VO)])
    half = place_ref[1]
    rows = rows_ref[...]
    for copy in copies:
        copy.wait()
    both = project(rows, w_qk, w_vo)
    normed = head_norm(both[:, :HD])
    values = jnp.where(low_lanes(LOCAL), both[:, HD:], 0.0).astype(jnp.bfloat16)
    kept_ref[:LOCAL] = normed
    kept_ref[LOCAL:] = pick(half, values)
    given_ref[:LOCAL] = normed
    given_ref[LOCAL:] = pick(1 - half, values)


def own_project_kernel(rows_ref, pieces_ref, own_ref, keys, values, w_q, w_k, w_v, sems):
    copies = fetch(
        pieces_ref,
        sems,
        [
            (w_q, 0),
            (w_k, ROWS),
            (w_v, 2 * ROWS),
            (keys, AT_SHARED_K),
            (values, AT_SHARED_V),
        ],
    )
    rows = rows_ref[...]
    copies[0].wait()
    copies[1].wait()
    both = project(rows, w_q, w_k)
    own_ref[:LOCAL] = head_norm(both[:, :HD])
    own_ref[LOCAL : 2 * LOCAL] = head_norm(both[:, HD:])
    copies[2].wait()
    own_ref[2 * LOCAL :] = project(rows, w_v).astype(jnp.bfloat16)
    copies[3].wait()
    copies[4].wait()


def weigh(queries, keys):
    return jnp.exp(across(queries, keys) * (1.0 / math.sqrt(HD)))


def gather_values(numerator, values):
    return jnp.dot(numerator.astype(jnp.bfloat16), values, preferred_element_type=jnp.float32)


def attend_stale(queries, keys, values, first_column, row_patch, total, gathered):
    patches = keys.shape[1]
    step = 512 // patches
    shape = (queries.shape[0], step * patches)
    column_patch = first_column + lax.broadcasted_iota(jnp.int32, shape, 1) % patches
    stale_here = column_patch != row_patch
    for low in range(0, SOURCES, step):
        some_keys = keys[low : low + step].reshape(step * patches, HD)
        some_values = values[low : low + step].reshape(step * patches, HD)
        numerator = jnp.where(stale_here, weigh(queries, some_keys), 0.0)
        total = total + jnp.sum(numerator, axis=1, keepdims=True)
        gathered = gathered + gather_values(numerator, some_values)
    return total, gathered


def patch_of_rows(place_ref):
    second = lax.broadcasted_iota(jnp.int32, (LOCAL, 1), 0) >= PT
    return place_ref[0] + second.astype(jnp.int32)


def shared_attend_kernel(
    place_ref, kept_ref, got_ref, keys, values, sums_ref, given_ref
):
    half = place_ref[1]
    kept, got = kept_ref[:LOCAL], got_ref[:LOCAL]
    queries = jnp.where(half == 0, kept, got)
    fresh_keys = jnp.where(half == 0, got[:PT], kept[PT:])
    mine, other = kept_ref[LOCAL:].astype(jnp.float32), got_ref[LOCAL:].astype(jnp.float32)
    low = jnp.where(half == 0, mine, other)
    high = jnp.where(half == 0, other, mine)
    fresh_values = jnp.where(low_lanes(PT), low, pltpu.roll(high, HALF, 1)).astype(jnp.bfloat16)
    fresh = weigh(pick(half, queries), fresh_keys)

    def placed(rows):
        nothing = jnp.zeros_like(rows)
        return jnp.concatenate(
            [jnp.where(half == 0, rows, nothing), jnp.where(half == 0, nothing, rows)], axis=0
        )

    total = placed(jnp.sum(fresh, axis=1, keepdims=True))
    gathered = placed(gather_values(fresh, fresh_values))
    total, gathered = attend_stale(
        queries,
        keys,
        values,
        half * (PATCHES // 2),
        patch_of_rows(place_ref),
        total,
        gathered,
    )
    swapped = pltpu.roll(gathered, HALF, 1)
    first = low_lanes(LOCAL)
    sums_ref[...] = jnp.where(first, total, jnp.where(half == 0, swapped, gathered))
    given_ref[...] = jnp.where(first, total, jnp.where(half == 0, gathered, swapped))


def own_attend_kernel(
    place_ref, own_ref, earlier_ref, pieces_ref, attended_ref, w_own, w_vo, keys, values, sems
):
    del earlier_ref
    copies = fetch(
        pieces_ref,
        sems,
        [(keys, AT_K), (values, AT_V), (w_own, AT_OUT), (w_vo, AT_SHARED_VO)],
    )
    queries = own_ref[:LOCAL]
    fresh = weigh(queries, own_ref[LOCAL : 2 * LOCAL])
    row_at = lax.broadcasted_iota(jnp.int32, (LOCAL, 1), 0)
    column_at = lax.broadcasted_iota(jnp.int32, (LOCAL, LOCAL), 1)
    fresh = jnp.where((row_at >= PT) == (column_at >= PT), fresh, 0.0)
    total = jnp.sum(fresh, axis=1, keepdims=True)
    gathered = gather_values(fresh, own_ref[2 * LOCAL :])
    copies[0].wait()
    copies[1].wait()
    total, gathered = attend_stale(
        queries, keys, values, 0, patch_of_rows(place_ref), total, gathered
    )
    attended_ref[...] = (gathered / total).astype(jnp.bfloat16)
    copies[2].wait()
    copies[3].wait()


def finish_kernel(attended_ref, sums_ref, got_ref, w_own, w_vo, partial_ref):
    sums = sums_ref[...] + got_ref[...]
    shared = jnp.where(low_lanes(LOCAL), 0.0, sums / sums[:, :1]).astype(jnp.bfloat16)
    attention = jnp.concatenate([attended_ref[...], shared], axis=1)
    step = 8
    width = step * ROWS
    for low in range(0, SOURCES, step):
        weight = jnp.concatenate(
            [
                w_own[low : low + step].reshape(width, HD),
                w_vo[low : low + step].reshape(width, HD),
            ],
            axis=1,
        )
        partial_ref[:, low * ROWS : low * ROWS + width] = across(attention, weight).astype(
            jnp.bfloat16
        )


def to_own_order(array):
    lead = array.shape[:-1]
    split = array.reshape(lead + (NY, NZ * NC, ROWS))
    return jnp.swapaxes(split, -3, -2).reshape(lead + (D,))


def to_given_order(array):
    lead = array.shape[:-1]
    split = array.reshape(lead + (NZ * NC, NY, ROWS))
    return jnp.swapaxes(split, -3, -2).reshape(lead + (D,))


def exchange(array, axes):
    return lax.all_to_all(array, axes, split_axis=0, concat_axis=0, tiled=True)


def body(latent, modulation, w_qkv, w_out, stale):
    x_at, y_at = lax.axis_index("x"), lax.axis_index("y")
    pair_at = lax.axis_index("z") * NC + lax.axis_index("c")
    place = jnp.stack([2 * pair_at, y_at % 2]).astype(jnp.int32)

    sent = pl.pallas_call(
        pack_kernel,
        out_shape=jax.ShapeDtypeStruct((MEMBERS, PIECE, HD), jnp.bfloat16),
        in_specs=[ANY, ANY, VMEM],
        out_specs=VMEM,
        scratch_shapes=[
            pltpu.VMEM((ROWS, 3 * D), jnp.bfloat16),
            pltpu.VMEM((ROWS, D), jnp.bfloat16),
            pltpu.SemaphoreType.DMA((2,)),
        ],
        compiler_params=PARAMS,
        name="pack",
    )(w_qkv[0], w_out[0].T, jnp.swapaxes(stale[0, :, 0], 0, 1))
    received = exchange(sent, HEAD_AXES).reshape(BLOCKS, NY, PIECE, HD)

    pieces = [
        lax.all_gather(received[block], REST_AXES, axis=0, tiled=True) for block in range(BLOCKS)
    ]

    terms = to_own_order(lax.all_gather(modulation[0], "x", axis=0, tiled=False))
    wanted = latent.reshape(NZ, NC, 2, D)
    wanted = lax.dynamic_index_in_dim(wanted, x_at // 2, 2, keepdims=False)
    core_at = lax.axis_index("c")
    same = lax.dynamic_index_in_dim(wanted, core_at, 1, keepdims=False)
    other = lax.dynamic_index_in_dim(wanted, 1 - core_at, 1, keepdims=False)
    other = lax.ppermute(other, "c", [(0, 1), (1, 0)])
    mine = exchange(jnp.where(core_at == x_at % 2, same, other), "z")
    current = to_own_order(mine)

    def term(block, which):
        return terms[block, which][None]

    spread = jax.ShapeDtypeStruct((LOCAL, D), jnp.bfloat16)
    owned = jax.ShapeDtypeStruct((OWN, D), jnp.bfloat16)
    normed = pl.pallas_call(
        first_kernel,
        out_shape=spread,
        in_specs=[VMEM] * 3,
        out_specs=VMEM,
        compiler_params=PARAMS,
        name="first",
    )(current, term(0, 0), term(0, 1))
    weight = pltpu.VMEM((SOURCES, ROWS, HD), jnp.bfloat16)
    cache = pltpu.VMEM((SOURCES, PATCHES, HD), jnp.bfloat16)
    half_cache = jax.ShapeDtypeStruct((SOURCES, PATCHES // 2, HD), jnp.bfloat16)
    kept_weight = jax.ShapeDtypeStruct((SOURCES, ROWS, HD), jnp.bfloat16)
    sums_of = jax.ShapeDtypeStruct((LOCAL, HD), jnp.float32)

    def rows_of(count):
        return jax.ShapeDtypeStruct((count, HD), jnp.bfloat16)

    def local(kernel, in_specs, out_specs, out_shape, scratch, copies, elements):
        return pl.pallas_call(
            kernel,
            out_shape=out_shape,
            in_specs=in_specs,
            out_specs=out_specs,
            scratch_shapes=scratch + [pltpu.SemaphoreType.DMA((copies,))] * (copies > 0),
            compiler_params=PARAMS if copies else SMALL,
            cost_estimate=pl.CostEstimate(
                flops=2 * LOCAL * elements, bytes_accessed=2 * elements, transcendentals=0
            ),
            name=kernel.__name__,
        )

    def swap(array):
        return lax.ppermute(array, "y", [(at, at ^ 1) for at in range(NY)])

    outputs = []
    for block in range(BLOCKS):
        rows = exchange(normed, HEAD_AXES)
        source = pieces[block]
        kept, given = local(
            shared_project_kernel, (SMEM, VMEM, ANY), (VMEM, VMEM),
            (rows_of(LOCAL + PT), rows_of(LOCAL + PT)), [weight] * 2, 2, 2 * D * HD,
        )(place, rows, source)
        got = swap(given)
        own, keys, values = local(
            own_project_kernel, (VMEM, ANY), (VMEM, VMEM, VMEM),
            (rows_of(3 * LOCAL), half_cache, half_cache), [weight] * 3, 5, 3 * D * HD,
        )(rows, source)
        sums, given = local(
            shared_attend_kernel, (SMEM,) + (VMEM,) * 4, (VMEM, VMEM),
            (sums_of, sums_of), [], 0, PATCHES * PT * HD,
        )(place, kept, got, keys, values)
        got = swap(given)
        attended, w_own, w_vo = local(
            own_attend_kernel, (SMEM, VMEM, VMEM, ANY), (VMEM, VMEM, VMEM),
            (rows_of(LOCAL), kept_weight, kept_weight), [cache] * 2, 4, 2 * PATCHES * PT * HD,
        )(place, own, sums, source)
        partial = local(
            finish_kernel, (VMEM,) * 5, VMEM, spread, [], 0, 2 * D * HD,
        )(attended, sums, got, w_own, w_vo)
        parts = exchange(partial, HEAD_AXES)
        if block + 1 < BLOCKS:
            current, normed = pl.pallas_call(
                middle_kernel,
                out_shape=(owned, spread),
                in_specs=[VMEM] * 5,
                out_specs=(VMEM, VMEM),
                compiler_params=PARAMS,
                name="middle",
            )(parts, current, term(block, 2), term(block + 1, 0), term(block + 1, 1))
        else:
            current = pl.pallas_call(
                last_kernel,
                out_shape=owned,
                in_specs=[VMEM] * 3,
                out_specs=VMEM,
                compiler_params=PARAMS,
                name="last",
            )(parts, current, term(block, 2))
        outputs.append(to_given_order(current))
    outputs = jnp.stack(outputs)
    moved = [lax.dynamic_index_in_dim(outputs, x_at, 0, keepdims=False)]
    for step in range(1, NX):
        leaving = lax.dynamic_index_in_dim(outputs, (x_at + step) % NX, 0, keepdims=False)
        moved.append(lax.ppermute(leaving, "x", [(at, (at + step) % NX) for at in range(NX)]))
    moved = jnp.stack(moved)
    placed = jnp.stack(
        [
            lax.dynamic_index_in_dim(moved, (x_at - origin) % NX, 0, keepdims=False)
            for origin in range(NX)
        ]
    )
    placed = placed.reshape(2, NC, NZ, D).transpose(2, 1, 0, 3).reshape(PATCHES, D)
    placed = exchange(placed, REST_AXES)
    return placed[None, :, None]


def solution(mesh):
    own_mesh = Mesh(mesh.devices.reshape(NX, NY, NZ, NC), ("x",) + SP)
    return jax.shard_map(
        body,
        mesh=own_mesh,
        in_specs=(
            P(None, SP, None),
            P("x", None, None),
            P("x", SP, None),
            P("x", None, SP),
            P("x", None, SP, None, None),
        ),
        out_specs=P("x", None, SP, None),
        check_vma=False,
    )
```

```python
import math

import jax
import jax.numpy as jnp
from jax import lax
from jax.experimental import pallas as pl
from jax.experimental.pallas import tpu as pltpu
from jax.sharding import Mesh
from jax.sharding import PartitionSpec as P

D = 3072
HEADS = 24
HD = 128
PT = 64
PATCHES = 32
BLOCKS = 4
NX, NY, NZ, NC = 4, 4, 8, 2
SP = ("y", "z", "c")
HEAD_AXES = ("x", "y")
REST_AXES = ("z", "c")
MEMBERS = NX * NY
SOURCES = NY * NZ * NC
ROWS = D // SOURCES
OWN = 8
LOCAL = 2 * PT
AT_OUT, AT_K, AT_V, AT_SHARED = 3 * ROWS, 4 * ROWS, 4 * ROWS + PATCHES, 4 * ROWS + 2 * PATCHES
AT_SHARED_VO = AT_SHARED + ROWS
AT_SHARED_K = AT_SHARED + 2 * ROWS
AT_SHARED_V = AT_SHARED_K + PATCHES // 2
PIECE = AT_SHARED_V + PATCHES // 2
HALF = HD // 2
WIDTH = NC * NY * ROWS
FIRST_Z = 3
ANY = pl.BlockSpec(memory_space=pl.ANY)
SMEM = pl.BlockSpec(memory_space=pltpu.SMEM)
VMEM = pl.BlockSpec(memory_space=pltpu.VMEM)
SMALL = pltpu.CompilerParams(vmem_limit_bytes=24 * 1024 * 1024)
PARAMS = pltpu.CompilerParams(vmem_limit_bytes=24 * 1024 * 1024)


def head_norm(values):
    return (
        values * lax.rsqrt(jnp.mean(values * values, axis=-1, keepdims=True) + 1e-06)
    ).astype(jnp.bfloat16)


def modulate(rows, shift_term, scale_term):
    average = jnp.mean(rows, axis=-1, keepdims=True)
    centered = rows - average
    variance = jnp.mean(centered * centered, axis=-1, keepdims=True)
    return (centered * lax.rsqrt(variance + 1e-06) * (1.0 + scale_term) + shift_term).astype(
        jnp.bfloat16
    )


def pack_kernel(qkv_from, out_from, stale_ref, sent_ref, qkv_ref, out_ref, sems):
    copies = [
        pltpu.make_async_copy(qkv_from, qkv_ref, sems.at[0]),
        pltpu.make_async_copy(out_from, out_ref, sems.at[1]),
    ]
    for copy in copies:
        copy.start()

    def columns(head):
        return slice(head * HD, (head + 1) * HD)

    def put(member, low, rows):
        sent_ref[member, low : low + rows.shape[0], :] = rows

    def each():
        for member in range(MEMBERS):
            triple, half = divmod(member, 2)
            yield member, half, 3 * triple + 2 * half, 3 * triple + 1

    for member, half, own, shared in each():
        put(member, AT_K, stale_ref[0, :, columns(own)])
        put(member, AT_V, stale_ref[1, :, columns(own)])
        some = slice(half * PATCHES // 2, (half + 1) * PATCHES // 2)
        put(member, AT_SHARED_K, stale_ref[0, some, columns(shared)])
        put(member, AT_SHARED_V, stale_ref[1, some, columns(shared)])
    copies[1].wait()
    for member, half, own, shared in each():
        put(member, AT_OUT, out_ref[:, columns(own)])
    copies[0].wait()
    for member, half, own, shared in each():
        for part in range(3):
            put(member, part * ROWS, qkv_ref[:, columns(part * HEADS + own)])
        put(member, AT_SHARED, qkv_ref[:, columns(half * HEADS + shared)])
        w_v = qkv_ref[:, columns(2 * HEADS + shared)]
        w_o = out_ref[:, columns(shared)]
        lanes = slice(half * HALF, (half + 1) * HALF)
        put(member, AT_SHARED_VO, jnp.concatenate([w_v[:, lanes], w_o[:, lanes]], axis=1))


def first_kernel(rows_ref, shift_ref, scale_ref, normed_ref):
    normed = modulate(rows_ref[...].astype(jnp.float32), shift_ref[...], scale_ref[...])
    twice = jnp.concatenate([normed, normed], axis=0)
    for at in range(0, LOCAL, 2 * OWN):
        normed_ref[at : at + 2 * OWN, :] = twice


def sum_rows(parts_ref, rows_ref, gate_ref):
    total = jnp.zeros((2 * OWN, D), jnp.float32)
    for at in range(0, LOCAL, 2 * OWN):
        total = total + parts_ref[at : at + 2 * OWN, :].astype(jnp.float32)
    summed = total[:OWN] + total[OWN:]
    return (rows_ref[...].astype(jnp.float32) + gate_ref[...] * summed).astype(jnp.bfloat16)


def middle_kernel(parts_ref, rows_ref, gate_ref, shift_ref, scale_ref, updated_ref, normed_ref):
    updated = sum_rows(parts_ref, rows_ref, gate_ref)
    updated_ref[...] = updated
    normed = modulate(updated.astype(jnp.float32), shift_ref[...], scale_ref[...])
    twice = jnp.concatenate([normed, normed], axis=0)
    for at in range(0, LOCAL, 2 * OWN):
        normed_ref[at : at + 2 * OWN, :] = twice


def last_kernel(parts_ref, rows_ref, gate_ref, updated_ref):
    updated_ref[...] = sum_rows(parts_ref, rows_ref, gate_ref)


def across(left, right):
    return lax.dot_general(
        left, right, (((1,), (1,)), ((), ())), preferred_element_type=jnp.float32
    )


def piece_of(ref, low, count):
    return ref[:, :, low : low + count, :].reshape(NC * NY * count, HD)


def project(place_ref, rows_ref, refs, lows):
    total = jnp.zeros((LOCAL, len(lows) * HD), jnp.float32)
    for number, ref in enumerate(refs):
        at = pl.multiple_of(place_ref[FIRST_Z + number] * WIDTH, WIDTH)
        weight = jnp.concatenate([piece_of(ref, low, ROWS) for low in lows], axis=1)
        total = total + jnp.dot(
            rows_ref[:, pl.ds(at, WIDTH)], weight, preferred_element_type=jnp.float32
        )
    return total


def low_lanes(rows):
    return lax.broadcasted_iota(jnp.int32, (rows, HD), 1) < HALF


def pick(half, both):
    return jnp.where(half == 0, both[:PT], both[PT:])


def shared_project_kernel(place_ref, rows_ref, *refs):
    *pieces, kept_ref, given_ref = refs
    half = place_ref[1]
    both = project(place_ref, rows_ref, pieces, (AT_SHARED, AT_SHARED_VO))
    normed = head_norm(both[:, :HD])
    values = jnp.where(low_lanes(LOCAL), both[:, HD:], 0.0).astype(jnp.bfloat16)
    kept_ref[:LOCAL] = normed
    kept_ref[LOCAL:] = pick(half, values)
    given_ref[:LOCAL] = normed
    given_ref[LOCAL:] = pick(1 - half, values)


def own_project_kernel(place_ref, rows_ref, *refs):
    *pieces, own_ref = refs
    own = project(place_ref, rows_ref, pieces, (0, ROWS, 2 * ROWS))
    own_ref[:LOCAL] = head_norm(own[:, :HD])
    own_ref[LOCAL : 2 * LOCAL] = head_norm(own[:, HD : 2 * HD])
    own_ref[2 * LOCAL :] = own[:, 2 * HD :].astype(jnp.bfloat16)


def weigh(queries, keys):
    return jnp.exp(across(queries, keys) * (1.0 / math.sqrt(HD)))


def gather_values(numerator, values):
    return jnp.dot(numerator.astype(jnp.bfloat16), values, preferred_element_type=jnp.float32)


def attend_stale(
    queries, pieces, key_low, value_low, patches, first_column, row_patch, total, gathered
):
    shape = (queries.shape[0], NC * NY * patches)
    column_patch = first_column + lax.broadcasted_iota(jnp.int32, shape, 1) % patches
    stale_here = column_patch != row_patch
    for ref in pieces:
        keys = piece_of(ref, key_low, patches)
        numerator = jnp.where(stale_here, weigh(queries, keys), 0.0)
        total = total + jnp.sum(numerator, axis=1, keepdims=True)
        gathered = gathered + gather_values(numerator, piece_of(ref, value_low, patches))
    return total, gathered


def patch_of_rows(place_ref):
    second = lax.broadcasted_iota(jnp.int32, (LOCAL, 1), 0) >= PT
    return place_ref[0] + second.astype(jnp.int32)


def shared_attend_kernel(place_ref, kept_ref, got_ref, earlier_ref, *refs):
    del earlier_ref
    *pieces, sums_ref, given_ref = refs
    half = place_ref[1]
    kept, got = kept_ref[:LOCAL], got_ref[:LOCAL]
    queries = jnp.where(half == 0, kept, got)
    fresh_keys = jnp.where(half == 0, got[:PT], kept[PT:])
    mine, other = kept_ref[LOCAL:].astype(jnp.float32), got_ref[LOCAL:].astype(jnp.float32)
    low = jnp.where(half == 0, mine, other)
    high = jnp.where(half == 0, other, mine)
    fresh_values = jnp.where(low_lanes(PT), low, pltpu.roll(high, HALF, 1)).astype(jnp.bfloat16)
    fresh = weigh(pick(half, queries), fresh_keys)

    def placed(rows):
        nothing = jnp.zeros_like(rows)
        return jnp.concatenate(
            [jnp.where(half == 0, rows, nothing), jnp.where(half == 0, nothing, rows)], axis=0
        )

    total = placed(jnp.sum(fresh, axis=1, keepdims=True))
    gathered = placed(gather_values(fresh, fresh_values))
    total, gathered = attend_stale(
        queries,
        pieces,
        AT_SHARED_K,
        AT_SHARED_V,
        PATCHES // 2,
        half * (PATCHES // 2),
        patch_of_rows(place_ref),
        total,
        gathered,
    )
    swapped = pltpu.roll(gathered, HALF, 1)
    first = low_lanes(LOCAL)
    sums_ref[...] = jnp.where(first, total, jnp.where(half == 0, swapped, gathered))
    given_ref[...] = jnp.where(first, total, jnp.where(half == 0, gathered, swapped))


def own_attend_kernel(place_ref, own_ref, earlier_ref, *refs):
    del earlier_ref
    *pieces, attended_ref = refs
    queries = own_ref[:LOCAL]
    fresh = weigh(queries, own_ref[LOCAL : 2 * LOCAL])
    row_at = lax.broadcasted_iota(jnp.int32, (LOCAL, 1), 0)
    column_at = lax.broadcasted_iota(jnp.int32, (LOCAL, LOCAL), 1)
    fresh = jnp.where((row_at >= PT) == (column_at >= PT), fresh, 0.0)
    total = jnp.sum(fresh, axis=1, keepdims=True)
    gathered = gather_values(fresh, own_ref[2 * LOCAL :])
    total, gathered = attend_stale(
        queries, pieces, AT_K, AT_V, PATCHES, 0, patch_of_rows(place_ref), total, gathered
    )
    attended_ref[...] = (gathered / total).astype(jnp.bfloat16)


def finish_kernel(place_ref, attended_ref, sums_ref, got_ref, *refs):
    *pieces, partial_ref = refs
    sums = sums_ref[...] + got_ref[...]
    shared = jnp.where(low_lanes(LOCAL), 0.0, sums / sums[:, :1]).astype(jnp.bfloat16)
    attention = jnp.concatenate([attended_ref[...], shared], axis=1)
    for number, ref in enumerate(pieces):
        at = pl.multiple_of(place_ref[FIRST_Z + number] * WIDTH, WIDTH)
        weight = jnp.concatenate(
            [piece_of(ref, AT_OUT, ROWS), piece_of(ref, AT_SHARED_VO, ROWS)], axis=1
        )
        partial_ref[:, pl.ds(at, WIDTH)] = across(attention, weight).astype(jnp.bfloat16)


def pair_kernel(place_ref, own_ref, partner_ref, earlier_ref, pair_ref):
    del earlier_ref
    first = place_ref[2] == 0

    @pl.when(first)
    def _():
        pair_ref[0] = own_ref[...]
        pair_ref[1] = partner_ref[...]

    @pl.when(jnp.logical_not(first))
    def _():
        pair_ref[0] = partner_ref[...]
        pair_ref[1] = own_ref[...]


def to_own_order(array):
    lead = array.shape[:-1]
    split = array.reshape(lead + (NY, NZ * NC, ROWS))
    return jnp.swapaxes(split, -3, -2).reshape(lead + (D,))


def to_given_order(array):
    lead = array.shape[:-1]
    split = array.reshape(lead + (NZ * NC, NY, ROWS))
    return jnp.swapaxes(split, -3, -2).reshape(lead + (D,))


def exchange(array, axes):
    return lax.all_to_all(array, axes, split_axis=0, concat_axis=0, tiled=True)


def body(latent, modulation, w_qkv, w_out, stale):
    x_at, y_at = lax.axis_index("x"), lax.axis_index("y")
    pair_at = lax.axis_index("z") * NC + lax.axis_index("c")
    core_at, z_at = lax.axis_index("c"), lax.axis_index("z")
    way = 1 - 2 * core_at
    seen = [(z_at - way * step) % NZ for step in (0, 1, 2, 3, 4, -1, -2, -3)]
    place = jnp.stack([2 * pair_at, y_at % 2, core_at] + seen).astype(jnp.int32)
    swapped_cores = [(0, 1), (1, 0)]
    onward = [
        (z * NC + c, (z + 1 - 2 * c) % NZ * NC + c) for z in range(NZ) for c in range(NC)
    ]

    def go_round(own_piece, earlier):
        pair = pl.pallas_call(
            pair_kernel,
            out_shape=jax.ShapeDtypeStruct((NC,) + own_piece.shape, jnp.bfloat16),
            in_specs=[SMEM, VMEM, VMEM, VMEM],
            out_specs=VMEM,
            compiler_params=SMALL,
            name="pair",
        )(place, own_piece, lax.ppermute(own_piece, "c", swapped_cores), earlier)
        passed = [pair]
        for _ in range(NZ // 2):
            passed.append(lax.ppermute(passed[-1], REST_AXES, onward))
        return passed + [lax.ppermute(one, "c", swapped_cores) for one in passed[1 : NZ // 2]]


    sent = pl.pallas_call(
        pack_kernel,
        out_shape=jax.ShapeDtypeStruct((MEMBERS, PIECE, HD), jnp.bfloat16),
        in_specs=[ANY, ANY, VMEM],
        out_specs=VMEM,
        scratch_shapes=[
            pltpu.VMEM((ROWS, 3 * D), jnp.bfloat16),
            pltpu.VMEM((ROWS, D), jnp.bfloat16),
            pltpu.SemaphoreType.DMA((2,)),
        ],
        compiler_params=PARAMS,
        name="pack",
    )(w_qkv[0], w_out[0].T, jnp.swapaxes(stale[0, :, 0], 0, 1))
    received = exchange(sent, HEAD_AXES).reshape(BLOCKS, NY, PIECE, HD)

    source = go_round(received[0], stale[0, :8, 0, 0])

    terms = to_own_order(lax.all_gather(modulation[0], "x", axis=0, tiled=False))
    wanted = latent.reshape(NZ, NC, 2, D)
    wanted = lax.dynamic_index_in_dim(wanted, x_at // 2, 2, keepdims=False)
    same = lax.dynamic_index_in_dim(wanted, core_at, 1, keepdims=False)
    other = lax.dynamic_index_in_dim(wanted, 1 - core_at, 1, keepdims=False)
    other = lax.ppermute(other, "c", [(0, 1), (1, 0)])
    mine = exchange(jnp.where(core_at == x_at % 2, same, other), "z")
    current = to_own_order(mine)

    def term(block, which):
        return terms[block, which][None]

    spread = jax.ShapeDtypeStruct((LOCAL, D), jnp.bfloat16)
    owned = jax.ShapeDtypeStruct((OWN, D), jnp.bfloat16)
    normed = pl.pallas_call(
        first_kernel,
        out_shape=spread,
        in_specs=[VMEM] * 3,
        out_specs=VMEM,
        compiler_params=PARAMS,
        name="first",
    )(current, term(0, 0), term(0, 1))
    sums_of = jax.ShapeDtypeStruct((LOCAL, HD), jnp.float32)

    def rows_of(count):
        return jax.ShapeDtypeStruct((count, HD), jnp.bfloat16)

    def local(kernel, in_specs, out_shape, elements):
        return pl.pallas_call(
            kernel,
            out_shape=out_shape,
            in_specs=in_specs + (VMEM,) * NZ,
            out_specs=(VMEM,) * len(out_shape) if isinstance(out_shape, tuple) else VMEM,
            compiler_params=SMALL,
            cost_estimate=pl.CostEstimate(
                flops=2 * LOCAL * elements, bytes_accessed=2 * elements, transcendentals=0
            ),
            name=kernel.__name__,
        )

    def swap(array):
        return lax.ppermute(array, "y", [(at, at ^ 1) for at in range(NY)])

    outputs = []
    for block in range(BLOCKS):
        rows = exchange(normed, HEAD_AXES)
        kept, given = local(
            shared_project_kernel, (SMEM, VMEM),
            (rows_of(LOCAL + PT), rows_of(LOCAL + PT)), 2 * D * HD,
        )(place, rows, *source)
        got = swap(given)
        following = go_round(received[block + 1], kept) if block + 1 < BLOCKS else None
        own = local(own_project_kernel, (SMEM, VMEM), rows_of(3 * LOCAL), 3 * D * HD)(
            place, rows, *source
        )
        sums, given = local(
            shared_attend_kernel, (SMEM, VMEM, VMEM, VMEM), (sums_of, sums_of), PATCHES * PT * HD
        )(place, kept, got, own, *source)
        got = swap(given)
        attended = local(
            own_attend_kernel, (SMEM, VMEM, VMEM), rows_of(LOCAL), 2 * PATCHES * PT * HD
        )(place, own, sums, *source)
        partial = local(finish_kernel, (SMEM, VMEM, VMEM, VMEM), spread, 2 * D * HD)(
            place, attended, sums, got, *source
        )
        source = following
        parts = exchange(partial, HEAD_AXES)
        if block + 1 < BLOCKS:
            current, normed = pl.pallas_call(
                middle_kernel,
                out_shape=(owned, spread),
                in_specs=[VMEM] * 5,
                out_specs=(VMEM, VMEM),
                compiler_params=PARAMS,
                name="middle",
            )(parts, current, term(block, 2), term(block + 1, 0), term(block + 1, 1))
        else:
            current = pl.pallas_call(
                last_kernel,
                out_shape=owned,
                in_specs=[VMEM] * 3,
                out_specs=VMEM,
                compiler_params=PARAMS,
                name="last",
            )(parts, current, term(block, 2))
        outputs.append(to_given_order(current))
    outputs = jnp.stack(outputs)
    moved = [lax.dynamic_index_in_dim(outputs, x_at, 0, keepdims=False)]
    for step in range(1, NX):
        leaving = lax.dynamic_index_in_dim(outputs, (x_at + step) % NX, 0, keepdims=False)
        moved.append(lax.ppermute(leaving, "x", [(at, (at + step) % NX) for at in range(NX)]))
    moved = jnp.stack(moved)
    placed = jnp.stack(
        [
            lax.dynamic_index_in_dim(moved, (x_at - origin) % NX, 0, keepdims=False)
            for origin in range(NX)
        ]
    )
    placed = placed.reshape(2, NC, NZ, D).transpose(2, 1, 0, 3).reshape(PATCHES, D)
    placed = exchange(placed, REST_AXES)
    return placed[None, :, None]


def solution(mesh):
    own_mesh = Mesh(mesh.devices.reshape(NX, NY, NZ, NC), ("x",) + SP)
    return jax.shard_map(
        body,
        mesh=own_mesh,
        in_specs=(
            P(None, SP, None),
            P("x", None, None),
            P("x", SP, None),
            P("x", None, SP),
            P("x", None, SP, None, None),
        ),
        out_specs=P("x", None, SP, None),
        check_vma=False,
    )
```

```python
import math

import jax
import jax.numpy as jnp
from jax import lax
from jax.experimental import pallas as pl
from jax.experimental.pallas import tpu as pltpu
from jax.sharding import Mesh
from jax.sharding import PartitionSpec as P

D = 3072
HEADS = 24
HD = 128
PT = 64
PATCHES = 32
BLOCKS = 4
NX, NY, NZ, NC = 4, 4, 8, 2
SP = ("y", "z", "c")
HEAD_AXES = ("x", "y")
REST_AXES = ("z", "c")
MEMBERS = NX * NY
SOURCES = NY * NZ * NC
ROWS = D // SOURCES
OWN = 8
LOCAL = 2 * PT
AT_OUT, AT_K, AT_V, AT_SHARED = 3 * ROWS, 4 * ROWS, 4 * ROWS + PATCHES, 4 * ROWS + 2 * PATCHES
AT_SHARED_VO = AT_SHARED + ROWS
AT_SHARED_K = AT_SHARED + 2 * ROWS
AT_SHARED_V = AT_SHARED_K + PATCHES // 2
PIECE = AT_SHARED_V + PATCHES // 2
HALF = HD // 2
ANY = pl.BlockSpec(memory_space=pl.ANY)
SMEM = pl.BlockSpec(memory_space=pltpu.SMEM)
VMEM = pl.BlockSpec(memory_space=pltpu.VMEM)
SMALL = pltpu.CompilerParams(vmem_limit_bytes=24 * 1024 * 1024)
PARAMS = pltpu.CompilerParams(vmem_limit_bytes=48 * 1024 * 1024)


def head_norm(values):
    return (
        values * lax.rsqrt(jnp.mean(values * values, axis=-1, keepdims=True) + 1e-06)
    ).astype(jnp.bfloat16)


def modulate(rows, shift_term, scale_term):
    average = jnp.mean(rows, axis=-1, keepdims=True)
    centered = rows - average
    variance = jnp.mean(centered * centered, axis=-1, keepdims=True)
    return (centered * lax.rsqrt(variance + 1e-06) * (1.0 + scale_term) + shift_term).astype(
        jnp.bfloat16
    )


def pack_kernel(
    qkv_from, out_from, stale_from, sent_to, qkv_ref, out_ref, stale_ref, sent_ref, sems, sent_sems
):
    copies = [
        pltpu.make_async_copy(source, target, sems.at[number])
        for number, (source, target) in enumerate(
            ((stale_from, stale_ref), (out_from, out_ref), (qkv_from, qkv_ref))
        )
    ]
    for copy in copies:
        copy.start()

    def columns(head):
        return slice(head * HD, (head + 1) * HD)

    def put(member, low, rows):
        sent_ref[member, low : low + rows.shape[0], :] = rows

    def each():
        for member in range(MEMBERS):
            triple, half = divmod(member, 2)
            yield member, half, 3 * triple + 2 * half, 3 * triple + 1

    copies[0].wait()
    for member, half, own, shared in each():
        some = slice(half * PATCHES // 2, (half + 1) * PATCHES // 2)
        for kind, own_low, shared_low in ((0, AT_K, AT_SHARED_K), (1, AT_V, AT_SHARED_V)):
            put(member, own_low, stale_ref[:, kind, columns(own)])
            put(member, shared_low, stale_ref[some, kind, columns(shared)])
    copies[1].wait()
    for member, half, own, shared in each():
        put(member, AT_OUT, out_ref[:, columns(own)])
    copies[2].wait()
    leaving = []
    for member, half, own, shared in each():
        for part in range(3):
            put(member, part * ROWS, qkv_ref[:, columns(part * HEADS + own)])
        put(member, AT_SHARED, qkv_ref[:, columns(half * HEADS + shared)])
        w_v = qkv_ref[:, columns(2 * HEADS + shared)]
        w_o = out_ref[:, columns(shared)]
        lanes = slice(half * HALF, (half + 1) * HALF)
        put(member, AT_SHARED_VO, jnp.concatenate([w_v[:, lanes], w_o[:, lanes]], axis=1))
        leaving.append(
            pltpu.make_async_copy(sent_ref.at[member], sent_to.at[member], sent_sems.at[member])
        )
        leaving[-1].start()
    for copy in leaving:
        copy.wait()


def first_kernel(rows_ref, shift_ref, scale_ref, normed_ref):
    normed = modulate(rows_ref[...].astype(jnp.float32), shift_ref[...], scale_ref[...])
    twice = jnp.concatenate([normed, normed], axis=0)
    for at in range(0, LOCAL, 2 * OWN):
        normed_ref[at : at + 2 * OWN, :] = twice


def sum_rows(parts_ref, rows_ref, gate_ref):
    total = jnp.zeros((2 * OWN, D), jnp.float32)
    for at in range(0, LOCAL, 2 * OWN):
        total = total + parts_ref[at : at + 2 * OWN, :].astype(jnp.float32)
    summed = total[:OWN] + total[OWN:]
    return (rows_ref[...].astype(jnp.float32) + gate_ref[...] * summed).astype(jnp.bfloat16)


def middle_kernel(parts_ref, rows_ref, gate_ref, shift_ref, scale_ref, updated_ref, normed_ref):
    updated = sum_rows(parts_ref, rows_ref, gate_ref)
    updated_ref[...] = updated
    normed = modulate(updated.astype(jnp.float32), shift_ref[...], scale_ref[...])
    twice = jnp.concatenate([normed, normed], axis=0)
    for at in range(0, LOCAL, 2 * OWN):
        normed_ref[at : at + 2 * OWN, :] = twice


def last_kernel(parts_ref, rows_ref, gate_ref, updated_ref):
    updated_ref[...] = sum_rows(parts_ref, rows_ref, gate_ref)


def across(left, right):
    return lax.dot_general(
        left, right, (((1,), (1,)), ((), ())), preferred_element_type=jnp.float32
    )


def fetch(pieces_ref, sems, wanted):
    copies = [
        pltpu.make_async_copy(
            pieces_ref.at[:, low : low + target.shape[1], :], target, sems.at[number]
        )
        for number, (target, low) in enumerate(wanted)
    ]
    for copy in copies:
        copy.start()
    return copies


def project(rows, *parts):
    weight = jnp.concatenate([part[...].reshape(D, HD) for part in parts], axis=1)
    return jnp.dot(rows, weight, preferred_element_type=jnp.float32)


def low_lanes(rows):
    return lax.broadcasted_iota(jnp.int32, (rows, HD), 1) < HALF


def pick(half, both):
    return jnp.where(half == 0, both[:PT], both[PT:])


def shared_project_kernel(place_ref, rows_ref, pieces_ref, kept_ref, given_ref, w_qk, w_vo, sems):
    copies = fetch(pieces_ref, sems, [(w_qk, AT_SHARED), (w_vo, AT_SHARED_VO)])
    half = place_ref[1]
    rows = rows_ref[...]
    for copy in copies:
        copy.wait()
    both = project(rows, w_qk, w_vo)
    normed = head_norm(both[:, :HD])
    values = jnp.where(low_lanes(LOCAL), both[:, HD:], 0.0).astype(jnp.bfloat16)
    kept_ref[:LOCAL] = normed
    kept_ref[LOCAL:] = pick(half, values)
    given_ref[:LOCAL] = normed
    given_ref[LOCAL:] = pick(1 - half, values)


def own_project_kernel(rows_ref, pieces_ref, own_ref, keys, values, w_q, w_k, w_v, sems):
    copies = fetch(
        pieces_ref,
        sems,
        [
            (w_q, 0),
            (w_k, ROWS),
            (w_v, 2 * ROWS),
            (keys, AT_SHARED_K),
            (values, AT_SHARED_V),
        ],
    )
    rows = rows_ref[...]
    copies[0].wait()
    copies[1].wait()
    both = project(rows, w_q, w_k)
    own_ref[:LOCAL] = head_norm(both[:, :HD])
    own_ref[LOCAL : 2 * LOCAL] = head_norm(both[:, HD:])
    copies[2].wait()
    own_ref[2 * LOCAL :] = project(rows, w_v).astype(jnp.bfloat16)
    copies[3].wait()
    copies[4].wait()


def weigh(queries, keys):
    return jnp.exp(across(queries, keys) * (1.0 / math.sqrt(HD)))


def gather_values(numerator, values):
    return jnp.dot(numerator.astype(jnp.bfloat16), values, preferred_element_type=jnp.float32)


def attend_stale(queries, keys, values, first_column, row_patch, total, gathered):
    patches = keys.shape[1]
    step = 512 // patches
    shape = (queries.shape[0], step * patches)
    column_patch = first_column + lax.broadcasted_iota(jnp.int32, shape, 1) % patches
    stale_here = column_patch != row_patch
    for low in range(0, SOURCES, step):
        some_keys = keys[low : low + step].reshape(step * patches, HD)
        some_values = values[low : low + step].reshape(step * patches, HD)
        numerator = jnp.where(stale_here, weigh(queries, some_keys), 0.0)
        total = total + jnp.sum(numerator, axis=1, keepdims=True)
        gathered = gathered + gather_values(numerator, some_values)
    return total, gathered


def patch_of_rows(place_ref):
    second = lax.broadcasted_iota(jnp.int32, (LOCAL, 1), 0) >= PT
    return place_ref[0] + second.astype(jnp.int32)


def shared_attend_kernel(
    place_ref, kept_ref, got_ref, keys, values, sums_ref, given_ref
):
    half = place_ref[1]
    kept, got = kept_ref[:LOCAL], got_ref[:LOCAL]
    queries = jnp.where(half == 0, kept, got)
    fresh_keys = jnp.where(half == 0, got[:PT], kept[PT:])
    mine, other = kept_ref[LOCAL:].astype(jnp.float32), got_ref[LOCAL:].astype(jnp.float32)
    low = jnp.where(half == 0, mine, other)
    high = jnp.where(half == 0, other, mine)
    fresh_values = jnp.where(low_lanes(PT), low, pltpu.roll(high, HALF, 1)).astype(jnp.bfloat16)
    fresh = weigh(pick(half, queries), fresh_keys)

    def placed(rows):
        nothing = jnp.zeros_like(rows)
        return jnp.concatenate(
            [jnp.where(half == 0, rows, nothing), jnp.where(half == 0, nothing, rows)], axis=0
        )

    total = placed(jnp.sum(fresh, axis=1, keepdims=True))
    gathered = placed(gather_values(fresh, fresh_values))
    total, gathered = attend_stale(
        queries,
        keys,
        values,
        half * (PATCHES // 2),
        patch_of_rows(place_ref),
        total,
        gathered,
    )
    swapped = pltpu.roll(gathered, HALF, 1)
    first = low_lanes(LOCAL)
    sums_ref[...] = jnp.where(first, total, jnp.where(half == 0, swapped, gathered))
    given_ref[...] = jnp.where(first, total, jnp.where(half == 0, gathered, swapped))


def own_attend_kernel(
    place_ref, own_ref, earlier_ref, pieces_ref, attended_ref, w_own, w_vo, keys, values, sems
):
    del earlier_ref
    copies = fetch(
        pieces_ref,
        sems,
        [(keys, AT_K), (values, AT_V), (w_own, AT_OUT), (w_vo, AT_SHARED_VO)],
    )
    queries = own_ref[:LOCAL]
    fresh = weigh(queries, own_ref[LOCAL : 2 * LOCAL])
    row_at = lax.broadcasted_iota(jnp.int32, (LOCAL, 1), 0)
    column_at = lax.broadcasted_iota(jnp.int32, (LOCAL, LOCAL), 1)
    fresh = jnp.where((row_at >= PT) == (column_at >= PT), fresh, 0.0)
    total = jnp.sum(fresh, axis=1, keepdims=True)
    gathered = gather_values(fresh, own_ref[2 * LOCAL :])
    copies[0].wait()
    copies[1].wait()
    total, gathered = attend_stale(
        queries, keys, values, 0, patch_of_rows(place_ref), total, gathered
    )
    attended_ref[...] = (gathered / total).astype(jnp.bfloat16)
    copies[2].wait()
    copies[3].wait()


def finish_kernel(attended_ref, sums_ref, got_ref, w_own, w_vo, partial_ref):
    sums = sums_ref[...] + got_ref[...]
    shared = jnp.where(low_lanes(LOCAL), 0.0, sums / sums[:, :1]).astype(jnp.bfloat16)
    attention = jnp.concatenate([attended_ref[...], shared], axis=1)
    step = 8
    width = step * ROWS
    for low in range(0, SOURCES, step):
        weight = jnp.concatenate(
            [
                w_own[low : low + step].reshape(width, HD),
                w_vo[low : low + step].reshape(width, HD),
            ],
            axis=1,
        )
        partial_ref[:, low * ROWS : low * ROWS + width] = across(attention, weight).astype(
            jnp.bfloat16
        )


def to_own_order(array):
    lead = array.shape[:-1]
    split = array.reshape(lead + (NY, NZ * NC, ROWS))
    return jnp.swapaxes(split, -3, -2).reshape(lead + (D,))


def to_given_order(array):
    lead = array.shape[:-1]
    split = array.reshape(lead + (NZ * NC, NY, ROWS))
    return jnp.swapaxes(split, -3, -2).reshape(lead + (D,))


def exchange(array, axes):
    return lax.all_to_all(array, axes, split_axis=0, concat_axis=0, tiled=True)


def body(latent, modulation, w_qkv, w_out, stale):
    x_at, y_at = lax.axis_index("x"), lax.axis_index("y")
    pair_at = lax.axis_index("z") * NC + lax.axis_index("c")
    place = jnp.stack([2 * pair_at, y_at % 2]).astype(jnp.int32)

    sent = pl.pallas_call(
        pack_kernel,
        out_shape=jax.ShapeDtypeStruct((MEMBERS, PIECE, HD), jnp.bfloat16),
        in_specs=[ANY] * 3,
        out_specs=ANY,
        scratch_shapes=[
            pltpu.VMEM((ROWS, 3 * D), jnp.bfloat16),
            pltpu.VMEM((ROWS, D), jnp.bfloat16),
            pltpu.VMEM((PATCHES, 2, D), jnp.bfloat16),
            pltpu.VMEM((MEMBERS, PIECE, HD), jnp.bfloat16),
            pltpu.SemaphoreType.DMA((3,)),
            pltpu.SemaphoreType.DMA((MEMBERS,)),
        ],
        compiler_params=pltpu.CompilerParams(vmem_limit_bytes=60 * 1024 * 1024),
        name="pack",
    )(w_qkv[0], w_out[0].T, stale[0, :, 0])
    received = exchange(sent, HEAD_AXES).reshape(BLOCKS, NY, PIECE, HD)

    pieces = [
        lax.all_gather(received[block], REST_AXES, axis=0, tiled=True) for block in range(BLOCKS)
    ]

    terms = to_own_order(lax.all_gather(modulation[0], "x", axis=0, tiled=False))
    wanted = latent.reshape(NZ, NC, 2, D)
    wanted = lax.dynamic_index_in_dim(wanted, x_at // 2, 2, keepdims=False)
    core_at = lax.axis_index("c")
    same = lax.dynamic_index_in_dim(wanted, core_at, 1, keepdims=False)
    other = lax.dynamic_index_in_dim(wanted, 1 - core_at, 1, keepdims=False)
    other = lax.ppermute(other, "c", [(0, 1), (1, 0)])
    mine = exchange(jnp.where(core_at == x_at % 2, same, other), "z")
    current = to_own_order(mine)

    def term(block, which):
        return terms[block, which][None]

    spread = jax.ShapeDtypeStruct((LOCAL, D), jnp.bfloat16)
    owned = jax.ShapeDtypeStruct((OWN, D), jnp.bfloat16)
    normed = pl.pallas_call(
        first_kernel,
        out_shape=spread,
        in_specs=[VMEM] * 3,
        out_specs=VMEM,
        compiler_params=PARAMS,
        name="first",
    )(current, term(0, 0), term(0, 1))
    weight = pltpu.VMEM((SOURCES, ROWS, HD), jnp.bfloat16)
    cache = pltpu.VMEM((SOURCES, PATCHES, HD), jnp.bfloat16)
    half_cache = jax.ShapeDtypeStruct((SOURCES, PATCHES // 2, HD), jnp.bfloat16)
    kept_weight = jax.ShapeDtypeStruct((SOURCES, ROWS, HD), jnp.bfloat16)
    sums_of = jax.ShapeDtypeStruct((LOCAL, HD), jnp.float32)

    def rows_of(count):
        return jax.ShapeDtypeStruct((count, HD), jnp.bfloat16)

    def local(kernel, in_specs, out_specs, out_shape, scratch, copies, elements):
        return pl.pallas_call(
            kernel,
            out_shape=out_shape,
            in_specs=in_specs,
            out_specs=out_specs,
            scratch_shapes=scratch + [pltpu.SemaphoreType.DMA((copies,))] * (copies > 0),
            compiler_params=PARAMS if copies else SMALL,
            cost_estimate=pl.CostEstimate(
                flops=2 * LOCAL * elements, bytes_accessed=2 * elements, transcendentals=0
            ),
            name=kernel.__name__,
        )

    def swap(array):
        return lax.ppermute(array, "y", [(at, at ^ 1) for at in range(NY)])

    outputs = []
    for block in range(BLOCKS):
        rows = exchange(normed, HEAD_AXES)
        source = pieces[block]
        kept, given = local(
            shared_project_kernel, (SMEM, VMEM, ANY), (VMEM, VMEM),
            (rows_of(LOCAL + PT), rows_of(LOCAL + PT)), [weight] * 2, 2, 2 * D * HD,
        )(place, rows, source)
        got = swap(given)
        own, keys, values = local(
            own_project_kernel, (VMEM, ANY), (VMEM, VMEM, VMEM),
            (rows_of(3 * LOCAL), half_cache, half_cache), [weight] * 3, 5, 3 * D * HD,
        )(rows, source)
        sums, given = local(
            shared_attend_kernel, (SMEM,) + (VMEM,) * 4, (VMEM, VMEM),
            (sums_of, sums_of), [], 0, PATCHES * PT * HD,
        )(place, kept, got, keys, values)
        got = swap(given)
        attended, w_own, w_vo = local(
            own_attend_kernel, (SMEM, VMEM, VMEM, ANY), (VMEM, VMEM, VMEM),
            (rows_of(LOCAL), kept_weight, kept_weight), [cache] * 2, 4, 2 * PATCHES * PT * HD,
        )(place, own, sums, source)
        partial = local(
            finish_kernel, (VMEM,) * 5, VMEM, spread, [], 0, 2 * D * HD,
        )(attended, sums, got, w_own, w_vo)
        parts = exchange(partial, HEAD_AXES)
        if block + 1 < BLOCKS:
            current, normed = pl.pallas_call(
                middle_kernel,
                out_shape=(owned, spread),
                in_specs=[VMEM] * 5,
                out_specs=(VMEM, VMEM),
                compiler_params=PARAMS,
                name="middle",
            )(parts, current, term(block, 2), term(block + 1, 0), term(block + 1, 1))
        else:
            current = pl.pallas_call(
                last_kernel,
                out_shape=owned,
                in_specs=[VMEM] * 3,
                out_specs=VMEM,
                compiler_params=PARAMS,
                name="last",
            )(parts, current, term(block, 2))
        outputs.append(to_given_order(current))
    outputs = jnp.stack(outputs)
    moved = [lax.dynamic_index_in_dim(outputs, x_at, 0, keepdims=False)]
    for step in range(1, NX):
        leaving = lax.dynamic_index_in_dim(outputs, (x_at + step) % NX, 0, keepdims=False)
        moved.append(lax.ppermute(leaving, "x", [(at, (at + step) % NX) for at in range(NX)]))
    moved = jnp.stack(moved)
    placed = jnp.stack(
        [
            lax.dynamic_index_in_dim(moved, (x_at - origin) % NX, 0, keepdims=False)
            for origin in range(NX)
        ]
    )
    placed = placed.reshape(2, NC, NZ, D).transpose(2, 1, 0, 3).reshape(PATCHES, D)
    placed = exchange(placed, REST_AXES)
    return placed[None, :, None]


def solution(mesh):
    own_mesh = Mesh(mesh.devices.reshape(NX, NY, NZ, NC), ("x",) + SP)
    return jax.shard_map(
        body,
        mesh=own_mesh,
        in_specs=(
            P(None, SP, None),
            P("x", None, None),
            P("x", SP, None),
            P("x", None, SP),
            P("x", None, SP, None, None),
        ),
        out_specs=P("x", None, SP, None),
        check_vma=False,
    )
```

```python
import math

import jax
import jax.numpy as jnp
from jax import lax
from jax.experimental import pallas as pl
from jax.experimental.pallas import tpu as pltpu
from jax.sharding import Mesh
from jax.sharding import PartitionSpec as P

D = 3072
HEADS = 24
HD = 128
PT = 64
PATCHES = 32
BLOCKS = 4
NX, NY, NZ, NC = 4, 4, 8, 2
SP = ("y", "z", "c")
HEAD_AXES = ("x", "y")
REST_AXES = ("z", "c")
MEMBERS = NX * NY
SOURCES = NY * NZ * NC
ROWS = D // SOURCES
OWN = 8
LOCAL = 2 * PT
AT_OUT, AT_K, AT_V, AT_SHARED = 3 * ROWS, 4 * ROWS, 4 * ROWS + PATCHES, 4 * ROWS + 2 * PATCHES
AT_SHARED_VO = AT_SHARED + ROWS
AT_SHARED_K = AT_SHARED + 2 * ROWS
AT_SHARED_V = AT_SHARED_K + PATCHES // 2
PIECE = AT_SHARED_V + PATCHES // 2
HALF = HD // 2
ANY = pl.BlockSpec(memory_space=pl.ANY)
SMEM = pl.BlockSpec(memory_space=pltpu.SMEM)
VMEM = pl.BlockSpec(memory_space=pltpu.VMEM)
SMALL = pltpu.CompilerParams(vmem_limit_bytes=24 * 1024 * 1024)
PARAMS = pltpu.CompilerParams(vmem_limit_bytes=48 * 1024 * 1024)


def head_norm(values):
    return (
        values * lax.rsqrt(jnp.mean(values * values, axis=-1, keepdims=True) + 1e-06)
    ).astype(jnp.bfloat16)


def modulate(rows, shift_term, scale_term):
    average = jnp.mean(rows, axis=-1, keepdims=True)
    centered = rows - average
    variance = jnp.mean(centered * centered, axis=-1, keepdims=True)
    return (centered * lax.rsqrt(variance + 1e-06) * (1.0 + scale_term) + shift_term).astype(
        jnp.bfloat16
    )


def pack_kernel(
    qkv_from, out_from, stale_from, sent_to, qkv_ref, out_ref, stale_ref, sent_ref, sems, sent_sems
):
    copies = [
        pltpu.make_async_copy(source, target, sems.at[number])
        for number, (source, target) in enumerate(
            ((stale_from, stale_ref), (out_from, out_ref), (qkv_from, qkv_ref))
        )
    ]
    for copy in copies:
        copy.start()

    def columns(head):
        return slice(head * HD, (head + 1) * HD)

    def put(member, low, rows):
        sent_ref[member, low : low + rows.shape[0], :] = rows

    def each():
        for member in range(MEMBERS):
            triple, half = divmod(member, 2)
            yield member, half, 3 * triple + 2 * half, 3 * triple + 1

    copies[0].wait()
    for member, half, own, shared in each():
        some = slice(half * PATCHES // 2, (half + 1) * PATCHES // 2)
        for kind, own_low, shared_low in ((0, AT_K, AT_SHARED_K), (1, AT_V, AT_SHARED_V)):
            put(member, own_low, stale_ref[:, kind, columns(own)])
            put(member, shared_low, stale_ref[some, kind, columns(shared)])
    copies[1].wait()
    for member, half, own, shared in each():
        put(member, AT_OUT, out_ref[:, columns(own)])
    copies[2].wait()
    leaving = []
    for member, half, own, shared in each():
        for part in range(3):
            put(member, part * ROWS, qkv_ref[:, columns(part * HEADS + own)])
        put(member, AT_SHARED, qkv_ref[:, columns(half * HEADS + shared)])
        w_v = qkv_ref[:, columns(2 * HEADS + shared)]
        w_o = out_ref[:, columns(shared)]
        lanes = slice(half * HALF, (half + 1) * HALF)
        put(member, AT_SHARED_VO, jnp.concatenate([w_v[:, lanes], w_o[:, lanes]], axis=1))
        leaving.append(
            pltpu.make_async_copy(sent_ref.at[member], sent_to.at[member], sent_sems.at[member])
        )
        leaving[-1].start()
    for copy in leaving:
        copy.wait()


def first_kernel(rows_ref, shift_ref, scale_ref, normed_ref):
    normed = modulate(rows_ref[...].astype(jnp.float32), shift_ref[...], scale_ref[...])
    twice = jnp.concatenate([normed, normed], axis=0)
    for at in range(0, LOCAL, 2 * OWN):
        normed_ref[at : at + 2 * OWN, :] = twice


def sum_rows(parts_ref, rows_ref, gate_ref):
    total = jnp.zeros((2 * OWN, D), jnp.float32)
    for at in range(0, LOCAL, 2 * OWN):
        total = total + parts_ref[at : at + 2 * OWN, :].astype(jnp.float32)
    summed = total[:OWN] + total[OWN:]
    return (rows_ref[...].astype(jnp.float32) + gate_ref[...] * summed).astype(jnp.bfloat16)


def middle_kernel(parts_ref, rows_ref, gate_ref, shift_ref, scale_ref, updated_ref, normed_ref):
    updated = sum_rows(parts_ref, rows_ref, gate_ref)
    updated_ref[...] = updated
    normed = modulate(updated.astype(jnp.float32), shift_ref[...], scale_ref[...])
    twice = jnp.concatenate([normed, normed], axis=0)
    for at in range(0, LOCAL, 2 * OWN):
        normed_ref[at : at + 2 * OWN, :] = twice


def last_kernel(parts_ref, rows_ref, gate_ref, updated_ref):
    updated_ref[...] = sum_rows(parts_ref, rows_ref, gate_ref)


def across(left, right):
    return lax.dot_general(
        left, right, (((1,), (1,)), ((), ())), preferred_element_type=jnp.float32
    )


def fetch(pieces_ref, sems, wanted):
    copies = [
        pltpu.make_async_copy(
            pieces_ref.at[:, low : low + target.shape[1], :], target, sems.at[number]
        )
        for number, (target, low) in enumerate(wanted)
    ]
    for copy in copies:
        copy.start()
    return copies


def project(rows, *parts):
    weight = jnp.concatenate([part[...].reshape(D, HD) for part in parts], axis=1)
    return jnp.dot(rows, weight, preferred_element_type=jnp.float32)


def low_lanes(rows):
    return lax.broadcasted_iota(jnp.int32, (rows, HD), 1) < HALF


def pick(half, both):
    return jnp.where(half == 0, both[:PT], both[PT:])


def shared_project_kernel(place_ref, rows_ref, pieces_ref, kept_ref, given_ref, w_qk, w_vo, sems):
    copies = fetch(pieces_ref, sems, [(w_qk, AT_SHARED), (w_vo, AT_SHARED_VO)])
    half = place_ref[1]
    rows = rows_ref[...]
    for copy in copies:
        copy.wait()
    both = project(rows, w_qk, w_vo)
    normed = head_norm(both[:, :HD])
    values = jnp.where(low_lanes(LOCAL), both[:, HD:], 0.0).astype(jnp.bfloat16)
    kept_ref[:LOCAL] = normed
    kept_ref[LOCAL:] = pick(half, values)
    given_ref[:LOCAL] = normed
    given_ref[LOCAL:] = pick(1 - half, values)


def own_project_kernel(rows_ref, pieces_ref, own_ref, keys, values, w_q, w_k, w_v, sems):
    copies = fetch(
        pieces_ref,
        sems,
        [
            (w_q, 0),
            (w_k, ROWS),
            (w_v, 2 * ROWS),
            (keys, AT_SHARED_K),
            (values, AT_SHARED_V),
        ],
    )
    rows = rows_ref[...]
    copies[0].wait()
    copies[1].wait()
    both = project(rows, w_q, w_k)
    own_ref[:LOCAL] = head_norm(both[:, :HD])
    own_ref[LOCAL : 2 * LOCAL] = head_norm(both[:, HD:])
    copies[2].wait()
    own_ref[2 * LOCAL :] = project(rows, w_v).astype(jnp.bfloat16)
    copies[3].wait()
    copies[4].wait()


def weigh(queries, keys):
    return jnp.exp(across(queries, keys) * (1.0 / math.sqrt(HD)))


def gather_values(numerator, values):
    return jnp.dot(numerator.astype(jnp.bfloat16), values, preferred_element_type=jnp.float32)


def attend_stale(queries, keys, values, first_column, row_patch, total, gathered):
    patches = keys.shape[1]
    step = 512 // patches
    shape = (queries.shape[0], step * patches)
    column_patch = first_column + lax.broadcasted_iota(jnp.int32, shape, 1) % patches
    stale_here = column_patch != row_patch
    for low in range(0, SOURCES, step):
        some_keys = keys[low : low + step].reshape(step * patches, HD)
        some_values = values[low : low + step].reshape(step * patches, HD)
        numerator = jnp.where(stale_here, weigh(queries, some_keys), 0.0)
        total = total + jnp.sum(numerator, axis=1, keepdims=True)
        gathered = gathered + gather_values(numerator, some_values)
    return total, gathered


def patch_of_rows(place_ref):
    second = lax.broadcasted_iota(jnp.int32, (LOCAL, 1), 0) >= PT
    return place_ref[0] + second.astype(jnp.int32)


def shared_attend_kernel(
    place_ref, kept_ref, got_ref, keys, values, sums_ref, given_ref
):
    half = place_ref[1]
    kept, got = kept_ref[:LOCAL], got_ref[:LOCAL]
    queries = jnp.where(half == 0, kept, got)
    fresh_keys = jnp.where(half == 0, got[:PT], kept[PT:])
    mine, other = kept_ref[LOCAL:].astype(jnp.float32), got_ref[LOCAL:].astype(jnp.float32)
    low = jnp.where(half == 0, mine, other)
    high = jnp.where(half == 0, other, mine)
    fresh_values = jnp.where(low_lanes(PT), low, pltpu.roll(high, HALF, 1)).astype(jnp.bfloat16)
    fresh = weigh(pick(half, queries), fresh_keys)

    def placed(rows):
        nothing = jnp.zeros_like(rows)
        return jnp.concatenate(
            [jnp.where(half == 0, rows, nothing), jnp.where(half == 0, nothing, rows)], axis=0
        )

    total = placed(jnp.sum(fresh, axis=1, keepdims=True))
    gathered = placed(gather_values(fresh, fresh_values))
    total, gathered = attend_stale(
        queries,
        keys,
        values,
        half * (PATCHES // 2),
        patch_of_rows(place_ref),
        total,
        gathered,
    )
    swapped = pltpu.roll(gathered, HALF, 1)
    first = low_lanes(LOCAL)
    sums_ref[...] = jnp.where(first, total, jnp.where(half == 0, swapped, gathered))
    given_ref[...] = jnp.where(first, total, jnp.where(half == 0, gathered, swapped))


def own_attend_kernel(
    place_ref, own_ref, earlier_ref, pieces_ref, attended_ref, w_own, w_vo, keys, values, sems
):
    del earlier_ref
    copies = fetch(
        pieces_ref,
        sems,
        [(keys, AT_K), (values, AT_V), (w_own, AT_OUT), (w_vo, AT_SHARED_VO)],
    )
    queries = own_ref[:LOCAL]
    fresh = weigh(queries, own_ref[LOCAL : 2 * LOCAL])
    row_at = lax.broadcasted_iota(jnp.int32, (LOCAL, 1), 0)
    column_at = lax.broadcasted_iota(jnp.int32, (LOCAL, LOCAL), 1)
    fresh = jnp.where((row_at >= PT) == (column_at >= PT), fresh, 0.0)
    total = jnp.sum(fresh, axis=1, keepdims=True)
    gathered = gather_values(fresh, own_ref[2 * LOCAL :])
    copies[0].wait()
    copies[1].wait()
    total, gathered = attend_stale(
        queries, keys, values, 0, patch_of_rows(place_ref), total, gathered
    )
    attended_ref[...] = (gathered / total).astype(jnp.bfloat16)
    copies[2].wait()
    copies[3].wait()


def finish_kernel(attended_ref, sums_ref, got_ref, w_own, w_vo, partial_ref):
    sums = sums_ref[...] + got_ref[...]
    shared = jnp.where(low_lanes(LOCAL), 0.0, sums / sums[:, :1]).astype(jnp.bfloat16)
    attention = jnp.concatenate([attended_ref[...], shared], axis=1)
    step = 8
    width = step * ROWS
    for low in range(0, SOURCES, step):
        weight = jnp.concatenate(
            [
                w_own[low : low + step].reshape(width, HD),
                w_vo[low : low + step].reshape(width, HD),
            ],
            axis=1,
        )
        partial_ref[:, low * ROWS : low * ROWS + width] = across(attention, weight).astype(
            jnp.bfloat16
        )


def to_own_order(array):
    lead = array.shape[:-1]
    split = array.reshape(lead + (NY, NZ * NC, ROWS))
    return jnp.swapaxes(split, -3, -2).reshape(lead + (D,))


def to_given_order(array):
    lead = array.shape[:-1]
    split = array.reshape(lead + (NZ * NC, NY, ROWS))
    return jnp.swapaxes(split, -3, -2).reshape(lead + (D,))


def exchange(array, axes):
    return lax.all_to_all(array, axes, split_axis=0, concat_axis=0, tiled=True)


def body(latent, modulation, w_qkv, w_out, stale):
    x_at, y_at = lax.axis_index("x"), lax.axis_index("y")
    pair_at = lax.axis_index("z") * NC + lax.axis_index("c")
    place = jnp.stack([2 * pair_at, y_at % 2]).astype(jnp.int32)

    sent = pl.pallas_call(
        pack_kernel,
        out_shape=jax.ShapeDtypeStruct((MEMBERS, PIECE, HD), jnp.bfloat16),
        in_specs=[ANY] * 3,
        out_specs=ANY,
        scratch_shapes=[
            pltpu.VMEM((ROWS, 3 * D), jnp.bfloat16),
            pltpu.VMEM((ROWS, D), jnp.bfloat16),
            pltpu.VMEM((PATCHES, 2, D), jnp.bfloat16),
            pltpu.VMEM((MEMBERS, PIECE, HD), jnp.bfloat16),
            pltpu.SemaphoreType.DMA((3,)),
            pltpu.SemaphoreType.DMA((MEMBERS,)),
        ],
        compiler_params=pltpu.CompilerParams(vmem_limit_bytes=60 * 1024 * 1024),
        name="pack",
    )(w_qkv[0], w_out[0].T, stale[0, :, 0])
    received = exchange(sent, HEAD_AXES).reshape(BLOCKS, NY, PIECE, HD)

    pieces = [
        lax.all_gather(received[block], REST_AXES, axis=0, tiled=True) for block in range(BLOCKS)
    ]

    given = to_own_order(modulation[0])
    known = jnp.stack(
        [given]
        + [
            lax.ppermute(given, "x", [(at, (at + step) % NX) for at in range(NX)])
            for step in range(1, NX)
        ]
    )
    terms = [
        lax.dynamic_index_in_dim(known, (x_at - block) % NX, 0, keepdims=False)
        for block in range(BLOCKS)
    ]
    wanted = latent.reshape(NZ, NC, 2, D)
    wanted = lax.dynamic_index_in_dim(wanted, x_at // 2, 2, keepdims=False)
    core_at = lax.axis_index("c")
    same = lax.dynamic_index_in_dim(wanted, core_at, 1, keepdims=False)
    other = lax.dynamic_index_in_dim(wanted, 1 - core_at, 1, keepdims=False)
    other = lax.ppermute(other, "c", [(0, 1), (1, 0)])
    mine = exchange(jnp.where(core_at == x_at % 2, same, other), "z")
    current = to_own_order(mine)

    def term(block, which):
        return terms[block][which][None]

    spread = jax.ShapeDtypeStruct((LOCAL, D), jnp.bfloat16)
    owned = jax.ShapeDtypeStruct((OWN, D), jnp.bfloat16)
    normed = pl.pallas_call(
        first_kernel,
        out_shape=spread,
        in_specs=[VMEM] * 3,
        out_specs=VMEM,
        compiler_params=PARAMS,
        name="first",
    )(current, term(0, 0), term(0, 1))
    weight = pltpu.VMEM((SOURCES, ROWS, HD), jnp.bfloat16)
    cache = pltpu.VMEM((SOURCES, PATCHES, HD), jnp.bfloat16)
    half_cache = jax.ShapeDtypeStruct((SOURCES, PATCHES // 2, HD), jnp.bfloat16)
    kept_weight = jax.ShapeDtypeStruct((SOURCES, ROWS, HD), jnp.bfloat16)
    sums_of = jax.ShapeDtypeStruct((LOCAL, HD), jnp.float32)

    def rows_of(count):
        return jax.ShapeDtypeStruct((count, HD), jnp.bfloat16)

    def local(kernel, in_specs, out_specs, out_shape, scratch, copies, elements):
        return pl.pallas_call(
            kernel,
            out_shape=out_shape,
            in_specs=in_specs,
            out_specs=out_specs,
            scratch_shapes=scratch + [pltpu.SemaphoreType.DMA((copies,))] * (copies > 0),
            compiler_params=PARAMS if copies else SMALL,
            cost_estimate=pl.CostEstimate(
                flops=2 * LOCAL * elements, bytes_accessed=2 * elements, transcendentals=0
            ),
            name=kernel.__name__,
        )

    def swap(array):
        return lax.ppermute(array, "y", [(at, at ^ 1) for at in range(NY)])

    outputs = []
    for block in range(BLOCKS):
        rows = exchange(normed, HEAD_AXES)
        source = pieces[block]
        kept, given = local(
            shared_project_kernel, (SMEM, VMEM, ANY), (VMEM, VMEM),
            (rows_of(LOCAL + PT), rows_of(LOCAL + PT)), [weight] * 2, 2, 2 * D * HD,
        )(place, rows, source)
        got = swap(given)
        own, keys, values = local(
            own_project_kernel, (VMEM, ANY), (VMEM, VMEM, VMEM),
            (rows_of(3 * LOCAL), half_cache, half_cache), [weight] * 3, 5, 3 * D * HD,
        )(rows, source)
        sums, given = local(
            shared_attend_kernel, (SMEM,) + (VMEM,) * 4, (VMEM, VMEM),
            (sums_of, sums_of), [], 0, PATCHES * PT * HD,
        )(place, kept, got, keys, values)
        got = swap(given)
        attended, w_own, w_vo = local(
            own_attend_kernel, (SMEM, VMEM, VMEM, ANY), (VMEM, VMEM, VMEM),
            (rows_of(LOCAL), kept_weight, kept_weight), [cache] * 2, 4, 2 * PATCHES * PT * HD,
        )(place, own, sums, source)
        partial = local(
            finish_kernel, (VMEM,) * 5, VMEM, spread, [], 0, 2 * D * HD,
        )(attended, sums, got, w_own, w_vo)
        parts = exchange(partial, HEAD_AXES)
        if block + 1 < BLOCKS:
            current, normed = pl.pallas_call(
                middle_kernel,
                out_shape=(owned, spread),
                in_specs=[VMEM] * 5,
                out_specs=(VMEM, VMEM),
                compiler_params=PARAMS,
                name="middle",
            )(parts, current, term(block, 2), term(block + 1, 0), term(block + 1, 1))
        else:
            current = pl.pallas_call(
                last_kernel,
                out_shape=owned,
                in_specs=[VMEM] * 3,
                out_specs=VMEM,
                compiler_params=PARAMS,
                name="last",
            )(parts, current, term(block, 2))
        outputs.append(to_given_order(current))
    outputs = jnp.stack(outputs)
    moved = [lax.dynamic_index_in_dim(outputs, x_at, 0, keepdims=False)]
    for step in range(1, NX):
        leaving = lax.dynamic_index_in_dim(outputs, (x_at + step) % NX, 0, keepdims=False)
        moved.append(lax.ppermute(leaving, "x", [(at, (at + step) % NX) for at in range(NX)]))
    moved = jnp.stack(moved)
    placed = jnp.stack(
        [
            lax.dynamic_index_in_dim(moved, (x_at - origin) % NX, 0, keepdims=False)
            for origin in range(NX)
        ]
    )
    placed = placed.reshape(2, NC, NZ, D).transpose(2, 1, 0, 3).reshape(PATCHES, D)
    placed = exchange(placed, REST_AXES)
    return placed[None, :, None]


def solution(mesh):
    own_mesh = Mesh(mesh.devices.reshape(NX, NY, NZ, NC), ("x",) + SP)
    return jax.shard_map(
        body,
        mesh=own_mesh,
        in_specs=(
            P(None, SP, None),
            P("x", None, None),
            P("x", SP, None),
            P("x", None, SP),
            P("x", None, SP, None, None),
        ),
        out_specs=P("x", None, SP, None),
        check_vma=False,
    )
```

```python
import math

import jax
import jax.numpy as jnp
from jax import lax
from jax.experimental import pallas as pl
from jax.experimental.pallas import tpu as pltpu
from jax.sharding import Mesh
from jax.sharding import PartitionSpec as P

D = 3072
HEADS = 24
HD = 128
PT = 64
PATCHES = 32
BLOCKS = 4
NX, NY, NZ, NC = 4, 4, 8, 2
SP = ("y", "z", "c")
HEAD_AXES = ("x", "y")
REST_AXES = ("z", "c")
MEMBERS = NX * NY
SOURCES = NY * NZ * NC
ROWS = D // SOURCES
OWN = 8
LOCAL = 2 * PT
AT_OUT, AT_K, AT_V, AT_SHARED = 3 * ROWS, 4 * ROWS, 4 * ROWS + PATCHES, 4 * ROWS + 2 * PATCHES
AT_SHARED_VO = AT_SHARED + ROWS
AT_SHARED_K = AT_SHARED + 2 * ROWS
AT_SHARED_V = AT_SHARED_K + PATCHES // 2
PIECE = AT_SHARED_V + PATCHES // 2
HALF = HD // 2
ANY = pl.BlockSpec(memory_space=pl.ANY)
SMEM = pl.BlockSpec(memory_space=pltpu.SMEM)
VMEM = pl.BlockSpec(memory_space=pltpu.VMEM)
SMALL = pltpu.CompilerParams(vmem_limit_bytes=24 * 1024 * 1024)
PARAMS = pltpu.CompilerParams(vmem_limit_bytes=48 * 1024 * 1024)


def head_norm(values):
    return (
        values * lax.rsqrt(jnp.mean(values * values, axis=-1, keepdims=True) + 1e-06)
    ).astype(jnp.bfloat16)


def modulate(rows, shift_term, scale_term):
    average = jnp.mean(rows, axis=-1, keepdims=True)
    centered = rows - average
    variance = jnp.mean(centered * centered, axis=-1, keepdims=True)
    return (centered * lax.rsqrt(variance + 1e-06) * (1.0 + scale_term) + shift_term).astype(
        jnp.bfloat16
    )


def pack_kernel(
    qkv_from, out_from, stale_from, sent_to, qkv_ref, out_ref, stale_ref, sent_ref, sems, sent_sems
):
    copies = [
        pltpu.make_async_copy(source, target, sems.at[number])
        for number, (source, target) in enumerate(
            ((stale_from, stale_ref), (out_from, out_ref), (qkv_from, qkv_ref))
        )
    ]
    for copy in copies:
        copy.start()

    def columns(head):
        return slice(head * HD, (head + 1) * HD)

    def put(member, low, rows):
        sent_ref[member, low : low + rows.shape[0], :] = rows

    def each():
        for member in range(MEMBERS):
            triple, half = divmod(member, 2)
            yield member, half, 3 * triple + 2 * half, 3 * triple + 1

    copies[0].wait()
    for member, half, own, shared in each():
        some = slice(half * PATCHES // 2, (half + 1) * PATCHES // 2)
        for kind, own_low, shared_low in ((0, AT_K, AT_SHARED_K), (1, AT_V, AT_SHARED_V)):
            put(member, own_low, stale_ref[:, kind, columns(own)])
            put(member, shared_low, stale_ref[some, kind, columns(shared)])
    copies[1].wait()
    for member, half, own, shared in each():
        put(member, AT_OUT, out_ref[:, columns(own)])
    copies[2].wait()
    leaving = []
    for member, half, own, shared in each():
        for part in range(3):
            put(member, part * ROWS, qkv_ref[:, columns(part * HEADS + own)])
        put(member, AT_SHARED, qkv_ref[:, columns(half * HEADS + shared)])
        w_v = qkv_ref[:, columns(2 * HEADS + shared)]
        w_o = out_ref[:, columns(shared)]
        lanes = slice(half * HALF, (half + 1) * HALF)
        put(member, AT_SHARED_VO, jnp.concatenate([w_v[:, lanes], w_o[:, lanes]], axis=1))
        leaving.append(
            pltpu.make_async_copy(sent_ref.at[member], sent_to.at[member], sent_sems.at[member])
        )
        leaving[-1].start()
    for copy in leaving:
        copy.wait()


def later_kernel(received_ref, earlier_ref, *targets):
    del earlier_ref
    for block, target in enumerate(targets):
        target[...] = received_ref[block + 1]


def first_kernel(rows_ref, shift_ref, scale_ref, normed_ref):
    normed = modulate(rows_ref[...].astype(jnp.float32), shift_ref[...], scale_ref[...])
    twice = jnp.concatenate([normed, normed], axis=0)
    for at in range(0, LOCAL, 2 * OWN):
        normed_ref[at : at + 2 * OWN, :] = twice


def sum_rows(parts_ref, rows_ref, gate_ref):
    total = jnp.zeros((2 * OWN, D), jnp.float32)
    for at in range(0, LOCAL, 2 * OWN):
        total = total + parts_ref[at : at + 2 * OWN, :].astype(jnp.float32)
    summed = total[:OWN] + total[OWN:]
    return (rows_ref[...].astype(jnp.float32) + gate_ref[...] * summed).astype(jnp.bfloat16)


def middle_kernel(parts_ref, rows_ref, gate_ref, shift_ref, scale_ref, updated_ref, normed_ref):
    updated = sum_rows(parts_ref, rows_ref, gate_ref)
    updated_ref[...] = updated
    normed = modulate(updated.astype(jnp.float32), shift_ref[...], scale_ref[...])
    twice = jnp.concatenate([normed, normed], axis=0)
    for at in range(0, LOCAL, 2 * OWN):
        normed_ref[at : at + 2 * OWN, :] = twice


def last_kernel(parts_ref, rows_ref, gate_ref, updated_ref):
    updated_ref[...] = sum_rows(parts_ref, rows_ref, gate_ref)


def across(left, right):
    return lax.dot_general(
        left, right, (((1,), (1,)), ((), ())), preferred_element_type=jnp.float32
    )


def fetch(pieces_ref, sems, wanted):
    copies = [
        pltpu.make_async_copy(
            pieces_ref.at[:, low : low + target.shape[1], :], target, sems.at[number]
        )
        for number, (target, low) in enumerate(wanted)
    ]
    for copy in copies:
        copy.start()
    return copies


def project(rows, *parts):
    weight = jnp.concatenate([part[...].reshape(D, HD) for part in parts], axis=1)
    return jnp.dot(rows, weight, preferred_element_type=jnp.float32)


def low_lanes(rows):
    return lax.broadcasted_iota(jnp.int32, (rows, HD), 1) < HALF


def pick(half, both):
    return jnp.where(half == 0, both[:PT], both[PT:])


def shared_project_kernel(place_ref, rows_ref, pieces_ref, kept_ref, given_ref, w_qk, w_vo, sems):
    copies = fetch(pieces_ref, sems, [(w_qk, AT_SHARED), (w_vo, AT_SHARED_VO)])
    half = place_ref[1]
    rows = rows_ref[...]
    for copy in copies:
        copy.wait()
    both = project(rows, w_qk, w_vo)
    normed = head_norm(both[:, :HD])
    values = jnp.where(low_lanes(LOCAL), both[:, HD:], 0.0).astype(jnp.bfloat16)
    kept_ref[:LOCAL] = normed
    kept_ref[LOCAL:] = pick(half, values)
    given_ref[:LOCAL] = normed
    given_ref[LOCAL:] = pick(1 - half, values)


def own_project_kernel(rows_ref, pieces_ref, own_ref, keys, values, w_q, w_k, w_v, sems):
    copies = fetch(
        pieces_ref,
        sems,
        [
            (w_q, 0),
            (w_k, ROWS),
            (w_v, 2 * ROWS),
            (keys, AT_SHARED_K),
            (values, AT_SHARED_V),
        ],
    )
    rows = rows_ref[...]
    copies[0].wait()
    copies[1].wait()
    both = project(rows, w_q, w_k)
    own_ref[:LOCAL] = head_norm(both[:, :HD])
    own_ref[LOCAL : 2 * LOCAL] = head_norm(both[:, HD:])
    copies[2].wait()
    own_ref[2 * LOCAL :] = project(rows, w_v).astype(jnp.bfloat16)
    copies[3].wait()
    copies[4].wait()


def weigh(queries, keys):
    return jnp.exp(across(queries, keys) * (1.0 / math.sqrt(HD)))


def gather_values(numerator, values):
    return jnp.dot(numerator.astype(jnp.bfloat16), values, preferred_element_type=jnp.float32)


def attend_stale(queries, keys, values, first_column, row_patch, total, gathered):
    patches = keys.shape[1]
    step = 512 // patches
    shape = (queries.shape[0], step * patches)
    column_patch = first_column + lax.broadcasted_iota(jnp.int32, shape, 1) % patches
    stale_here = column_patch != row_patch
    for low in range(0, SOURCES, step):
        some_keys = keys[low : low + step].reshape(step * patches, HD)
        some_values = values[low : low + step].reshape(step * patches, HD)
        numerator = jnp.where(stale_here, weigh(queries, some_keys), 0.0)
        total = total + jnp.sum(numerator, axis=1, keepdims=True)
        gathered = gathered + gather_values(numerator, some_values)
    return total, gathered


def patch_of_rows(place_ref):
    second = lax.broadcasted_iota(jnp.int32, (LOCAL, 1), 0) >= PT
    return place_ref[0] + second.astype(jnp.int32)


def shared_attend_kernel(
    place_ref, kept_ref, got_ref, keys, values, sums_ref, given_ref
):
    half = place_ref[1]
    kept, got = kept_ref[:LOCAL], got_ref[:LOCAL]
    queries = jnp.where(half == 0, kept, got)
    fresh_keys = jnp.where(half == 0, got[:PT], kept[PT:])
    mine, other = kept_ref[LOCAL:].astype(jnp.float32), got_ref[LOCAL:].astype(jnp.float32)
    low = jnp.where(half == 0, mine, other)
    high = jnp.where(half == 0, other, mine)
    fresh_values = jnp.where(low_lanes(PT), low, pltpu.roll(high, HALF, 1)).astype(jnp.bfloat16)
    fresh = weigh(pick(half, queries), fresh_keys)

    def placed(rows):
        nothing = jnp.zeros_like(rows)
        return jnp.concatenate(
            [jnp.where(half == 0, rows, nothing), jnp.where(half == 0, nothing, rows)], axis=0
        )

    total = placed(jnp.sum(fresh, axis=1, keepdims=True))
    gathered = placed(gather_values(fresh, fresh_values))
    total, gathered = attend_stale(
        queries,
        keys,
        values,
        half * (PATCHES // 2),
        patch_of_rows(place_ref),
        total,
        gathered,
    )
    swapped = pltpu.roll(gathered, HALF, 1)
    first = low_lanes(LOCAL)
    sums_ref[...] = jnp.where(first, total, jnp.where(half == 0, swapped, gathered))
    given_ref[...] = jnp.where(first, total, jnp.where(half == 0, gathered, swapped))


def own_attend_kernel(
    place_ref, own_ref, earlier_ref, pieces_ref, attended_ref, w_own, w_vo, keys, values, sems
):
    del earlier_ref
    copies = fetch(
        pieces_ref,
        sems,
        [(keys, AT_K), (values, AT_V), (w_own, AT_OUT), (w_vo, AT_SHARED_VO)],
    )
    queries = own_ref[:LOCAL]
    fresh = weigh(queries, own_ref[LOCAL : 2 * LOCAL])
    row_at = lax.broadcasted_iota(jnp.int32, (LOCAL, 1), 0)
    column_at = lax.broadcasted_iota(jnp.int32, (LOCAL, LOCAL), 1)
    fresh = jnp.where((row_at >= PT) == (column_at >= PT), fresh, 0.0)
    total = jnp.sum(fresh, axis=1, keepdims=True)
    gathered = gather_values(fresh, own_ref[2 * LOCAL :])
    copies[0].wait()
    copies[1].wait()
    total, gathered = attend_stale(
        queries, keys, values, 0, patch_of_rows(place_ref), total, gathered
    )
    attended_ref[...] = (gathered / total).astype(jnp.bfloat16)
    copies[2].wait()
    copies[3].wait()


def finish_kernel(attended_ref, sums_ref, got_ref, w_own, w_vo, partial_ref):
    sums = sums_ref[...] + got_ref[...]
    shared = jnp.where(low_lanes(LOCAL), 0.0, sums / sums[:, :1]).astype(jnp.bfloat16)
    attention = jnp.concatenate([attended_ref[...], shared], axis=1)
    step = 8
    width = step * ROWS
    for low in range(0, SOURCES, step):
        weight = jnp.concatenate(
            [
                w_own[low : low + step].reshape(width, HD),
                w_vo[low : low + step].reshape(width, HD),
            ],
            axis=1,
        )
        partial_ref[:, low * ROWS : low * ROWS + width] = across(attention, weight).astype(
            jnp.bfloat16
        )


def to_own_order(array):
    lead = array.shape[:-1]
    split = array.reshape(lead + (NY, NZ * NC, ROWS))
    return jnp.swapaxes(split, -3, -2).reshape(lead + (D,))


def to_given_order(array):
    lead = array.shape[:-1]
    split = array.reshape(lead + (NZ * NC, NY, ROWS))
    return jnp.swapaxes(split, -3, -2).reshape(lead + (D,))


def exchange(array, axes):
    return lax.all_to_all(array, axes, split_axis=0, concat_axis=0, tiled=True)


def body(latent, modulation, w_qkv, w_out, stale):
    x_at, y_at = lax.axis_index("x"), lax.axis_index("y")
    pair_at = lax.axis_index("z") * NC + lax.axis_index("c")
    place = jnp.stack([2 * pair_at, y_at % 2]).astype(jnp.int32)

    sent = pl.pallas_call(
        pack_kernel,
        out_shape=jax.ShapeDtypeStruct((MEMBERS, PIECE, HD), jnp.bfloat16),
        in_specs=[ANY] * 3,
        out_specs=ANY,
        scratch_shapes=[
            pltpu.VMEM((ROWS, 3 * D), jnp.bfloat16),
            pltpu.VMEM((ROWS, D), jnp.bfloat16),
            pltpu.VMEM((PATCHES, 2, D), jnp.bfloat16),
            pltpu.VMEM((MEMBERS, PIECE, HD), jnp.bfloat16),
            pltpu.SemaphoreType.DMA((3,)),
            pltpu.SemaphoreType.DMA((MEMBERS,)),
        ],
        compiler_params=pltpu.CompilerParams(vmem_limit_bytes=60 * 1024 * 1024),
        name="pack",
    )(w_qkv[0], w_out[0].T, stale[0, :, 0])
    received = exchange(sent, HEAD_AXES).reshape(BLOCKS, NY, PIECE, HD)

    def gather(own_piece):
        return lax.all_gather(own_piece, REST_AXES, axis=0, tiled=True)

    pieces = [gather(received[0])]

    given = to_own_order(modulation[0])
    known = jnp.stack(
        [given]
        + [
            lax.ppermute(given, "x", [(at, (at + step) % NX) for at in range(NX)])
            for step in range(1, NX)
        ]
    )
    terms = [
        lax.dynamic_index_in_dim(known, (x_at - block) % NX, 0, keepdims=False)
        for block in range(BLOCKS)
    ]
    wanted = latent.reshape(NZ, NC, 2, D)
    wanted = lax.dynamic_index_in_dim(wanted, x_at // 2, 2, keepdims=False)
    core_at = lax.axis_index("c")
    same = lax.dynamic_index_in_dim(wanted, core_at, 1, keepdims=False)
    other = lax.dynamic_index_in_dim(wanted, 1 - core_at, 1, keepdims=False)
    other = lax.ppermute(other, "c", [(0, 1), (1, 0)])
    mine = exchange(jnp.where(core_at == x_at % 2, same, other), "z")
    current = to_own_order(mine)

    def term(block, which):
        return terms[block][which][None]

    spread = jax.ShapeDtypeStruct((LOCAL, D), jnp.bfloat16)
    owned = jax.ShapeDtypeStruct((OWN, D), jnp.bfloat16)
    normed = pl.pallas_call(
        first_kernel,
        out_shape=spread,
        in_specs=[VMEM] * 3,
        out_specs=VMEM,
        compiler_params=PARAMS,
        name="first",
    )(current, term(0, 0), term(0, 1))
    later = pl.pallas_call(
        later_kernel,
        out_shape=[jax.ShapeDtypeStruct((NY, PIECE, HD), jnp.bfloat16)] * (BLOCKS - 1),
        in_specs=[VMEM, VMEM],
        out_specs=[VMEM] * (BLOCKS - 1),
        compiler_params=SMALL,
        name="later",
    )(received, normed)
    pieces += [gather(own_piece) for own_piece in later]
    weight = pltpu.VMEM((SOURCES, ROWS, HD), jnp.bfloat16)
    cache = pltpu.VMEM((SOURCES, PATCHES, HD), jnp.bfloat16)
    half_cache = jax.ShapeDtypeStruct((SOURCES, PATCHES // 2, HD), jnp.bfloat16)
    kept_weight = jax.ShapeDtypeStruct((SOURCES, ROWS, HD), jnp.bfloat16)
    sums_of = jax.ShapeDtypeStruct((LOCAL, HD), jnp.float32)

    def rows_of(count):
        return jax.ShapeDtypeStruct((count, HD), jnp.bfloat16)

    def local(kernel, in_specs, out_specs, out_shape, scratch, copies, elements):
        return pl.pallas_call(
            kernel,
            out_shape=out_shape,
            in_specs=in_specs,
            out_specs=out_specs,
            scratch_shapes=scratch + [pltpu.SemaphoreType.DMA((copies,))] * (copies > 0),
            compiler_params=PARAMS if copies else SMALL,
            cost_estimate=pl.CostEstimate(
                flops=2 * LOCAL * elements, bytes_accessed=2 * elements, transcendentals=0
            ),
            name=kernel.__name__,
        )

    def swap(array):
        return lax.ppermute(array, "y", [(at, at ^ 1) for at in range(NY)])

    outputs = []
    for block in range(BLOCKS):
        rows = exchange(normed, HEAD_AXES)
        source = pieces[block]
        kept, given = local(
            shared_project_kernel, (SMEM, VMEM, ANY), (VMEM, VMEM),
            (rows_of(LOCAL + PT), rows_of(LOCAL + PT)), [weight] * 2, 2, 2 * D * HD,
        )(place, rows, source)
        got = swap(given)
        own, keys, values = local(
            own_project_kernel, (VMEM, ANY), (VMEM, VMEM, VMEM),
            (rows_of(3 * LOCAL), half_cache, half_cache), [weight] * 3, 5, 3 * D * HD,
        )(rows, source)
        sums, given = local(
            shared_attend_kernel, (SMEM,) + (VMEM,) * 4, (VMEM, VMEM),
            (sums_of, sums_of), [], 0, PATCHES * PT * HD,
        )(place, kept, got, keys, values)
        got = swap(given)
        attended, w_own, w_vo = local(
            own_attend_kernel, (SMEM, VMEM, VMEM, ANY), (VMEM, VMEM, VMEM),
            (rows_of(LOCAL), kept_weight, kept_weight), [cache] * 2, 4, 2 * PATCHES * PT * HD,
        )(place, own, sums, source)
        partial = local(
            finish_kernel, (VMEM,) * 5, VMEM, spread, [], 0, 2 * D * HD,
        )(attended, sums, got, w_own, w_vo)
        parts = exchange(partial, HEAD_AXES)
        if block + 1 < BLOCKS:
            current, normed = pl.pallas_call(
                middle_kernel,
                out_shape=(owned, spread),
                in_specs=[VMEM] * 5,
                out_specs=(VMEM, VMEM),
                compiler_params=PARAMS,
                name="middle",
            )(parts, current, term(block, 2), term(block + 1, 0), term(block + 1, 1))
        else:
            current = pl.pallas_call(
                last_kernel,
                out_shape=owned,
                in_specs=[VMEM] * 3,
                out_specs=VMEM,
                compiler_params=PARAMS,
                name="last",
            )(parts, current, term(block, 2))
        outputs.append(to_given_order(current))
    outputs = jnp.stack(outputs)
    moved = [lax.dynamic_index_in_dim(outputs, x_at, 0, keepdims=False)]
    for step in range(1, NX):
        leaving = lax.dynamic_index_in_dim(outputs, (x_at + step) % NX, 0, keepdims=False)
        moved.append(lax.ppermute(leaving, "x", [(at, (at + step) % NX) for at in range(NX)]))
    moved = jnp.stack(moved)
    placed = jnp.stack(
        [
            lax.dynamic_index_in_dim(moved, (x_at - origin) % NX, 0, keepdims=False)
            for origin in range(NX)
        ]
    )
    placed = placed.reshape(2, NC, NZ, D).transpose(2, 1, 0, 3).reshape(PATCHES, D)
    placed = exchange(placed, REST_AXES)
    return placed[None, :, None]


def solution(mesh):
    own_mesh = Mesh(mesh.devices.reshape(NX, NY, NZ, NC), ("x",) + SP)
    return jax.shard_map(
        body,
        mesh=own_mesh,
        in_specs=(
            P(None, SP, None),
            P("x", None, None),
            P("x", SP, None),
            P("x", None, SP),
            P("x", None, SP, None, None),
        ),
        out_specs=P("x", None, SP, None),
        check_vma=False,
    )
```

```python
import math

import jax
import jax.numpy as jnp
from jax import lax
from jax.experimental import pallas as pl
from jax.experimental.pallas import tpu as pltpu
from jax.sharding import Mesh
from jax.sharding import PartitionSpec as P

D = 3072
HEADS = 24
HD = 128
PT = 64
PATCHES = 32
BLOCKS = 4
NX, NY, NZ, NC = 4, 4, 8, 2
SP = ("y", "z", "c")
HEAD_AXES = ("x", "y")
REST_AXES = ("z", "c")
MEMBERS = NX * NY
SOURCES = NY * NZ * NC
ROWS = D // SOURCES
OWN = 8
LOCAL = 2 * PT
AT_OUT, AT_K, AT_V, AT_SHARED = 3 * ROWS, 4 * ROWS, 4 * ROWS + PATCHES, 4 * ROWS + 2 * PATCHES
AT_SHARED_VO = AT_SHARED + ROWS
AT_SHARED_K = AT_SHARED + 2 * ROWS
AT_SHARED_V = AT_SHARED_K + PATCHES // 2
PIECE = AT_SHARED_V + PATCHES // 2
HALF = HD // 2
ANY = pl.BlockSpec(memory_space=pl.ANY)
SMEM = pl.BlockSpec(memory_space=pltpu.SMEM)
VMEM = pl.BlockSpec(memory_space=pltpu.VMEM)
SMALL = pltpu.CompilerParams(vmem_limit_bytes=24 * 1024 * 1024)
PARAMS = pltpu.CompilerParams(vmem_limit_bytes=48 * 1024 * 1024)


def head_norm(values):
    return (
        values * lax.rsqrt(jnp.mean(values * values, axis=-1, keepdims=True) + 1e-06)
    ).astype(jnp.bfloat16)


def modulate(rows, shift_term, scale_term):
    average = jnp.mean(rows, axis=-1, keepdims=True)
    centered = rows - average
    variance = jnp.mean(centered * centered, axis=-1, keepdims=True)
    return (centered * lax.rsqrt(variance + 1e-06) * (1.0 + scale_term) + shift_term).astype(
        jnp.bfloat16
    )


def pack_kernel(
    qkv_from, out_from, stale_from, sent_to, qkv_ref, out_ref, stale_ref, sent_ref, sems, sent_sems
):
    copies = [
        pltpu.make_async_copy(source, target, sems.at[number])
        for number, (source, target) in enumerate(
            ((stale_from, stale_ref), (out_from, out_ref), (qkv_from, qkv_ref))
        )
    ]
    for copy in copies:
        copy.start()

    def columns(head):
        return slice(head * HD, (head + 1) * HD)

    def put(member, low, rows):
        sent_ref[member, low : low + rows.shape[0], :] = rows

    def each():
        for member in range(MEMBERS):
            triple, half = divmod(member, 2)
            yield member, half, 3 * triple + 2 * half, 3 * triple + 1

    copies[0].wait()
    for member, half, own, shared in each():
        some = slice(half * PATCHES // 2, (half + 1) * PATCHES // 2)
        for kind, own_low, shared_low in ((0, AT_K, AT_SHARED_K), (1, AT_V, AT_SHARED_V)):
            put(member, own_low, stale_ref[:, kind, columns(own)])
            put(member, shared_low, stale_ref[some, kind, columns(shared)])
    copies[1].wait()
    for member, half, own, shared in each():
        put(member, AT_OUT, out_ref[:, columns(own)])
    copies[2].wait()
    leaving = []
    for member, half, own, shared in each():
        for part in range(3):
            put(member, part * ROWS, qkv_ref[:, columns(part * HEADS + own)])
        put(member, AT_SHARED, qkv_ref[:, columns(half * HEADS + shared)])
        w_v = qkv_ref[:, columns(2 * HEADS + shared)]
        w_o = out_ref[:, columns(shared)]
        lanes = slice(half * HALF, (half + 1) * HALF)
        put(member, AT_SHARED_VO, jnp.concatenate([w_v[:, lanes], w_o[:, lanes]], axis=1))
        leaving.append(
            pltpu.make_async_copy(sent_ref.at[member], sent_to.at[member], sent_sems.at[member])
        )
        leaving[-1].start()
    for copy in leaving:
        copy.wait()


def later_kernel(received_ref, earlier_ref, *targets):
    del earlier_ref
    for block, target in enumerate(targets):
        target[...] = received_ref[block + 1]


def first_kernel(rows_ref, shift_ref, scale_ref, normed_ref):
    normed = modulate(rows_ref[...].astype(jnp.float32), shift_ref[...], scale_ref[...])
    twice = jnp.concatenate([normed, normed], axis=0)
    for at in range(0, LOCAL, 2 * OWN):
        normed_ref[at : at + 2 * OWN, :] = twice


def sum_rows(parts_ref, rows_ref, gate_ref):
    total = jnp.zeros((2 * OWN, D), jnp.float32)
    for at in range(0, LOCAL, 2 * OWN):
        total = total + parts_ref[at : at + 2 * OWN, :].astype(jnp.float32)
    summed = total[:OWN] + total[OWN:]
    return (rows_ref[...].astype(jnp.float32) + gate_ref[...] * summed).astype(jnp.bfloat16)


def middle_kernel(parts_ref, rows_ref, gate_ref, shift_ref, scale_ref, updated_ref, normed_ref):
    updated = sum_rows(parts_ref, rows_ref, gate_ref)
    updated_ref[...] = updated
    normed = modulate(updated.astype(jnp.float32), shift_ref[...], scale_ref[...])
    twice = jnp.concatenate([normed, normed], axis=0)
    for at in range(0, LOCAL, 2 * OWN):
        normed_ref[at : at + 2 * OWN, :] = twice


def last_kernel(parts_ref, rows_ref, gate_ref, updated_ref):
    updated_ref[...] = sum_rows(parts_ref, rows_ref, gate_ref)


def across(left, right):
    return lax.dot_general(
        left, right, (((1,), (1,)), ((), ())), preferred_element_type=jnp.float32
    )


def fetch(pieces_ref, sems, wanted):
    copies = [
        pltpu.make_async_copy(
            pieces_ref.at[:, low : low + target.shape[1], :], target, sems.at[number]
        )
        for number, (target, low) in enumerate(wanted)
    ]
    for copy in copies:
        copy.start()
    return copies


def project(rows, *parts):
    weight = jnp.concatenate([part[...].reshape(D, HD) for part in parts], axis=1)
    return jnp.dot(rows, weight, preferred_element_type=jnp.float32)


def low_lanes(rows):
    return lax.broadcasted_iota(jnp.int32, (rows, HD), 1) < HALF


def pick(half, both):
    return jnp.where(half == 0, both[:PT], both[PT:])


def shared_project_kernel(place_ref, rows_ref, pieces_ref, kept_ref, given_ref, w_qk, w_vo, sems):
    copies = fetch(pieces_ref, sems, [(w_qk, AT_SHARED), (w_vo, AT_SHARED_VO)])
    half = place_ref[1]
    rows = rows_ref[...]
    for copy in copies:
        copy.wait()
    both = project(rows, w_qk, w_vo)
    normed = head_norm(both[:, :HD])
    values = jnp.where(low_lanes(LOCAL), both[:, HD:], 0.0).astype(jnp.bfloat16)
    kept_ref[:LOCAL] = normed
    kept_ref[LOCAL:] = pick(half, values)
    given_ref[:LOCAL] = normed
    given_ref[LOCAL:] = pick(1 - half, values)


def own_project_kernel(rows_ref, pieces_ref, own_ref, keys, values, w_q, w_k, w_v, sems):
    copies = fetch(
        pieces_ref,
        sems,
        [
            (w_q, 0),
            (w_k, ROWS),
            (w_v, 2 * ROWS),
            (keys, AT_SHARED_K),
            (values, AT_SHARED_V),
        ],
    )
    rows = rows_ref[...]
    copies[0].wait()
    copies[1].wait()
    both = project(rows, w_q, w_k)
    own_ref[:LOCAL] = head_norm(both[:, :HD])
    own_ref[LOCAL : 2 * LOCAL] = head_norm(both[:, HD:])
    copies[2].wait()
    own_ref[2 * LOCAL :] = project(rows, w_v).astype(jnp.bfloat16)
    copies[3].wait()
    copies[4].wait()


def weigh(queries, keys):
    return jnp.exp(across(queries, keys) * (1.0 / math.sqrt(HD)))


def gather_values(numerator, values):
    return jnp.dot(numerator.astype(jnp.bfloat16), values, preferred_element_type=jnp.float32)


def attend_stale(queries, keys, values, first_column, row_patch, total, gathered):
    patches = keys.shape[1]
    step = 512 // patches
    shape = (queries.shape[0], step * patches)
    column_patch = first_column + lax.broadcasted_iota(jnp.int32, shape, 1) % patches
    stale_here = column_patch != row_patch
    for low in range(0, SOURCES, step):
        some_keys = keys[low : low + step].reshape(step * patches, HD)
        some_values = values[low : low + step].reshape(step * patches, HD)
        numerator = jnp.where(stale_here, weigh(queries, some_keys), 0.0)
        total = total + jnp.sum(numerator, axis=1, keepdims=True)
        gathered = gathered + gather_values(numerator, some_values)
    return total, gathered


def patch_of_rows(place_ref):
    second = lax.broadcasted_iota(jnp.int32, (LOCAL, 1), 0) >= PT
    return place_ref[0] + second.astype(jnp.int32)


def shared_attend_kernel(
    place_ref, kept_ref, got_ref, keys, values, sums_ref, given_ref
):
    half = place_ref[1]
    kept, got = kept_ref[:LOCAL], got_ref[:LOCAL]
    queries = jnp.where(half == 0, kept, got)
    fresh_keys = jnp.where(half == 0, got[:PT], kept[PT:])
    mine, other = kept_ref[LOCAL:].astype(jnp.float32), got_ref[LOCAL:].astype(jnp.float32)
    low = jnp.where(half == 0, mine, other)
    high = jnp.where(half == 0, other, mine)
    fresh_values = jnp.where(low_lanes(PT), low, pltpu.roll(high, HALF, 1)).astype(jnp.bfloat16)
    fresh = weigh(pick(half, queries), fresh_keys)

    def placed(rows):
        nothing = jnp.zeros_like(rows)
        return jnp.concatenate(
            [jnp.where(half == 0, rows, nothing), jnp.where(half == 0, nothing, rows)], axis=0
        )

    total = placed(jnp.sum(fresh, axis=1, keepdims=True))
    gathered = placed(gather_values(fresh, fresh_values))
    total, gathered = attend_stale(
        queries,
        keys,
        values,
        half * (PATCHES // 2),
        patch_of_rows(place_ref),
        total,
        gathered,
    )
    swapped = pltpu.roll(gathered, HALF, 1)
    first = low_lanes(LOCAL)
    sums_ref[...] = jnp.where(first, total, jnp.where(half == 0, swapped, gathered))
    given_ref[...] = jnp.where(first, total, jnp.where(half == 0, gathered, swapped))


def own_attend_kernel(
    place_ref, own_ref, earlier_ref, pieces_ref, attended_ref, w_own, w_vo, keys, values, sems
):
    del earlier_ref
    copies = fetch(
        pieces_ref,
        sems,
        [(keys, AT_K), (values, AT_V), (w_own, AT_OUT), (w_vo, AT_SHARED_VO)],
    )
    queries = own_ref[:LOCAL]
    fresh = weigh(queries, own_ref[LOCAL : 2 * LOCAL])
    row_at = lax.broadcasted_iota(jnp.int32, (LOCAL, 1), 0)
    column_at = lax.broadcasted_iota(jnp.int32, (LOCAL, LOCAL), 1)
    fresh = jnp.where((row_at >= PT) == (column_at >= PT), fresh, 0.0)
    total = jnp.sum(fresh, axis=1, keepdims=True)
    gathered = gather_values(fresh, own_ref[2 * LOCAL :])
    copies[0].wait()
    copies[1].wait()
    total, gathered = attend_stale(
        queries, keys, values, 0, patch_of_rows(place_ref), total, gathered
    )
    attended_ref[...] = (gathered / total).astype(jnp.bfloat16)
    copies[2].wait()
    copies[3].wait()


def finish_kernel(attended_ref, sums_ref, got_ref, w_own, w_vo, partial_ref):
    sums = sums_ref[...] + got_ref[...]
    shared = jnp.where(low_lanes(LOCAL), 0.0, sums / sums[:, :1]).astype(jnp.bfloat16)
    attention = jnp.concatenate([attended_ref[...], shared], axis=1)
    step = 8
    width = step * ROWS
    for low in range(0, SOURCES, step):
        weight = jnp.concatenate(
            [
                w_own[low : low + step].reshape(width, HD),
                w_vo[low : low + step].reshape(width, HD),
            ],
            axis=1,
        )
        partial_ref[:, low * ROWS : low * ROWS + width] = across(attention, weight).astype(
            jnp.bfloat16
        )


def to_own_order(array):
    lead = array.shape[:-1]
    split = array.reshape(lead + (NY, NZ * NC, ROWS))
    return jnp.swapaxes(split, -3, -2).reshape(lead + (D,))


def to_given_order(array):
    lead = array.shape[:-1]
    split = array.reshape(lead + (NZ * NC, NY, ROWS))
    return jnp.swapaxes(split, -3, -2).reshape(lead + (D,))


def exchange(array, axes):
    return lax.all_to_all(array, axes, split_axis=0, concat_axis=0, tiled=True)


def body(latent, modulation, w_qkv, w_out, stale):
    x_at, y_at = lax.axis_index("x"), lax.axis_index("y")
    pair_at = lax.axis_index("z") * NC + lax.axis_index("c")
    place = jnp.stack([2 * pair_at, y_at % 2]).astype(jnp.int32)

    sent = pl.pallas_call(
        pack_kernel,
        out_shape=jax.ShapeDtypeStruct((MEMBERS, PIECE, HD), jnp.bfloat16),
        in_specs=[ANY] * 3,
        out_specs=ANY,
        scratch_shapes=[
            pltpu.VMEM((ROWS, 3 * D), jnp.bfloat16),
            pltpu.VMEM((ROWS, D), jnp.bfloat16),
            pltpu.VMEM((PATCHES, 2, D), jnp.bfloat16),
            pltpu.VMEM((MEMBERS, PIECE, HD), jnp.bfloat16),
            pltpu.SemaphoreType.DMA((3,)),
            pltpu.SemaphoreType.DMA((MEMBERS,)),
        ],
        compiler_params=pltpu.CompilerParams(vmem_limit_bytes=60 * 1024 * 1024),
        name="pack",
    )(w_qkv[0], w_out[0].T, stale[0, :, 0])
    received = exchange(sent, HEAD_AXES).reshape(BLOCKS, NY, PIECE, HD)

    def gather(own_piece):
        return lax.all_gather(own_piece, REST_AXES, axis=0, tiled=True)

    pieces = [gather(received[0])]

    given = to_own_order(modulation[0])
    known = jnp.stack(
        [given]
        + [
            lax.ppermute(given, "x", [(at, (at + step) % NX) for at in range(NX)])
            for step in range(1, NX)
        ]
    )
    terms = [
        lax.dynamic_index_in_dim(known, (x_at - block) % NX, 0, keepdims=False)
        for block in range(BLOCKS)
    ]
    wanted = latent.reshape(NZ, NC, 2, D)
    wanted = lax.dynamic_index_in_dim(wanted, x_at // 2, 2, keepdims=False)
    core_at = lax.axis_index("c")
    same = lax.dynamic_index_in_dim(wanted, core_at, 1, keepdims=False)
    other = lax.dynamic_index_in_dim(wanted, 1 - core_at, 1, keepdims=False)
    other = lax.ppermute(other, "c", [(0, 1), (1, 0)])
    mine = exchange(jnp.where(core_at == x_at % 2, same, other), "z")
    current = to_own_order(mine)

    def term(block, which):
        return terms[block][which][None]

    spread = jax.ShapeDtypeStruct((LOCAL, D), jnp.bfloat16)
    owned = jax.ShapeDtypeStruct((OWN, D), jnp.bfloat16)
    normed = pl.pallas_call(
        first_kernel,
        out_shape=spread,
        in_specs=[VMEM] * 3,
        out_specs=VMEM,
        compiler_params=PARAMS,
        name="first",
    )(current, term(0, 0), term(0, 1))
    weight = pltpu.VMEM((SOURCES, ROWS, HD), jnp.bfloat16)
    cache = pltpu.VMEM((SOURCES, PATCHES, HD), jnp.bfloat16)
    half_cache = jax.ShapeDtypeStruct((SOURCES, PATCHES // 2, HD), jnp.bfloat16)
    kept_weight = jax.ShapeDtypeStruct((SOURCES, ROWS, HD), jnp.bfloat16)
    sums_of = jax.ShapeDtypeStruct((LOCAL, HD), jnp.float32)

    def rows_of(count):
        return jax.ShapeDtypeStruct((count, HD), jnp.bfloat16)

    def local(kernel, in_specs, out_specs, out_shape, scratch, copies, elements):
        return pl.pallas_call(
            kernel,
            out_shape=out_shape,
            in_specs=in_specs,
            out_specs=out_specs,
            scratch_shapes=scratch + [pltpu.SemaphoreType.DMA((copies,))] * (copies > 0),
            compiler_params=PARAMS if copies else SMALL,
            cost_estimate=pl.CostEstimate(
                flops=2 * LOCAL * elements, bytes_accessed=2 * elements, transcendentals=0
            ),
            name=kernel.__name__,
        )

    def swap(array):
        return lax.ppermute(array, "y", [(at, at ^ 1) for at in range(NY)])

    outputs = []
    for block in range(BLOCKS):
        rows = exchange(normed, HEAD_AXES)
        if block == 0:
            later = pl.pallas_call(
                later_kernel,
                out_shape=[jax.ShapeDtypeStruct((NY, PIECE, HD), jnp.bfloat16)] * (BLOCKS - 1),
                in_specs=[VMEM, VMEM],
                out_specs=[VMEM] * (BLOCKS - 1),
                compiler_params=SMALL,
                name="later",
            )(received, rows)
            pieces += [gather(own_piece) for own_piece in later]
        source = pieces[block]
        kept, given = local(
            shared_project_kernel, (SMEM, VMEM, ANY), (VMEM, VMEM),
            (rows_of(LOCAL + PT), rows_of(LOCAL + PT)), [weight] * 2, 2, 2 * D * HD,
        )(place, rows, source)
        got = swap(given)
        own, keys, values = local(
            own_project_kernel, (VMEM, ANY), (VMEM, VMEM, VMEM),
            (rows_of(3 * LOCAL), half_cache, half_cache), [weight] * 3, 5, 3 * D * HD,
        )(rows, source)
        sums, given = local(
            shared_attend_kernel, (SMEM,) + (VMEM,) * 4, (VMEM, VMEM),
            (sums_of, sums_of), [], 0, PATCHES * PT * HD,
        )(place, kept, got, keys, values)
        got = swap(given)
        attended, w_own, w_vo = local(
            own_attend_kernel, (SMEM, VMEM, VMEM, ANY), (VMEM, VMEM, VMEM),
            (rows_of(LOCAL), kept_weight, kept_weight), [cache] * 2, 4, 2 * PATCHES * PT * HD,
        )(place, own, sums, source)
        partial = local(
            finish_kernel, (VMEM,) * 5, VMEM, spread, [], 0, 2 * D * HD,
        )(attended, sums, got, w_own, w_vo)
        parts = exchange(partial, HEAD_AXES)
        if block + 1 < BLOCKS:
            current, normed = pl.pallas_call(
                middle_kernel,
                out_shape=(owned, spread),
                in_specs=[VMEM] * 5,
                out_specs=(VMEM, VMEM),
                compiler_params=PARAMS,
                name="middle",
            )(parts, current, term(block, 2), term(block + 1, 0), term(block + 1, 1))
        else:
            current = pl.pallas_call(
                last_kernel,
                out_shape=owned,
                in_specs=[VMEM] * 3,
                out_specs=VMEM,
                compiler_params=PARAMS,
                name="last",
            )(parts, current, term(block, 2))
        outputs.append(to_given_order(current))
    outputs = jnp.stack(outputs)
    moved = [lax.dynamic_index_in_dim(outputs, x_at, 0, keepdims=False)]
    for step in range(1, NX):
        leaving = lax.dynamic_index_in_dim(outputs, (x_at + step) % NX, 0, keepdims=False)
        moved.append(lax.ppermute(leaving, "x", [(at, (at + step) % NX) for at in range(NX)]))
    moved = jnp.stack(moved)
    placed = jnp.stack(
        [
            lax.dynamic_index_in_dim(moved, (x_at - origin) % NX, 0, keepdims=False)
            for origin in range(NX)
        ]
    )
    placed = placed.reshape(2, NC, NZ, D).transpose(2, 1, 0, 3).reshape(PATCHES, D)
    placed = exchange(placed, REST_AXES)
    return placed[None, :, None]


def solution(mesh):
    own_mesh = Mesh(mesh.devices.reshape(NX, NY, NZ, NC), ("x",) + SP)
    return jax.shard_map(
        body,
        mesh=own_mesh,
        in_specs=(
            P(None, SP, None),
            P("x", None, None),
            P("x", SP, None),
            P("x", None, SP),
            P("x", None, SP, None, None),
        ),
        out_specs=P("x", None, SP, None),
        check_vma=False,
    )
```
